768 devices in a mesh: slab: 96 (over z, x, core), tile: 8 (over y).
Axes of the slice: x: 4, y: 8, z: 12, core: 2. Of those that a mesh axis runs over, the one named last changes fastest.
Arguments:
- initial_field: float32 [3, 768, 128, 384], P(None, 'slab', 'tile'), may hold values from -6 to 6
- source: float32 [3, 768, 128, 384], P(None, 'slab', 'tile'), may hold values from -12 to 12
- material: int32 [768, 128, 384], P('slab', 'tile'), may hold values from 0 to 7
- stiffness_table: float32 [8], replicated, may hold values from 0.5 to 4
- mass_table: float32 [8], replicated, may hold values from 0.1 to 1
- trace_cells: int32 [96, 8, 256], P('slab', 'tile'), may hold values from -1 to 147455, as said below
- near_blocks: bfloat16 [96, 8, 9, 256, 256], P('slab', 'tile'), may hold values from -0.125 to 0.125
- near_mask: int32 [96, 8, 9], P('slab', 'tile'), may hold values 0 or 1
- far_left: bfloat16 [16, 96, 8, 256], P(None, 'slab', 'tile'), may hold values from -1.5 to 1.5
- far_right: bfloat16 [16, 96, 96, 8, 256], P(None, None, 'slab', 'tile'), may hold values from -0.046875 to 0.046875
- block_ranks: int32 [96], P('slab'), may hold values from 1 to 16, as said below
Outputs:
- field: float32 [3, 768, 128, 384], P(None, 'slab', 'tile')
- boundary: float32 [96, 8, 256], P('slab', 'tile')
The draws below stay inside these ranges and needn't reach their ends.
Inputs may be any that keep to these rules, and one draw needn't show every extreme that they name: `trace_cells`: in each device's list the first entries are distinct positions within that device's block and the rest are -1; some device fills all 256 slots. `block_ranks`: some block row has rank 16.
All inputs are finite; a program needn't handle non-finite values. No bound on the sum of `near_mask` on one device may be relied on, other than what follows from the above.
Results may differ from the reference program's by a relative error of at most 0.007.
Values may be sent and summed in bfloat16 or wider, within the bound.
No kernel may reach another device: no remote copies, remote signals or barrier semaphores. Data moves between devices by JAX's collectives and lax.ppermute only.
A program may use at most 32 MiB of HBM per device.

```python
import math
import jax
import jax.numpy as jnp
from jax import lax

CZ = 8
CY = 16
NX = 384
CAP = 256
K = 16
NMAT = 8
SWEEPS = 2
NZ = 768
NY = 128
N_SLAB = 96
N_TILE = 8


def draw_trace_cells(key, part):
    key = jax.random.fold_in(key, 11)
    keys = jax.random.split(key, 6)
    devices = N_SLAB * N_TILE
    local_size = 3 * CZ * CY * NX
    touching = jax.random.randint(keys[0], (N_SLAB, 1), 0, 2)
    heavy = jax.random.randint(keys[1], (N_SLAB, N_TILE), CAP // 2, CAP + 1)
    light = jax.random.randint(keys[2], (N_SLAB, N_TILE), 1, CAP // 4 + 1)
    counts = jnp.where(touching > 0, heavy, light).reshape(devices)
    chosen = jax.random.randint(keys[3], (), 0, devices)
    counts = jnp.where(jnp.arange(devices) == chosen, CAP, counts)
    starts = jax.random.randint(keys[4], (devices, 1), 0, local_size)
    steps = 6 * jax.random.randint(keys[5], (devices, 1), 0, local_size // 6) + 1
    slots = jnp.arange(CAP)[None, :]
    raw = (starts + slots * steps % local_size) % local_size
    live = slots < counts[:, None]
    return jnp.where(live, raw, -1).reshape(N_SLAB, N_TILE, CAP).astype(jnp.int32)


def draw_block_ranks(key, part):
    key = jax.random.fold_in(key, 12)
    first_key, second_key = jax.random.split(key)
    ranks = jax.random.randint(first_key, (N_SLAB,), 1, K + 1)
    chosen = jax.random.randint(second_key, (), 0, N_SLAB)
    return jnp.where(jnp.arange(N_SLAB) == chosen, K, ranks).astype(jnp.int32)


def plant(array, rng, smallest, top_value):
    place = [jax.random.randint(jax.random.fold_in(rng, axis), (), 0, length) for axis, length in enumerate(array.shape)]
    widest = array.shape.index(max(array.shape))
    next_to = place[:widest] + [(place[widest] + 1) % array.shape[widest]] + place[widest + 1:]
    return array.at[tuple(place)].set(smallest).at[tuple(next_to)].set(top_value)


def strengthened(entries, own_key, source, target, parts, factor):
    owner, partner = [(jnp.arange(entries.shape[position]) // (entries.shape[position] // parts)).reshape([-1 if axis == position else 1 for axis in range(entries.ndim)]) for position in (source, target)]
    chosen = jax.random.permutation(own_key, parts)[partner]
    strong = (owner == chosen) | (owner == (partner + parts // 2) % parts)
    return jnp.where(strong, factor * entries, entries)


def steps_of(rng, dims, cuts, smallest, largest):
    level = 1.0
    for dim, parts in cuts:
        steps = jax.random.uniform(jax.random.fold_in(jax.random.fold_in(rng, 6), dim), (parts,), jnp.float32, smallest / len(cuts), largest / len(cuts))
        level = level * jnp.repeat(jnp.exp(steps), dims[dim] // parts).reshape((-1,) + (1,) * (len(dims) - 1 - dim))
    return level


def noise(own_key, shape, scale, most, shards=(), kind=jnp.bfloat16):
    result = jax.random.normal(own_key, shape, jnp.float32) * scale
    if len(shards) > 0:
        result = steps_of(own_key, shape, shards, -0.22, 0.18) * result
    return jnp.clip(result, min=-most, max=most).astype(kind)


def noise_with(stream_key, shape, width, limit, cuts, heavy, kind=jnp.bfloat16):
    drawn = width * jax.random.normal(stream_key, shape, jnp.float32)
    if cuts:
        drawn = drawn * steps_of(stream_key, shape, cuts, -0.22, 0.18)
    return jnp.clip(strengthened(drawn, jax.random.fold_in(stream_key, 3), *heavy), -limit, limit).astype(kind)


def setup_inputs(seed: int = 0) -> dict:
    seeds = jax.random.split(jax.random.key(seed), 12)
    initial_field = noise(seeds[0], (3, NZ, NY, NX), 1.0, 6.0, ((1, 96), (2, 8)), jnp.float32)
    source = noise(seeds[1], (3, NZ, NY, NX), 2.0, 12.0, ((1, 96), (2, 8)), jnp.float32)
    material = plant(jax.random.randint(seeds[2], (NZ, NY, NX), 0, NMAT), jax.random.fold_in(seeds[2], 1), 0, NMAT - 1).astype(jnp.int32)
    stiffness_table = jnp.clip(jnp.exp(jax.random.uniform(seeds[3], (NMAT,), jnp.float32, math.log(0.5), math.log(4.0))), 0.5, 4.0)
    mass_table = jnp.clip(jnp.exp(jax.random.uniform(seeds[4], (NMAT,), jnp.float32, math.log(0.1), math.log(1.0))), 0.1, 1.0)
    trace_cells = draw_trace_cells(jax.random.fold_in(seeds[11], 71), 0)
    near_blocks = noise(seeds[6], (N_SLAB, N_TILE, 9, CAP, CAP), (9 * CAP) ** -0.5, 0.125, ((0, 96), (1, 8)))
    near_mask = plant((jax.random.randint(seeds[7], (N_SLAB, N_TILE, 9), 0, 3) < 2).astype(jnp.int32), jax.random.fold_in(seeds[7], 1), 0, 1)
    far_left = noise(seeds[8], (K, N_SLAB, N_TILE, CAP), K ** -0.5, 1.5, ((1, 96), (2, 8)))
    far_right = noise_with(seeds[9], (K, N_SLAB, N_SLAB, N_TILE, CAP), (N_SLAB * N_TILE * CAP) ** -0.5, 0.046875, ((2, 96), (3, 8)), (2, 1, 96, 4.75))
    block_ranks = draw_block_ranks(jax.random.fold_in(seeds[11], 71), 0)
    return {"initial_field": initial_field, "source": source, "material": material, "stiffness_table": stiffness_table, "mass_table": mass_table, "trace_cells": trace_cells, "near_blocks": near_blocks, "near_mask": near_mask, "far_left": far_left, "far_right": far_right, "block_ranks": block_ranks}


relax_weight = 0.8


def relax_cells(extended, sources, stiffness, diagonal):
    core = extended[:, 1:-1, 1:-1]
    shifted = jnp.pad(core, ((0, 0), (0, 0), (0, 0), (1, 1)))
    total = extended[:, 2:, 1:-1] + extended[:, :-2, 1:-1]
    total = total + extended[:, 1:-1, 2:] + extended[:, 1:-1, :-2]
    total = total + shifted[..., 2:] + shifted[..., :-2]
    residual = sources - (diagonal * core - stiffness * total)
    safe = jnp.where(diagonal > 0.0, diagonal, 1.0)
    return core + jnp.where(diagonal > 0.0, relax_weight * residual / safe, 0.0)


def reference(initial_field, source, material, stiffness_table, mass_table, trace_cells, near_blocks, near_mask, far_left, far_right, block_ranks):
    stiffness = stiffness_table[material]
    diagonal = 6.0 * stiffness + mass_table[material]
    field = initial_field
    for sweep in range(SWEEPS):
        extended = jnp.pad(field, ((0, 0), (1, 1), (1, 1), (0, 0)))
        field = relax_cells(extended, source, stiffness, diagonal)
    blocks = field.reshape(3, N_SLAB, CZ, N_TILE, CY, NX).transpose(1, 3, 0, 2, 4, 5).reshape(N_SLAB, N_TILE, 3 * CZ * CY * NX)
    picked = jnp.take_along_axis(blocks, jnp.maximum(trace_cells, 0).astype(jnp.int32), axis=2)
    traces = jnp.where(trace_cells >= 0, picked, 0.0).astype(jnp.bfloat16)
    padded = jnp.pad(traces, ((1, 1), (1, 1), (0, 0)))
    nearby = jnp.stack([padded[row_step:row_step + N_SLAB, col_step:col_step + N_TILE] for row_step in range(3) for col_step in range(3)], axis=2)
    nearby = nearby * near_mask[..., None].astype(jnp.bfloat16)

    def near_row(pair):
        blocks_row, vectors = pair
        return jnp.einsum("rqmn,rqn->rm", blocks_row.astype(jnp.float32), vectors.astype(jnp.float32))

    near_part = lax.map(near_row, (near_blocks, nearby))
    trace_values = traces.astype(jnp.float32)

    def far_row(right):
        return jnp.einsum("icjn,cjn->i", right.astype(jnp.float32), trace_values)

    partial_value = lax.map(far_row, far_right)
    keep = jnp.arange(K)[:, None] < block_ranks[None, :]
    coeffs = jnp.where(keep, partial_value, 0.0)
    far_part = jnp.einsum("kirn,ki->irn", far_left.astype(jnp.float32), coeffs)
    return field, near_part + far_part
```

```python
import functools

import jax
import jax.numpy as jnp
import numpy as np
from jax import lax
from jax.experimental import pallas as pl
from jax.experimental.pallas import tpu as pltpu
from jax.sharding import PartitionSpec as P

RELAX = 0.8
KEEP = 1.0 - RELAX
PLANE = 8
F32 = jnp.float32
BF16 = jnp.bfloat16
BOTH = ("slab", "tile")


def table_rows(stiff_ref, mass_ref):
    rows = []
    for entry in range(8):
        stiffness = jnp.full((8, 128), stiff_ref[entry], F32)
        inverse = RELAX / (6.0 * stiffness + mass_ref[entry])
        rows.append((inverse[:1, :1], (stiffness * inverse)[:1, :1]))
    return rows


def lookup(material, rows):
    weight = jnp.broadcast_to(rows[0][0], material.shape)
    coupling = jnp.broadcast_to(rows[0][1], material.shape)
    for entry in range(1, 8):
        here = material == entry
        weight = jnp.where(here, rows[entry][0], weight)
        coupling = jnp.where(here, rows[entry][1], coupling)
    return weight, coupling


def x_sum(value):
    width = value.shape[-1]
    lane = lax.broadcasted_iota(jnp.int32, value.shape, value.ndim - 1)
    before = jnp.where(lane == 0, 0.0, pltpu.roll(value, 1, value.ndim - 1))
    after = jnp.where(lane == width - 1, 0.0, pltpu.roll(value, width - 1, value.ndim - 1))
    return before + after


def row_sum(value, first, last):
    length = value.shape[0]
    row = lax.broadcasted_iota(jnp.int32, value.shape, 0)
    before = jnp.where(row == 0, first, pltpu.roll(value, 1, 0))
    after = jnp.where(row == length - 1, last, pltpu.roll(value, length - 1, 0))
    return before + after


def line_rows(ref, y, *lead):
    lines = [ref[(*lead, slice(16 * z + y, 16 * z + y + 1), slice(None))] for z in range(8)]
    row = lax.broadcasted_iota(jnp.int32, (8, lines[0].shape[1]), 0)
    value = jnp.broadcast_to(lines[0], row.shape)
    for z in range(1, 8):
        value = jnp.where(row == z, lines[z], value)
    return value


def y_faces(stiff_ref, mass_ref, field_ref, source_ref, material_ref, first_ref, last_ref):
    rows = table_rows(stiff_ref, mass_ref)
    for y, inner, out_ref in ((0, 1, first_ref), (15, 14, last_ref)):
        weight, coupling = lookup(line_rows(material_ref, y), rows)
        values, partials = [], []
        for c in range(3):
            value = line_rows(field_ref, y, c)
            beside = line_rows(field_ref, inner, c)
            sources = line_rows(source_ref, y, c)
            total = beside + row_sum(value, 0.0, 0.0) + x_sum(value)
            values.append(value)
            partials.append(KEEP * value + weight * sources + coupling * total)
        planes = values + partials + [coupling, jnp.zeros_like(coupling)]
        for pair in range(4):
            both = jnp.concatenate(planes[2 * pair:2 * pair + 2], axis=0)
            out_ref[16 * pair:16 * pair + 16, :] = both.astype(BF16)


def z_faces(stiff_ref, mass_ref, low_ref, high_ref, low_source_ref, high_source_ref, low_material_ref, high_material_ref,
            before_ref, after_ref, first_ref, last_ref):
    rows = table_rows(stiff_ref, mass_ref)
    before = [before_ref[16 * k:16 * k + 16, :].astype(F32) for k in range(2)]
    after = [after_ref[16 * k:16 * k + 16, :].astype(F32) for k in range(2)]
    for z, field_ref, source_ref, material_ref, out_ref in (
        (0, low_ref, low_source_ref, low_material_ref, first_ref),
        (7, high_ref, high_source_ref, high_material_ref, last_ref),
    ):
        weight, coupling = lookup(material_ref[...], rows)
        lines = []
        for c in range(3):
            at = 8 * (c % 2) + z
            lines.append((before[c // 2][at:at + 1, :], after[c // 2][at:at + 1, :]))
            outer, inner = (0, 16) if z == 0 else (16, 0)
            value = field_ref[c, outer:outer + 16, :]
            beside = field_ref[c, inner:inner + 16, :]
            total = beside + row_sum(value, *lines[c]) + x_sum(value)
            partial = KEEP * value + weight * source_ref[c] + coupling * total
            out_ref[16 * c:16 * c + 16, :] = value.astype(BF16)
            out_ref[48 + 16 * c:64 + 16 * c, :] = partial.astype(BF16)
        out_ref[96:112, :] = coupling.astype(BF16)
        row = lax.broadcasted_iota(jnp.int32, (16, coupling.shape[1]), 0)
        packed = jnp.zeros(row.shape, F32)
        for c in range(3):
            for side in range(2):
                packed = jnp.where(row == 2 * c + side, lines[c][side], packed)
        out_ref[112:128, :] = packed.astype(BF16)


def column_of(row):
    length = row.shape[1]
    down = lax.broadcasted_iota(jnp.int32, (length, length), 0)
    along = lax.broadcasted_iota(jnp.int32, (length, length), 1)
    return jnp.sum(jnp.where(down == along, row, 0.0), axis=1, keepdims=True)


def relax(planes, stiff_ref, mass_ref, field_ref, source_ref, material_ref, before_ref, after_ref, below_ref, above_ref,
          right_ref, cells_ref, out_ref, send_ref, once_ref, scaled_ref, coupling_ref, plain_ref):
    rows = table_rows(stiff_ref, mass_ref)
    y_halo = [[r[16 * k:16 * k + 16, :].astype(F32) for k in range(4)] for r in (before_ref, after_ref)]
    z_halo = [[r[16 * k:16 * k + 16, :].astype(F32) for k in range(8)] for r in (below_ref, above_ref)]

    def y_plane(side, k):
        return y_halo[side][k // 2][8 * (k % 2):8 * (k % 2) + 8]

    row8 = lax.broadcasted_iota(jnp.int32, (8, field_ref.shape[-1]), 0)
    rims = []
    for c in range(3):
        once_ref[c, 0] = z_halo[0][3 + c] + z_halo[0][6] * field_ref[c, 0:16, :]
        once_ref[c, 9] = z_halo[1][3 + c] + z_halo[1][6] * field_ref[c, 112:128, :]
        sides = []
        for side, y in ((0, 0), (1, 15)):
            beside = line_rows(field_ref, y, c)
            at = 2 * c + side
            beside = beside + jnp.where(row8 == 0, z_halo[0][7][at:at + 1], 0.0)
            beside = beside + jnp.where(row8 == 7, z_halo[1][7][at:at + 1], 0.0)
            sides.append(y_plane(side, 3 + c) + y_plane(side, 6) * beside)
        rims.append(sides)
    for z in range(8):
        here = slice(16 * z, 16 * z + 16)
        weight, coupling = lookup(material_ref[here, :], rows)
        coupling_ref[here, :] = coupling
        for c in range(3):
            value = field_ref[c, here, :]
            lower = z_halo[0][c] if z == 0 else field_ref[c, 16 * z - 16:16 * z, :]
            upper = z_halo[1][c] if z == 7 else field_ref[c, 16 * z + 16:16 * z + 32, :]
            total = lower + upper + row_sum(value, y_plane(0, c)[z:z + 1], y_plane(1, c)[z:z + 1]) + x_sum(value)
            scaled = weight * source_ref[c, here, :]
            scaled_ref[c, here, :] = scaled
            once_ref[c, z + 1] = KEEP * value + scaled + coupling * total
    for z in range(8):
        here = slice(16 * z, 16 * z + 16)
        coupling = coupling_ref[here, :]
        for c in range(3):
            value = once_ref[c, z + 1]
            total = once_ref[c, z] + once_ref[c, z + 2] + x_sum(value)
            total = total + row_sum(value, rims[c][0][z:z + 1], rims[c][1][z:z + 1])
            result = KEEP * value + scaled_ref[c, here, :] + coupling * total
            out_ref[c, here, :] = result
            plain_ref[128 * c + 16 * z:128 * c + 16 * z + 16, :] = result.astype(BF16)

    width = field_ref.shape[-1]
    count = cells_ref.shape[1]
    cells = cells_ref[...].astype(F32)
    line = jnp.floor((cells + 0.5) * (1.0 / width))
    line_column = column_of(line)
    place_column = column_of(cells - width * line)
    along = lax.broadcasted_iota(jnp.int32, (count, width), 1).astype(F32)
    chosen = jnp.where(along == line_column, 1.0, 0.0).astype(BF16)
    picked = jnp.dot(chosen, plain_ref[...], preferred_element_type=F32)
    single = jnp.where(along == place_column, picked, 0.0).astype(BF16)
    spread = jnp.dot(single, jnp.ones((width, 128), BF16), preferred_element_type=F32)
    far = jnp.dot(right_ref[...], spread.astype(BF16), preferred_element_type=F32)
    ranks = 16
    used = planes * ranks
    lane = lax.broadcasted_iota(jnp.int32, (PLANE, 128), 1)
    parts = [jnp.zeros((PLANE, 128), F32) for _ in range(3)]
    for k in range(ranks):
        for z in range(planes):
            group = far[PLANE * (k * planes + z):PLANE * (k * planes + z + 1), :]
            for at in (z * ranks + k, 192 + z * ranks + k):
                parts[at // 128] = jnp.where(lane == at % 128, group, parts[at // 128])
    both = jnp.concatenate(parts, axis=1)
    two = lax.broadcasted_iota(jnp.int32, both.shape, 1)
    high = both.astype(BF16).astype(F32)
    both = jnp.where(two < 192, high, both - high)
    tiles = send_ref.shape[0] // PLANE
    for to in range(PLANE):
        parts_row = jnp.broadcast_to(both[to:to + 1, :], (tiles, both.shape[1]))
        both_rows = parts_row if to % 2 == 0 else jnp.concatenate([both_rows, parts_row], axis=0)
        if to % 2 == 1:
            send_ref[(to - 1) * tiles:(to + 1) * tiles, 0:384] = both_rows.astype(BF16)
    down = lax.broadcasted_iota(jnp.int32, (128, 128), 0)
    across = lax.broadcasted_iota(jnp.int32, (128, 128), 1)
    for half in range(count // 128):
        piece = jnp.where(down == across, spread[128 * half:128 * half + 128, :], 0.0)
        piece = jnp.sum(piece, axis=0, keepdims=True)
        send_ref[:, 384 + 128 * half:512 + 128 * half] = jnp.broadcast_to(piece, (send_ref.shape[0], 128)).astype(BF16)


def fold(rows):
    total = jnp.sum(rows.astype(F32), axis=0, keepdims=True)
    return total + pltpu.roll(jnp.broadcast_to(total, (8, total.shape[1])), 192, 1)


def middle(tiles, got_ref, send_ref):
    across = lax.rem(lax.axis_index("slab"), PLANE)
    tile = lax.axis_index("tile")
    total = fold(got_ref[:, 0:384])
    high = total.astype(BF16).astype(F32)
    lane = lax.broadcasted_iota(jnp.int32, total.shape, 1)
    send = jnp.where(lane < 192, high, total - high)[0:1, :]
    send_ref[:, 0:384] = jnp.broadcast_to(send, (send_ref.shape[0], 384)).astype(BF16)
    row = lax.broadcasted_iota(jnp.int32, (16, got_ref.shape[0]), 0)
    along = lax.broadcasted_iota(jnp.int32, (16, got_ref.shape[0]), 1)
    other = jnp.where(across == 0, PLANE - 1, 0)
    wanted = tile + row - 1
    match = (row < 3) & (wanted >= 0) & (wanted < tiles) & (along == other * tiles + wanted)
    chosen = jnp.where(match, 1.0, 0.0).astype(BF16)
    relay = jnp.dot(chosen, got_ref[:, 384:640], preferred_element_type=F32)
    for b in range(3):
        send_ref[:, 384 + 256 * b:640 + 256 * b] = jnp.broadcast_to(relay[b:b + 1, :], (send_ref.shape[0], 256)).astype(BF16)


def finish(tiles, planes, mask_ref, rank_ref, got_ref, relay_ref, near_ref, left_ref, out_ref):
    slab = lax.axis_index("slab")
    across = lax.rem(slab, PLANE)
    plane = lax.div(slab, PLANE)
    tile = lax.axis_index("tile")
    row = lax.broadcasted_iota(jnp.int32, (16, got_ref.shape[0]), 0)
    along = lax.broadcasted_iota(jnp.int32, (16, got_ref.shape[0]), 1)
    third = lax.shift_right_logical(row * 11, 5)
    up = across + third - 1
    beside = tile + row - 3 * third - 1
    match = (row < 9) & (up >= 0) & (up < PLANE) & (beside >= 0) & (beside < tiles) & (along == up * tiles + beside)
    near = jnp.dot(jnp.where(match, 1.0, 0.0).astype(BF16), got_ref[:, 384:640], preferred_element_type=F32)
    row = lax.broadcasted_iota(jnp.int32, near.shape, 0)
    passed = relay_ref[...].astype(F32)
    from_row = lax.broadcasted_iota(jnp.int32, (passed.shape[0], 768), 0)
    under = jnp.sum(jnp.where((from_row == plane - 1) & (across == 0), passed[:, 384:], 0.0), axis=0, keepdims=True)
    over = jnp.sum(jnp.where((from_row == plane + 1) & (across == PLANE - 1), passed[:, 384:], 0.0), axis=0, keepdims=True)
    for b in range(3):
        near = jnp.where(row == b, near + under[:, 256 * b:256 * b + 256], near)
        near = jnp.where(row == 6 + b, near + over[:, 256 * b:256 * b + 256], near)
    listed = jnp.zeros(near.shape, F32)
    for q in range(9):
        listed = jnp.where(row == q, mask_ref[q].astype(F32), listed)
    near = (near * listed).astype(BF16)
    products = lax.dot_general(near, near_ref[...], (((1,), (1,)), ((), ())), preferred_element_type=F32)
    result = jnp.zeros((1, 256), F32)
    for q in range(9):
        result = result + products[q:q + 1, 256 * q:256 * q + 256]
    total = fold(passed[:, 0:384])[:, 0:256]
    lane = lax.broadcasted_iota(jnp.int32, total.shape, 1)
    own = (lane >= 16 * plane) & (lane < 16 * plane + rank_ref[0])
    total = jnp.where(own, total, 0.0)
    high = total.astype(BF16).astype(F32)
    halves = jnp.concatenate([high, total - high], axis=0).astype(BF16)
    left = jnp.concatenate([left_ref[...]] * 16, axis=0)
    far = jnp.dot(halves, left, preferred_element_type=F32)
    out_ref[...] = result + far[0:1, :] + far[8:9, :]


def vmem():
    return pl.BlockSpec(memory_space=pltpu.VMEM)


def smem():
    return pl.BlockSpec(memory_space=pltpu.SMEM)


def exchange(first, last, axis):
    devices = lax.axis_size(axis)
    up = [(i, i + 1) for i in range(devices - 1)]
    down = [(j, i) for i, j in up]
    return lax.ppermute(last, axis, up), lax.ppermute(first, axis, down)


def local(initial_field, source, material, stiffness_table, mass_table, trace_cells, near_blocks, near_mask, far_left, far_right,
          block_ranks):
    slabs, tiles = lax.axis_size("slab"), lax.axis_size("tile")
    planes = slabs // PLANE
    field = initial_field.reshape(3, 128, 384)
    sources = source.reshape(3, 128, 384)
    cells = material.reshape(128, 384)
    face = jax.ShapeDtypeStruct((64, 384), BF16)
    params = pltpu.CompilerParams(vmem_limit_bytes=24 * 1024 * 1024)
    first, last = pl.pallas_call(
        y_faces,
        out_shape=(face, face),
        in_specs=[smem(), smem(), vmem(), vmem(), vmem()],
        out_specs=(vmem(), vmem()),
        compiler_params=params,
    )(stiffness_table, mass_table, field, sources, cells)
    before, after = exchange(first, last, "tile")
    face = jax.ShapeDtypeStruct((128, 384), BF16)
    first, last = pl.pallas_call(
        z_faces,
        grid=(1,),
        out_shape=(face, face),
        in_specs=[
            smem(), smem(),
            pl.BlockSpec((3, 32, 384), lambda i: (0, 0, 0)), pl.BlockSpec((3, 32, 384), lambda i: (0, 3, 0)),
            pl.BlockSpec((3, 16, 384), lambda i: (0, 0, 0)), pl.BlockSpec((3, 16, 384), lambda i: (0, 7, 0)),
            pl.BlockSpec((16, 384), lambda i: (0, 0)), pl.BlockSpec((16, 384), lambda i: (7, 0)),
            pl.BlockSpec((64, 384), lambda i: (0, 0)), pl.BlockSpec((64, 384), lambda i: (0, 0)),
        ],
        out_specs=(pl.BlockSpec((128, 384), lambda i: (0, 0)), pl.BlockSpec((128, 384), lambda i: (0, 0))),
        compiler_params=params,
    )(stiffness_table, mass_table, field, field, sources, sources, cells, cells, before, after)
    below, above = exchange(first, last, "slab")
    members = PLANE * tiles
    result, send = pl.pallas_call(
        functools.partial(relax, planes),
        out_shape=(jax.ShapeDtypeStruct((3, 128, 384), F32), jax.ShapeDtypeStruct((members, 640), BF16)),
        in_specs=[smem(), smem()] + [vmem()] * 9,
        out_specs=(vmem(), vmem()),
        scratch_shapes=[
            pltpu.VMEM((3, 10, 16, 384), F32),
            pltpu.VMEM((3, 128, 384), F32),
            pltpu.VMEM((128, 384), F32),
            pltpu.VMEM((384, 384), BF16),
        ],
        compiler_params=params,
    )(stiffness_table, mass_table, field, sources, cells, before, after, below, above,
      far_right.reshape(-1, 256), trace_cells.reshape(1, 256))
    ids = np.arange(slabs * tiles).reshape(planes, members)
    got = lax.all_to_all(send, BOTH, 0, 0, axis_index_groups=ids.tolist())
    send = pl.pallas_call(
        functools.partial(middle, tiles),
        out_shape=jax.ShapeDtypeStruct((planes, 1152), BF16),
        in_specs=[vmem()],
        out_specs=vmem(),
        compiler_params=params,
    )(got)
    relay = lax.all_to_all(send, BOTH, 0, 0, axis_index_groups=ids.T.tolist())
    boundary = pl.pallas_call(
        functools.partial(finish, tiles, planes),
        out_shape=jax.ShapeDtypeStruct((1, 256), F32),
        in_specs=[smem(), smem()] + [vmem()] * 4,
        out_specs=vmem(),
        compiler_params=params,
    )(near_mask.reshape(9), block_ranks, got, relay, near_blocks.reshape(-1, 256), far_left.reshape(16, 256))
    return result.reshape(initial_field.shape), boundary.reshape(1, 1, 256)


def solution(mesh):
    placed = (
        P(None, "slab", "tile", None),
        P(None, "slab", "tile", None),
        P("slab", "tile", None),
        P(),
        P(),
        P("slab", "tile", None),
        P("slab", "tile", None, None, None),
        P("slab", "tile", None),
        P(None, "slab", "tile", None),
        P(None, None, "slab", "tile", None),
        P("slab"),
    )
    return jax.shard_map(
        local,
        mesh=mesh,
        in_specs=placed,
        out_specs=(P(None, "slab", "tile", None), P("slab", "tile", None)),
        check_vma=False,
    )
```

```python
import functools

import jax
import jax.numpy as jnp
import numpy as np
from jax import lax
from jax.experimental import pallas as pl
from jax.experimental.pallas import tpu as pltpu
from jax.sharding import PartitionSpec as P

RELAX = 0.8
KEEP = 1.0 - RELAX
PLANE = 8
F32 = jnp.float32
BF16 = jnp.bfloat16
BOTH = ("slab", "tile")


def table_rows(stiff_ref, mass_ref):
    rows = []
    for entry in range(8):
        stiffness = jnp.full((8, 128), stiff_ref[entry], F32)
        inverse = RELAX / (6.0 * stiffness + mass_ref[entry])
        rows.append((inverse[:1, :1], (stiffness * inverse)[:1, :1]))
    return rows


def lookup(material, rows):
    weight = jnp.broadcast_to(rows[0][0], material.shape)
    coupling = jnp.broadcast_to(rows[0][1], material.shape)
    for entry in range(1, 8):
        here = material == entry
        weight = jnp.where(here, rows[entry][0], weight)
        coupling = jnp.where(here, rows[entry][1], coupling)
    return weight, coupling


def x_sum(value):
    width = value.shape[-1]
    lane = lax.broadcasted_iota(jnp.int32, value.shape, value.ndim - 1)
    before = jnp.where(lane == 0, 0.0, pltpu.roll(value, 1, value.ndim - 1))
    after = jnp.where(lane == width - 1, 0.0, pltpu.roll(value, width - 1, value.ndim - 1))
    return before + after


def row_sum(value, first, last):
    length = value.shape[0]
    row = lax.broadcasted_iota(jnp.int32, value.shape, 0)
    before = jnp.where(row == 0, first, pltpu.roll(value, 1, 0))
    after = jnp.where(row == length - 1, last, pltpu.roll(value, length - 1, 0))
    return before + after


def line_rows(ref, y, *lead):
    lines = [ref[(*lead, slice(16 * z + y, 16 * z + y + 1), slice(None))] for z in range(8)]
    row = lax.broadcasted_iota(jnp.int32, (8, lines[0].shape[1]), 0)
    value = jnp.broadcast_to(lines[0], row.shape)
    for z in range(1, 8):
        value = jnp.where(row == z, lines[z], value)
    return value


def y_faces(stiff_hbm, mass_hbm, field_hbm, source_hbm, material_hbm, first_ref, last_ref,
            stiff_ref, mass_ref, field_ref, source_ref, material_ref, sems):
    pairs = ((stiff_hbm, stiff_ref), (mass_hbm, mass_ref), (material_hbm, material_ref), (field_hbm, field_ref), (source_hbm, source_ref))
    copies = [pltpu.make_async_copy(src, dst, sems.at[k]) for k, (src, dst) in enumerate(pairs)]
    for copy in copies:
        copy.start()
    for copy in copies:
        copy.wait()
    rows = table_rows(stiff_ref, mass_ref)
    for y, inner, out_ref in ((0, 1, first_ref), (15, 14, last_ref)):
        weight, coupling = lookup(line_rows(material_ref, y), rows)
        values, partials = [], []
        for c in range(3):
            value = line_rows(field_ref, y, c)
            beside = line_rows(field_ref, inner, c)
            sources = line_rows(source_ref, y, c)
            total = beside + row_sum(value, 0.0, 0.0) + x_sum(value)
            values.append(value)
            partials.append(KEEP * value + weight * sources + coupling * total)
        planes = values + partials + [coupling, jnp.zeros_like(coupling)]
        for pair in range(4):
            both = jnp.concatenate(planes[2 * pair:2 * pair + 2], axis=0)
            out_ref[16 * pair:16 * pair + 16, :] = both.astype(BF16)


def z_faces(stiff_ref, mass_ref, low_ref, high_ref, low_source_ref, high_source_ref, low_material_ref, high_material_ref,
            before_ref, after_ref, first_ref, last_ref):
    rows = table_rows(stiff_ref, mass_ref)
    before = [before_ref[16 * k:16 * k + 16, :].astype(F32) for k in range(2)]
    after = [after_ref[16 * k:16 * k + 16, :].astype(F32) for k in range(2)]
    for z, field_ref, source_ref, material_ref, out_ref in (
        (0, low_ref, low_source_ref, low_material_ref, first_ref),
        (7, high_ref, high_source_ref, high_material_ref, last_ref),
    ):
        weight, coupling = lookup(material_ref[...], rows)
        lines = []
        for c in range(3):
            at = 8 * (c % 2) + z
            lines.append((before[c // 2][at:at + 1, :], after[c // 2][at:at + 1, :]))
            outer, inner = (0, 16) if z == 0 else (16, 0)
            value = field_ref[c, outer:outer + 16, :]
            beside = field_ref[c, inner:inner + 16, :]
            total = beside + row_sum(value, *lines[c]) + x_sum(value)
            partial = KEEP * value + weight * source_ref[c] + coupling * total
            out_ref[16 * c:16 * c + 16, :] = value.astype(BF16)
            out_ref[48 + 16 * c:64 + 16 * c, :] = partial.astype(BF16)
        out_ref[96:112, :] = coupling.astype(BF16)
        row = lax.broadcasted_iota(jnp.int32, (16, coupling.shape[1]), 0)
        packed = jnp.zeros(row.shape, F32)
        for c in range(3):
            for side in range(2):
                packed = jnp.where(row == 2 * c + side, lines[c][side], packed)
        out_ref[112:128, :] = packed.astype(BF16)


def stacked(lines, height):
    row = lax.broadcasted_iota(jnp.int32, (height, lines[0].shape[1]), 0)
    value = jnp.broadcast_to(lines[0], row.shape)
    for k in range(1, len(lines)):
        value = jnp.where(row == k, lines[k], value)
    return value


def column_of(row):
    length = row.shape[1]
    down = lax.broadcasted_iota(jnp.int32, (length, length), 0)
    along = lax.broadcasted_iota(jnp.int32, (length, length), 1)
    return jnp.sum(jnp.where(down == along, row, 0.0), axis=1, keepdims=True)


def relax(planes, stiff_ref, mass_ref, field_ref, source_ref, material_ref, before_ref, after_ref, below_ref, above_ref,
          right_ref, cells_ref, out_ref, send_ref, once_ref, scaled_ref, coupling_ref, plain_ref):
    rows = table_rows(stiff_ref, mass_ref)
    y_halo = [[r[16 * k:16 * k + 16, :].astype(F32) for k in range(4)] for r in (before_ref, after_ref)]
    z_halo = [[r[16 * k:16 * k + 16, :].astype(F32) for k in range(8)] for r in (below_ref, above_ref)]

    def y_plane(side, k):
        return y_halo[side][k // 2][8 * (k % 2):8 * (k % 2) + 8]

    row8 = lax.broadcasted_iota(jnp.int32, (8, field_ref.shape[-1]), 0)
    rims = []
    for c in range(3):
        once_ref[c, 0] = z_halo[0][3 + c] + z_halo[0][6] * field_ref[c, 0:16, :]
        once_ref[c, 9] = z_halo[1][3 + c] + z_halo[1][6] * field_ref[c, 112:128, :]
        sides = []
        for side, y in ((0, 0), (1, 15)):
            beside = line_rows(field_ref, y, c)
            at = 2 * c + side
            beside = beside + jnp.where(row8 == 0, z_halo[0][7][at:at + 1], 0.0)
            beside = beside + jnp.where(row8 == 7, z_halo[1][7][at:at + 1], 0.0)
            sides.append(y_plane(side, 3 + c) + y_plane(side, 6) * beside)
        rims.append(sides)
    for z in range(8):
        here = slice(16 * z, 16 * z + 16)
        weight, coupling = lookup(material_ref[here, :], rows)
        coupling_ref[here, :] = coupling
        for c in range(3):
            value = field_ref[c, here, :]
            lower = z_halo[0][c] if z == 0 else field_ref[c, 16 * z - 16:16 * z, :]
            upper = z_halo[1][c] if z == 7 else field_ref[c, 16 * z + 16:16 * z + 32, :]
            total = lower + upper + row_sum(value, y_plane(0, c)[z:z + 1], y_plane(1, c)[z:z + 1]) + x_sum(value)
            scaled = weight * source_ref[c, here, :]
            scaled_ref[c, here, :] = scaled
            once_ref[c, z + 1] = KEEP * value + scaled + coupling * total
    for z in range(8):
        here = slice(16 * z, 16 * z + 16)
        coupling = coupling_ref[here, :]
        for c in range(3):
            value = once_ref[c, z + 1]
            total = once_ref[c, z] + once_ref[c, z + 2] + x_sum(value)
            total = total + row_sum(value, rims[c][0][z:z + 1], rims[c][1][z:z + 1])
            result = KEEP * value + scaled_ref[c, here, :] + coupling * total
            out_ref[c, here, :] = result
            plain_ref[128 * c + 16 * z:128 * c + 16 * z + 16, :] = result.astype(BF16)

    width = field_ref.shape[-1]
    count = cells_ref.shape[1]
    cells = cells_ref[...].astype(F32)
    line = jnp.floor((cells + 0.5) * (1.0 / width))
    line_column = column_of(line)
    place_column = column_of(cells - width * line)
    along = lax.broadcasted_iota(jnp.int32, (count, width), 1).astype(F32)
    chosen = jnp.where(along == line_column, 1.0, 0.0).astype(BF16)
    picked = jnp.dot(chosen, plain_ref[...], preferred_element_type=F32)
    single = jnp.where(along == place_column, picked, 0.0).astype(BF16)
    spread = jnp.dot(single, jnp.ones((width, 128), BF16), preferred_element_type=F32)
    far = jnp.dot(right_ref[...], spread.astype(BF16), preferred_element_type=F32)
    ranks = 16
    lane = lax.broadcasted_iota(jnp.int32, (PLANE, 128), 1)
    parts = [jnp.zeros((PLANE, 128), F32) for _ in range(2)]
    for k in range(ranks):
        for z in range(planes):
            group = far[PLANE * (k * planes + z):PLANE * (k * planes + z + 1), :]
            at = z * ranks + k
            parts[at // 128] = jnp.where(lane == at % 128, group, parts[at // 128])
    down = lax.broadcasted_iota(jnp.int32, (128, 128), 0)
    across = lax.broadcasted_iota(jnp.int32, (128, 128), 1)
    traces = []
    for half in range(2):
        piece = jnp.where(down == across, spread[128 * half:128 * half + 128, :], 0.0)
        traces.append(jnp.sum(piece, axis=0, keepdims=True))
    tiles = send_ref.shape[0] // PLANE
    for to in range(PLANE):
        packet = stacked([parts[0][to:to + 1, :], parts[1][to:to + 1, :]] + traces, 4).astype(BF16)
        for tile in range(tiles):
            send_ref[to * tiles + tile] = packet


def middle(tiles, got_ref, send_ref):
    across = lax.rem(lax.axis_index("slab"), PLANE)
    tile = lax.axis_index("tile")
    total = jnp.sum(got_ref[...].astype(F32), axis=0)
    other = jnp.where(across == 0, PLANE - 1, 0)
    relay = []
    for b in range(3):
        wanted = tile + b - 1
        inside = (wanted >= 0) & (wanted < tiles)
        packet = got_ref[other * tiles + jnp.clip(wanted, 0, tiles - 1)].astype(F32)
        packet = jnp.where(inside, packet, 0.0)
        relay += [packet[2:3, :], packet[3:4, :]]
    high = total.astype(BF16).astype(F32)
    low = total - high
    for half in range(2):
        packet = stacked([high[half:half + 1, :], low[half:half + 1, :]] + relay, 8).astype(BF16)
        for z in range(8 * half, min(8 * half + 8, send_ref.shape[0])):
            send_ref[z] = packet


def masked_rows(rows, mask_ref, first):
    value = jnp.zeros((16, 256), F32)
    row = lax.broadcasted_iota(jnp.int32, value.shape, 0)
    for k, (low, high) in enumerate(rows):
        line = jnp.concatenate([low, high], axis=1) * mask_ref[first + k].astype(F32)
        value = jnp.where(row == k, line, value)
    return value.astype(BF16)


def products(rows, blocks, count):
    every = lax.dot_general(rows, blocks, (((1,), (1,)), ((), ())), preferred_element_type=F32)
    result = every[0:1, 0:256]
    for k in range(1, count):
        result = result + every[k:k + 1, 256 * k:256 * k + 256]
    return result


def near_inside(tiles, mask_ref, got_ref, near_ref, out_ref):
    across = lax.rem(lax.axis_index("slab"), PLANE)
    tile = lax.axis_index("tile")
    rows = []
    for a in range(-1, 2):
        for b in range(-1, 2):
            up, beside = across + a, tile + b
            inside = (up >= 0) & (up < PLANE) & (beside >= 0) & (beside < tiles)
            packet = got_ref[jnp.clip(up, 0, PLANE - 1) * tiles + jnp.clip(beside, 0, tiles - 1)].astype(F32)
            packet = jnp.where(inside, packet, 0.0)
            rows.append((packet[2:3, :], packet[3:4, :]))
    out_ref[...] = products(masked_rows(rows, mask_ref, 0), near_ref[...], 9)


def finish(planes, mask_ref, rank_ref, part_ref, relay_ref, near_ref, left_ref, out_ref):
    slab = lax.axis_index("slab")
    across = lax.rem(slab, PLANE)
    plane = lax.div(slab, PLANE)
    upward = across == PLANE - 1
    start = jnp.where(upward, plane + 1, plane - 1)
    edge = ((across == 0) | upward) & (start >= 0) & (start < planes)
    packet = jnp.where(edge, relay_ref[jnp.clip(start, 0, planes - 1)].astype(F32), 0.0)
    rows = [(packet[2 + 2 * b:3 + 2 * b, :], packet[3 + 2 * b:4 + 2 * b, :]) for b in range(3)]
    first = jnp.where(upward, 6, 0)
    blocks = near_ref[pl.ds(pl.multiple_of(256 * first, 256), 768), :]
    near = products(masked_rows(rows, mask_ref, first), blocks, 3)
    total = jnp.sum(relay_ref[...].astype(F32), axis=0)
    total = jnp.broadcast_to(total[0:1, :] + total[1:2, :], (8, 128))
    lane = lax.broadcasted_iota(jnp.int32, total.shape, 1)
    at = 16 * lax.rem(plane, 8)
    total = jnp.where((lane >= at) & (lane < at + rank_ref[0]), total, 0.0)
    high = total.astype(BF16).astype(F32)
    halves = jnp.concatenate([high, total - high], axis=0).astype(BF16)
    left = jnp.concatenate([left_ref[...]] * 8, axis=0)
    far = jnp.dot(halves, left, preferred_element_type=F32)
    out_ref[...] = part_ref[...] + near + far[0:1, :] + far[8:9, :]


def vmem():
    return pl.BlockSpec(memory_space=pltpu.VMEM)


def smem():
    return pl.BlockSpec(memory_space=pltpu.SMEM)


def exchange(first, last, axis):
    devices = lax.axis_size(axis)
    up = [(i, i + 1) for i in range(devices - 1)]
    down = [(j, i) for i, j in up]
    return lax.ppermute(last, axis, up), lax.ppermute(first, axis, down)


def local(initial_field, source, material, stiffness_table, mass_table, trace_cells, near_blocks, near_mask, far_left, far_right,
          block_ranks):
    slabs, tiles = lax.axis_size("slab"), lax.axis_size("tile")
    planes = slabs // PLANE
    field = initial_field.reshape(3, 128, 384)
    sources = source.reshape(3, 128, 384)
    cells = material.reshape(128, 384)
    face = jax.ShapeDtypeStruct((64, 384), BF16)
    params = pltpu.CompilerParams(vmem_limit_bytes=24 * 1024 * 1024)
    first, last = pl.pallas_call(
        y_faces,
        out_shape=(face, face),
        in_specs=[pl.BlockSpec(memory_space=pltpu.HBM)] * 5,
        out_specs=(vmem(), vmem()),
        scratch_shapes=[
            pltpu.SMEM((8,), F32), pltpu.SMEM((8,), F32), pltpu.VMEM((3, 128, 384), F32), pltpu.VMEM((3, 128, 384), F32),
            pltpu.VMEM((128, 384), jnp.int32), pltpu.SemaphoreType.DMA((5,)),
        ],
        compiler_params=pltpu.CompilerParams(vmem_limit_bytes=48 * 1024 * 1024),
    )(stiffness_table, mass_table, field, sources, cells)
    before, after = exchange(first, last, "tile")
    face = jax.ShapeDtypeStruct((128, 384), BF16)
    first, last = pl.pallas_call(
        z_faces,
        grid=(1,),
        out_shape=(face, face),
        in_specs=[
            smem(), smem(),
            pl.BlockSpec((3, 32, 384), lambda i: (0, 0, 0)), pl.BlockSpec((3, 32, 384), lambda i: (0, 3, 0)),
            pl.BlockSpec((3, 16, 384), lambda i: (0, 0, 0)), pl.BlockSpec((3, 16, 384), lambda i: (0, 7, 0)),
            pl.BlockSpec((16, 384), lambda i: (0, 0)), pl.BlockSpec((16, 384), lambda i: (7, 0)),
            pl.BlockSpec((64, 384), lambda i: (0, 0)), pl.BlockSpec((64, 384), lambda i: (0, 0)),
        ],
        out_specs=(pl.BlockSpec((128, 384), lambda i: (0, 0)), pl.BlockSpec((128, 384), lambda i: (0, 0))),
        compiler_params=params,
    )(stiffness_table, mass_table, field, field, sources, sources, cells, cells, before, after)
    below, above = exchange(first, last, "slab")
    members = PLANE * tiles
    result, send = pl.pallas_call(
        functools.partial(relax, planes),
        out_shape=(jax.ShapeDtypeStruct((3, 128, 384), F32), jax.ShapeDtypeStruct((members, 4, 128), BF16)),
        in_specs=[smem(), smem()] + [vmem()] * 9,
        out_specs=(vmem(), vmem()),
        scratch_shapes=[
            pltpu.VMEM((3, 10, 16, 384), F32),
            pltpu.VMEM((3, 128, 384), F32),
            pltpu.VMEM((128, 384), F32),
            pltpu.VMEM((384, 384), BF16),
        ],
        compiler_params=params,
    )(stiffness_table, mass_table, field, sources, cells, before, after, below, above,
      far_right.reshape(-1, 256), trace_cells.reshape(1, 256))
    ids = np.arange(slabs * tiles).reshape(planes, members)
    got = lax.all_to_all(send, BOTH, 0, 0, axis_index_groups=ids.tolist(), tiled=True)
    send = pl.pallas_call(
        functools.partial(middle, tiles),
        out_shape=jax.ShapeDtypeStruct((planes, 8, 128), BF16),
        in_specs=[vmem()],
        out_specs=vmem(),
        compiler_params=params,
    )(got)
    relay = lax.all_to_all(send, BOTH, 0, 0, axis_index_groups=ids.T.tolist(), tiled=True)
    mask = near_mask.reshape(9)
    blocks = near_blocks.reshape(-1, 256)
    part = pl.pallas_call(
        functools.partial(near_inside, tiles),
        out_shape=jax.ShapeDtypeStruct((1, 256), F32),
        in_specs=[smem(), vmem(), vmem()],
        out_specs=vmem(),
        compiler_params=params,
        cost_estimate=pl.CostEstimate(flops=2 * 16 * 2304 * 256, bytes_accessed=2304 * 512, transcendentals=0),
    )(mask, got, blocks)
    boundary = pl.pallas_call(
        functools.partial(finish, planes),
        out_shape=jax.ShapeDtypeStruct((1, 256), F32),
        in_specs=[smem(), smem()] + [vmem()] * 4,
        out_specs=vmem(),
        compiler_params=params,
    )(mask, block_ranks, part, relay, blocks, far_left.reshape(16, 256))
    return result.reshape(initial_field.shape), boundary.reshape(1, 1, 256)


def solution(mesh):
    placed = (
        P(None, "slab", "tile", None),
        P(None, "slab", "tile", None),
        P("slab", "tile", None),
        P(),
        P(),
        P("slab", "tile", None),
        P("slab", "tile", None, None, None),
        P("slab", "tile", None),
        P(None, "slab", "tile", None),
        P(None, None, "slab", "tile", None),
        P("slab"),
    )
    return jax.shard_map(
        local,
        mesh=mesh,
        in_specs=placed,
        out_specs=(P(None, "slab", "tile", None), P("slab", "tile", None)),
        check_vma=False,
    )
```

```python
import functools

import jax
import jax.numpy as jnp
import numpy as np
from jax import lax
from jax.experimental import pallas as pl
from jax.experimental.pallas import tpu as pltpu
from jax.sharding import PartitionSpec as P

RELAX = 0.8
KEEP = 1.0 - RELAX
PLANE = 8
F32 = jnp.float32
BF16 = jnp.bfloat16
BOTH = ("slab", "tile")


def table_rows(stiff_ref, mass_ref):
    rows = []
    for entry in range(8):
        stiffness = jnp.full((8, 128), stiff_ref[entry], F32)
        inverse = RELAX / (6.0 * stiffness + mass_ref[entry])
        rows.append((inverse[:1, :1], (stiffness * inverse)[:1, :1]))
    return rows


def lookup(material, rows):
    weight = jnp.broadcast_to(rows[0][0], material.shape)
    coupling = jnp.broadcast_to(rows[0][1], material.shape)
    for entry in range(1, 8):
        here = material == entry
        weight = jnp.where(here, rows[entry][0], weight)
        coupling = jnp.where(here, rows[entry][1], coupling)
    return weight, coupling


def x_sum(value):
    width = value.shape[-1]
    lane = lax.broadcasted_iota(jnp.int32, value.shape, value.ndim - 1)
    before = jnp.where(lane == 0, 0.0, pltpu.roll(value, 1, value.ndim - 1))
    after = jnp.where(lane == width - 1, 0.0, pltpu.roll(value, width - 1, value.ndim - 1))
    return before + after


def row_sum(value, first, last):
    length = value.shape[0]
    row = lax.broadcasted_iota(jnp.int32, value.shape, 0)
    before = jnp.where(row == 0, first, pltpu.roll(value, 1, 0))
    after = jnp.where(row == length - 1, last, pltpu.roll(value, length - 1, 0))
    return before + after


def line_rows(ref, y, *lead):
    lines = [ref[(*lead, slice(16 * z + y, 16 * z + y + 1), slice(None))] for z in range(8)]
    row = lax.broadcasted_iota(jnp.int32, (8, lines[0].shape[1]), 0)
    value = jnp.broadcast_to(lines[0], row.shape)
    for z in range(1, 8):
        value = jnp.where(row == z, lines[z], value)
    return value


def y_faces(stiff_hbm, mass_hbm, field_hbm, source_hbm, material_hbm, first_ref, last_ref,
            stiff_ref, mass_ref, field_ref, source_ref, material_ref, sems):
    pairs = ((stiff_hbm, stiff_ref), (mass_hbm, mass_ref), (material_hbm, material_ref), (field_hbm, field_ref), (source_hbm, source_ref))
    copies = [pltpu.make_async_copy(src, dst, sems.at[k]) for k, (src, dst) in enumerate(pairs)]
    for copy in copies:
        copy.start()
    for copy in copies:
        copy.wait()
    rows = table_rows(stiff_ref, mass_ref)
    for y, inner, out_ref in ((0, 1, first_ref), (15, 14, last_ref)):
        weight, coupling = lookup(line_rows(material_ref, y), rows)
        values, partials = [], []
        for c in range(3):
            value = line_rows(field_ref, y, c)
            beside = line_rows(field_ref, inner, c)
            sources = line_rows(source_ref, y, c)
            total = beside + row_sum(value, 0.0, 0.0) + x_sum(value)
            values.append(value)
            partials.append(KEEP * value + weight * sources + coupling * total)
        planes = values + partials + [coupling, jnp.zeros_like(coupling)]
        for pair in range(4):
            both = jnp.concatenate(planes[2 * pair:2 * pair + 2], axis=0)
            out_ref[16 * pair:16 * pair + 16, :] = both.astype(BF16)


def z_faces(stiff_ref, mass_ref, low_ref, high_ref, low_source_ref, high_source_ref, low_material_ref, high_material_ref,
            before_ref, after_ref, first_ref, last_ref):
    rows = table_rows(stiff_ref, mass_ref)
    before = [before_ref[16 * k:16 * k + 16, :].astype(F32) for k in range(2)]
    after = [after_ref[16 * k:16 * k + 16, :].astype(F32) for k in range(2)]
    for z, field_ref, source_ref, material_ref, out_ref in (
        (0, low_ref, low_source_ref, low_material_ref, first_ref),
        (7, high_ref, high_source_ref, high_material_ref, last_ref),
    ):
        weight, coupling = lookup(material_ref[...], rows)
        lines = []
        for c in range(3):
            at = 8 * (c % 2) + z
            lines.append((before[c // 2][at:at + 1, :], after[c // 2][at:at + 1, :]))
            outer, inner = (0, 16) if z == 0 else (16, 0)
            value = field_ref[c, outer:outer + 16, :]
            beside = field_ref[c, inner:inner + 16, :]
            total = beside + row_sum(value, *lines[c]) + x_sum(value)
            partial = KEEP * value + weight * source_ref[c] + coupling * total
            out_ref[16 * c:16 * c + 16, :] = value.astype(BF16)
            out_ref[48 + 16 * c:64 + 16 * c, :] = partial.astype(BF16)
        out_ref[96:112, :] = coupling.astype(BF16)
        row = lax.broadcasted_iota(jnp.int32, (16, coupling.shape[1]), 0)
        packed = jnp.zeros(row.shape, F32)
        for c in range(3):
            for side in range(2):
                packed = jnp.where(row == 2 * c + side, lines[c][side], packed)
        out_ref[112:128, :] = packed.astype(BF16)


def stacked(lines, height):
    row = lax.broadcasted_iota(jnp.int32, (height, lines[0].shape[1]), 0)
    value = jnp.broadcast_to(lines[0], row.shape)
    for k in range(1, len(lines)):
        value = jnp.where(row == k, lines[k], value)
    return value


def column_of(row):
    length = row.shape[1]
    down = lax.broadcasted_iota(jnp.int32, (length, length), 0)
    along = lax.broadcasted_iota(jnp.int32, (length, length), 1)
    return jnp.sum(jnp.where(down == along, row, 0.0), axis=1, keepdims=True)


def bands(ref, count):
    return [ref[16 * k:16 * k + 16, :].astype(F32) for k in range(count)]


EDGES = (0, 1, 6, 7)


def relax_inner(stiff_ref, mass_ref, field_ref, source_ref, material_ref, before_ref, after_ref, cells_ref,
                once_ref, scaled_ref, coupling_ref, rim_ref, out_ref, edge_ref, place_ref, spread_ref, plain_ref):
    rows = table_rows(stiff_ref, mass_ref)
    halo = [bands(before_ref, 4), bands(after_ref, 4)]

    def y_plane(side, k):
        return halo[side][k // 2][8 * (k % 2):8 * (k % 2) + 8]

    for c in range(3):
        for side, y in ((0, 0), (1, 15)):
            rim_ref[6 * side + c] = y_plane(side, 3 + c) + y_plane(side, 6) * line_rows(field_ref, y, c)
    for side in range(2):
        rim_ref[6 * side + 3] = y_plane(side, 6)
    for z in range(8):
        here = slice(16 * z, 16 * z + 16)
        weight, coupling = lookup(material_ref[here, :], rows)
        coupling_ref[here, :] = coupling
        for c in range(3):
            value = field_ref[c, here, :]
            total = row_sum(value, y_plane(0, c)[z:z + 1], y_plane(1, c)[z:z + 1]) + x_sum(value)
            if z > 0:
                total = total + field_ref[c, 16 * z - 16:16 * z, :]
            if z < 7:
                total = total + field_ref[c, 16 * z + 16:16 * z + 32, :]
            scaled = weight * source_ref[c, here, :]
            scaled_ref[c, here, :] = scaled
            once_ref[c, here, :] = KEEP * value + scaled + coupling * total
    for z in range(2, 6):
        here = slice(16 * z, 16 * z + 16)
        for c in range(3):
            value = once_ref[c, here, :]
            total = once_ref[c, 16 * z - 16:16 * z, :] + once_ref[c, 16 * z + 16:16 * z + 32, :] + x_sum(value)
            total = total + row_sum(value, rim_ref[c, z:z + 1, :], rim_ref[6 + c, z:z + 1, :])
            result = KEEP * value + scaled_ref[c, here, :] + coupling_ref[here, :] * total
            out_ref[c, 16 * z - 32:16 * z - 16, :] = result
            at = 64 * c + 16 * z - 32
            plain_ref[at:at + 16, :] = result.astype(BF16)

    width = field_ref.shape[-1]
    count = cells_ref.shape[1]
    cells = cells_ref[...].astype(F32)
    line = jnp.floor((cells + 0.5) * (1.0 / width))
    place_column = column_of(cells - width * line)
    line_column = column_of(line)
    place_ref[...] = jnp.broadcast_to(place_column, (count, 128))
    along = lax.broadcasted_iota(jnp.int32, (count, 192), 1).astype(F32)
    part = jnp.floor(along * (1.0 / 64) + 0.001)
    shift = along - 64.0 * part
    inner = 128.0 * part + shift + 32.0
    outer = 128.0 * part + jnp.where(shift < 32.0, shift, shift + 64.0)
    edge_ref[...] = jnp.where(outer == line_column, 1.0, 0.0).astype(BF16)
    chosen = jnp.where(inner == line_column, 1.0, 0.0).astype(BF16)
    picked = jnp.dot(chosen, plain_ref[...], preferred_element_type=F32)
    spread_ref[...] = spread_of(picked, place_column)


def spread_of(picked, place_column):
    along = lax.broadcasted_iota(jnp.int32, picked.shape, 1).astype(F32)
    single = jnp.where(along == place_column, picked, 0.0).astype(BF16)
    return jnp.dot(single, jnp.ones((picked.shape[1], 128), BF16), preferred_element_type=F32)


def relax_edges(planes, field_ref, once_ref, scaled_ref, coupling_ref, rim_ref, inner_ref, edge_ref, place_ref, spread_ref,
                below_ref, above_ref, right_ref, out_ref, send_ref, plain_ref):
    halo = [bands(below_ref, 8), bands(above_ref, 8)]
    row8 = lax.broadcasted_iota(jnp.int32, (8, field_ref.shape[-1]), 0)
    for c in range(3):
        out_ref[c, 32:96, :] = inner_ref[c]
        once = {z: once_ref[c, 16 * z:16 * z + 16, :] for z in (1, 2, 5, 6)}
        once[0] = once_ref[c, 0:16, :] + coupling_ref[0:16, :] * halo[0][c]
        once[7] = once_ref[c, 112:128, :] + coupling_ref[112:128, :] * halo[1][c]
        once[-1] = halo[0][3 + c] + halo[0][6] * field_ref[c, 0:16, :]
        once[8] = halo[1][3 + c] + halo[1][6] * field_ref[c, 112:128, :]
        rims = []
        for side in range(2):
            at = 2 * c + side
            corner = jnp.where(row8 == 0, halo[0][7][at:at + 1], 0.0) + jnp.where(row8 == 7, halo[1][7][at:at + 1], 0.0)
            rims.append(rim_ref[6 * side + c] + rim_ref[6 * side + 3] * corner)
        for order, z in enumerate(EDGES):
            here = slice(16 * z, 16 * z + 16)
            total = once[z - 1] + once[z + 1] + x_sum(once[z])
            total = total + row_sum(once[z], rims[0][z:z + 1], rims[1][z:z + 1])
            result = KEEP * once[z] + scaled_ref[c, here, :] + coupling_ref[here, :] * total
            out_ref[c, here, :] = result
            at = 64 * c + 16 * order
            plain_ref[at:at + 16, :] = result.astype(BF16)

    picked = jnp.dot(edge_ref[...], plain_ref[...], preferred_element_type=F32)
    spread = spread_ref[...] + spread_of(picked, place_ref[:, 0:1])
    far = jnp.dot(right_ref[...], spread.astype(BF16), preferred_element_type=F32)
    ranks = 16
    lane = lax.broadcasted_iota(jnp.int32, (PLANE, 128), 1)
    parts = [jnp.zeros((PLANE, 128), F32) for _ in range(2)]
    for k in range(ranks):
        for z in range(planes):
            group = far[PLANE * (k * planes + z):PLANE * (k * planes + z + 1), :]
            at = z * ranks + k
            parts[at // 128] = jnp.where(lane == at % 128, group, parts[at // 128])
    down = lax.broadcasted_iota(jnp.int32, (128, 128), 0)
    across = lax.broadcasted_iota(jnp.int32, (128, 128), 1)
    traces = []
    for half in range(2):
        piece = jnp.where(down == across, spread[128 * half:128 * half + 128, :], 0.0)
        traces.append(jnp.sum(piece, axis=0, keepdims=True))
    tiles = send_ref.shape[0] // PLANE
    for to in range(PLANE):
        packet = stacked([parts[0][to:to + 1, :], parts[1][to:to + 1, :]] + traces, 4).astype(BF16)
        for tile in range(tiles):
            send_ref[to * tiles + tile] = packet


def middle(tiles, got_ref, send_ref):
    across = lax.rem(lax.axis_index("slab"), PLANE)
    tile = lax.axis_index("tile")
    total = jnp.sum(got_ref[...].astype(F32), axis=0)
    other = jnp.where(across == 0, PLANE - 1, 0)
    relay = []
    for b in range(3):
        wanted = tile + b - 1
        inside = (wanted >= 0) & (wanted < tiles)
        packet = got_ref[other * tiles + jnp.clip(wanted, 0, tiles - 1)].astype(F32)
        packet = jnp.where(inside, packet, 0.0)
        relay += [packet[2:3, :], packet[3:4, :]]
    high = total.astype(BF16).astype(F32)
    low = total - high
    for half in range(2):
        packet = stacked([high[half:half + 1, :], low[half:half + 1, :]] + relay, 8).astype(BF16)
        for z in range(8 * half, min(8 * half + 8, send_ref.shape[0])):
            send_ref[z] = packet


def masked_rows(rows, mask_ref, first):
    value = jnp.zeros((16, 256), F32)
    row = lax.broadcasted_iota(jnp.int32, value.shape, 0)
    for k, (low, high) in enumerate(rows):
        line = jnp.concatenate([low, high], axis=1) * mask_ref[first + k].astype(F32)
        value = jnp.where(row == k, line, value)
    return value.astype(BF16)


def products(rows, blocks, count):
    every = lax.dot_general(rows, blocks, (((1,), (1,)), ((), ())), preferred_element_type=F32)
    result = every[0:1, 0:256]
    for k in range(1, count):
        result = result + every[k:k + 1, 256 * k:256 * k + 256]
    return result


def near_inside(tiles, mask_ref, got_ref, near_ref, out_ref):
    across = lax.rem(lax.axis_index("slab"), PLANE)
    tile = lax.axis_index("tile")
    rows = []
    for a in range(-1, 2):
        for b in range(-1, 2):
            up, beside = across + a, tile + b
            inside = (up >= 0) & (up < PLANE) & (beside >= 0) & (beside < tiles)
            packet = got_ref[jnp.clip(up, 0, PLANE - 1) * tiles + jnp.clip(beside, 0, tiles - 1)].astype(F32)
            packet = jnp.where(inside, packet, 0.0)
            rows.append((packet[2:3, :], packet[3:4, :]))
    out_ref[...] = products(masked_rows(rows, mask_ref, 0), near_ref[...], 9)


def finish(planes, mask_ref, rank_ref, part_ref, relay_ref, near_ref, left_ref, out_ref):
    slab = lax.axis_index("slab")
    across = lax.rem(slab, PLANE)
    plane = lax.div(slab, PLANE)
    upward = across == PLANE - 1
    start = jnp.where(upward, plane + 1, plane - 1)
    edge = ((across == 0) | upward) & (start >= 0) & (start < planes)
    packet = jnp.where(edge, relay_ref[jnp.clip(start, 0, planes - 1)].astype(F32), 0.0)
    rows = [(packet[2 + 2 * b:3 + 2 * b, :], packet[3 + 2 * b:4 + 2 * b, :]) for b in range(3)]
    first = jnp.where(upward, 6, 0)
    blocks = near_ref[pl.ds(pl.multiple_of(256 * first, 256), 768), :]
    near = products(masked_rows(rows, mask_ref, first), blocks, 3)
    total = jnp.sum(relay_ref[...].astype(F32), axis=0)
    total = jnp.broadcast_to(total[0:1, :] + total[1:2, :], (8, 128))
    lane = lax.broadcasted_iota(jnp.int32, total.shape, 1)
    at = 16 * lax.rem(plane, 8)
    total = jnp.where((lane >= at) & (lane < at + rank_ref[0]), total, 0.0)
    high = total.astype(BF16).astype(F32)
    halves = jnp.concatenate([high, total - high], axis=0).astype(BF16)
    left = jnp.concatenate([left_ref[...]] * 8, axis=0)
    far = jnp.dot(halves, left, preferred_element_type=F32)
    out_ref[...] = part_ref[...] + near + far[0:1, :] + far[8:9, :]


def vmem():
    return pl.BlockSpec(memory_space=pltpu.VMEM)


def smem():
    return pl.BlockSpec(memory_space=pltpu.SMEM)


def exchange(first, last, axis):
    devices = lax.axis_size(axis)
    up = [(i, i + 1) for i in range(devices - 1)]
    down = [(j, i) for i, j in up]
    return lax.ppermute(last, axis, up), lax.ppermute(first, axis, down)


def local(initial_field, source, material, stiffness_table, mass_table, trace_cells, near_blocks, near_mask, far_left, far_right,
          block_ranks):
    slabs, tiles = lax.axis_size("slab"), lax.axis_size("tile")
    planes = slabs // PLANE
    field = initial_field.reshape(3, 128, 384)
    sources = source.reshape(3, 128, 384)
    cells = material.reshape(128, 384)
    volume = jax.ShapeDtypeStruct((3, 128, 384), F32)
    face = jax.ShapeDtypeStruct((64, 384), BF16)
    params = pltpu.CompilerParams(vmem_limit_bytes=24 * 1024 * 1024)
    first, last = pl.pallas_call(
        y_faces,
        out_shape=(face, face),
        in_specs=[pl.BlockSpec(memory_space=pltpu.HBM)] * 5,
        out_specs=(vmem(), vmem()),
        scratch_shapes=[
            pltpu.SMEM((8,), F32), pltpu.SMEM((8,), F32), pltpu.VMEM((3, 128, 384), F32), pltpu.VMEM((3, 128, 384), F32),
            pltpu.VMEM((128, 384), jnp.int32), pltpu.SemaphoreType.DMA((5,)),
        ],
        compiler_params=pltpu.CompilerParams(vmem_limit_bytes=56000 * 1024),
    )(stiffness_table, mass_table, field, sources, cells)
    before, after = exchange(first, last, "tile")
    face = jax.ShapeDtypeStruct((128, 384), BF16)
    first, last = pl.pallas_call(
        z_faces,
        grid=(1,),
        out_shape=(face, face),
        in_specs=[
            smem(), smem(),
            pl.BlockSpec((3, 32, 384), lambda i: (0, 0, 0)), pl.BlockSpec((3, 32, 384), lambda i: (0, 3, 0)),
            pl.BlockSpec((3, 16, 384), lambda i: (0, 0, 0)), pl.BlockSpec((3, 16, 384), lambda i: (0, 7, 0)),
            pl.BlockSpec((16, 384), lambda i: (0, 0)), pl.BlockSpec((16, 384), lambda i: (7, 0)),
            pl.BlockSpec((64, 384), lambda i: (0, 0)), pl.BlockSpec((64, 384), lambda i: (0, 0)),
        ],
        out_specs=(pl.BlockSpec((128, 384), lambda i: (0, 0)), pl.BlockSpec((128, 384), lambda i: (0, 0))),
        compiler_params=params,
    )(stiffness_table, mass_table, field, field, sources, sources, cells, cells, before, after)
    below, above = exchange(first, last, "slab")
    members = PLANE * tiles
    state = pl.pallas_call(
        relax_inner,
        out_shape=(
            volume, volume, jax.ShapeDtypeStruct((128, 384), F32), jax.ShapeDtypeStruct((12, 8, 384), F32),
            jax.ShapeDtypeStruct((3, 64, 384), F32), jax.ShapeDtypeStruct((256, 192), BF16),
            jax.ShapeDtypeStruct((256, 128), F32), jax.ShapeDtypeStruct((256, 128), F32),
        ),
        in_specs=[smem(), smem()] + [vmem()] * 6,
        out_specs=(vmem(),) * 8,
        scratch_shapes=[pltpu.VMEM((192, 384), BF16)],
        compiler_params=params,
        cost_estimate=pl.CostEstimate(flops=6_000_000, bytes_accessed=4_000_000, transcendentals=0),
    )(stiffness_table, mass_table, field, sources, cells, before, after, trace_cells.reshape(1, 256))
    result, send = pl.pallas_call(
        functools.partial(relax_edges, planes),
        out_shape=(volume, jax.ShapeDtypeStruct((members, 4, 128), BF16)),
        in_specs=[vmem()] * 12,
        out_specs=(vmem(), vmem()),
        scratch_shapes=[pltpu.VMEM((192, 384), BF16)],
        compiler_params=params,
    )(field, *state, below, above, far_right.reshape(-1, 256))
    ids = np.arange(slabs * tiles).reshape(planes, members)
    got = lax.all_to_all(send, BOTH, 0, 0, axis_index_groups=ids.tolist(), tiled=True)
    send = pl.pallas_call(
        functools.partial(middle, tiles),
        out_shape=jax.ShapeDtypeStruct((planes, 8, 128), BF16),
        in_specs=[vmem()],
        out_specs=vmem(),
        compiler_params=params,
    )(got)
    relay = lax.all_to_all(send, BOTH, 0, 0, axis_index_groups=ids.T.tolist(), tiled=True)
    mask = near_mask.reshape(9)
    blocks = near_blocks.reshape(-1, 256)
    part = pl.pallas_call(
        functools.partial(near_inside, tiles),
        out_shape=jax.ShapeDtypeStruct((1, 256), F32),
        in_specs=[smem(), vmem(), vmem()],
        out_specs=vmem(),
        compiler_params=params,
        cost_estimate=pl.CostEstimate(flops=2 * 16 * 2304 * 256, bytes_accessed=2304 * 512, transcendentals=0),
    )(mask, got, blocks)
    boundary = pl.pallas_call(
        functools.partial(finish, planes),
        out_shape=jax.ShapeDtypeStruct((1, 256), F32),
        in_specs=[smem(), smem()] + [vmem()] * 4,
        out_specs=vmem(),
        compiler_params=params,
    )(mask, block_ranks, part, relay, blocks, far_left.reshape(16, 256))
    return result.reshape(initial_field.shape), boundary.reshape(1, 1, 256)


def solution(mesh):
    placed = (
        P(None, "slab", "tile", None),
        P(None, "slab", "tile", None),
        P("slab", "tile", None),
        P(),
        P(),
        P("slab", "tile", None),
        P("slab", "tile", None, None, None),
        P("slab", "tile", None),
        P(None, "slab", "tile", None),
        P(None, None, "slab", "tile", None),
        P("slab"),
    )
    return jax.shard_map(
        local,
        mesh=mesh,
        in_specs=placed,
        out_specs=(P(None, "slab", "tile", None), P("slab", "tile", None)),
        check_vma=False,
    )
```

```python
import functools

import jax
import jax.numpy as jnp
import numpy as np
from jax import lax
from jax.experimental import pallas as pl
from jax.experimental.pallas import tpu as pltpu
from jax.sharding import PartitionSpec as P

RELAX = 0.8
KEEP = 1.0 - RELAX
PLANE = 8
F32 = jnp.float32
BF16 = jnp.bfloat16
BOTH = ("slab", "tile")


def table_rows(stiff_ref, mass_ref, width):
    weights, couplings = [], []
    for entry in range(8):
        stiffness = jnp.full((1, width), stiff_ref[entry], F32)
        inverse = RELAX / (6.0 * stiffness + mass_ref[entry])
        weights.append(inverse)
        couplings.append(stiffness * inverse)
    return weights + couplings


def ready_rows(table_ref):
    return [table_ref[k:k + 1, :] for k in range(16)]


def lookup(material, rows):
    weight = jnp.broadcast_to(rows[0], material.shape)
    coupling = jnp.broadcast_to(rows[8], material.shape)
    for entry in range(1, 8):
        here = material == entry
        weight = jnp.where(here, rows[entry], weight)
        coupling = jnp.where(here, rows[8 + entry], coupling)
    return weight, coupling


def x_sum(value):
    width = value.shape[-1]
    lane = lax.broadcasted_iota(jnp.int32, value.shape, value.ndim - 1)
    before = jnp.where(lane == 0, 0.0, pltpu.roll(value, 1, value.ndim - 1))
    after = jnp.where(lane == width - 1, 0.0, pltpu.roll(value, width - 1, value.ndim - 1))
    return before + after


def row_sum(value, first, last):
    length = value.shape[0]
    row = lax.broadcasted_iota(jnp.int32, value.shape, 0)
    before = jnp.where(row == 0, first, pltpu.roll(value, 1, 0))
    after = jnp.where(row == length - 1, last, pltpu.roll(value, length - 1, 0))
    return before + after


def line_rows(ref, y, *lead):
    lines = [ref[(*lead, slice(16 * z + y, 16 * z + y + 1), slice(None))] for z in range(8)]
    row = lax.broadcasted_iota(jnp.int32, (8, lines[0].shape[1]), 0)
    value = jnp.broadcast_to(lines[0], row.shape)
    for z in range(1, 8):
        value = jnp.where(row == z, lines[z], value)
    return value


def y_faces(stiff_hbm, mass_hbm, field_hbm, source_hbm, material_hbm, first_ref, last_ref, table_ref,
            stiff_ref, mass_ref, field_ref, source_ref, material_ref, sems):
    pairs = [(stiff_hbm, stiff_ref), (mass_hbm, mass_ref)]
    pairs += [(field_hbm.at[:, :, y, :], field_ref.at[k]) for k, y in enumerate((0, 15, 1, 14))]
    pairs += [(source_hbm.at[:, :, y, :], source_ref.at[k]) for k, y in enumerate((0, 15))]
    pairs += [(material_hbm.at[:, y, :], material_ref.at[k]) for k, y in enumerate((0, 15))]
    copies = [pltpu.make_async_copy(src, dst, sems.at[k]) for k, (src, dst) in enumerate(pairs)]
    for copy in copies:
        copy.start()
    for copy in copies:
        copy.wait()
    rows = table_rows(stiff_ref, mass_ref, table_ref.shape[1])
    table_ref[...] = jnp.concatenate(rows, axis=0)
    for k, out_ref in enumerate((first_ref, last_ref)):
        weight, coupling = lookup(material_ref[k], rows)
        values, partials = [], []
        for c in range(3):
            value = field_ref[k, c]
            total = field_ref[2 + k, c] + row_sum(value, 0.0, 0.0) + x_sum(value)
            values.append(value)
            partials.append(KEEP * value + weight * source_ref[k, c] + coupling * total)
        planes = values + partials + [coupling, jnp.zeros_like(coupling)]
        for pair in range(4):
            both = jnp.concatenate(planes[2 * pair:2 * pair + 2], axis=0)
            out_ref[16 * pair:16 * pair + 16, :] = both.astype(BF16)


def z_faces(table_ref, field_ref, source_ref, material_ref, before_ref, after_ref, far_ref, pair_ref):
    even = lax.rem(lax.axis_index("slab"), 2) == 0
    rows = ready_rows(table_ref)
    before = bands(before_ref, 2)
    after = bands(after_ref, 2)
    faces = []
    for z, beyond in ((0, 1), (7, 6)):
        here, inner = slice(16 * z, 16 * z + 16), slice(16 * beyond, 16 * beyond + 16)
        weight, coupling = lookup(material_ref[here, :], rows)
        lines, values, partials = [], [], []
        for c in range(3):
            at = 8 * (c % 2) + z
            lines += [before[c // 2][at:at + 1, :], after[c // 2][at:at + 1, :]]
            value = field_ref[c, here, :]
            total = field_ref[c, inner, :] + row_sum(value, lines[2 * c], lines[2 * c + 1]) + x_sum(value)
            values.append(value)
            partials.append(KEEP * value + weight * source_ref[c, here, :] + coupling * total)
        faces.append(values + partials + [coupling, stacked(lines, 16)])
    for k, (first, last) in enumerate(zip(*faces)):
        here = slice(16 * k, 16 * k + 16)
        far_ref[here, :] = jnp.where(even, first, last).astype(BF16)
        pair_ref[here, :] = jnp.where(even, last, first).astype(BF16)


def stacked(lines, height):
    row = lax.broadcasted_iota(jnp.int32, (height, lines[0].shape[1]), 0)
    value = jnp.zeros(row.shape, F32)
    for k in range(len(lines)):
        value = jnp.where(row == k, lines[k], value)
    return value


def column_of(row):
    length = row.shape[1]
    down = lax.broadcasted_iota(jnp.int32, (length, length), 0)
    along = lax.broadcasted_iota(jnp.int32, (length, length), 1)
    return jnp.sum(jnp.where(down == along, row, 0.0), axis=1, keepdims=True)


def bands(ref, count):
    return [ref[16 * k:16 * k + 16, :].astype(F32) for k in range(count)]


EDGES = (0, 1, 6, 7)


def relax_inner(table_ref, field_ref, source_ref, material_ref, before_ref, after_ref, cells_ref,
                once_ref, scaled_ref, coupling_ref, rim_ref, out_hbm, edge_ref, place_ref, spread_ref, plain_ref, out_ref, sems):
    rows = ready_rows(table_ref)
    halo = [bands(before_ref, 4), bands(after_ref, 4)]

    def y_plane(side, k):
        return halo[side][k // 2][8 * (k % 2):8 * (k % 2) + 8]

    for c in range(3):
        for side, y in ((0, 0), (1, 15)):
            rim_ref[6 * side + c] = y_plane(side, 3 + c) + y_plane(side, 6) * line_rows(field_ref, y, c)
    for side in range(2):
        rim_ref[6 * side + 3] = y_plane(side, 6)
    for z in range(8):
        here = slice(16 * z, 16 * z + 16)
        weight, coupling = lookup(material_ref[here, :], rows)
        coupling_ref[here, :] = coupling
        for c in range(3):
            value = field_ref[c, here, :]
            total = row_sum(value, y_plane(0, c)[z:z + 1], y_plane(1, c)[z:z + 1]) + x_sum(value)
            if z > 0:
                total = total + field_ref[c, 16 * z - 16:16 * z, :]
            if z < 7:
                total = total + field_ref[c, 16 * z + 16:16 * z + 32, :]
            scaled = weight * source_ref[c, here, :]
            scaled_ref[c, here, :] = scaled
            once_ref[c, here, :] = KEEP * value + scaled + coupling * total
    for z in range(2, 6):
        here = slice(16 * z, 16 * z + 16)
        for c in range(3):
            value = once_ref[c, here, :]
            total = once_ref[c, 16 * z - 16:16 * z, :] + once_ref[c, 16 * z + 16:16 * z + 32, :] + x_sum(value)
            total = total + row_sum(value, rim_ref[c, z:z + 1, :], rim_ref[6 + c, z:z + 1, :])
            result = KEEP * value + scaled_ref[c, here, :] + coupling_ref[here, :] * total
            out_ref[c, 16 * z - 32:16 * z - 16, :] = result
            at = 64 * c + 16 * z - 32
            plain_ref[at:at + 16, :] = result.astype(BF16)
    copies = [pltpu.make_async_copy(out_ref.at[c], out_hbm.at[c, pl.ds(32, 64), :], sems.at[c]) for c in range(3)]
    for copy in copies:
        copy.start()

    width = field_ref.shape[-1]
    count = cells_ref.shape[1]
    cells = cells_ref[...].astype(F32)
    line = jnp.floor((cells + 0.5) * (1.0 / width))
    place_column = column_of(cells - width * line)
    line_column = column_of(line)
    place_ref[...] = jnp.broadcast_to(place_column, (count, 128))
    along = lax.broadcasted_iota(jnp.int32, (count, 192), 1).astype(F32)
    part = jnp.floor(along * (1.0 / 64) + 0.001)
    shift = along - 64.0 * part
    inner = 128.0 * part + shift + 32.0
    outer = 128.0 * part + jnp.where(shift < 32.0, shift, shift + 64.0)
    edge_ref[...] = jnp.where(outer == line_column, 1.0, 0.0).astype(BF16)
    chosen = jnp.where(inner == line_column, 1.0, 0.0).astype(BF16)
    picked = jnp.dot(chosen, plain_ref[...], preferred_element_type=F32)
    spread_ref[...] = spread_of(picked, place_column)
    for copy in copies:
        copy.wait()


def spread_of(picked, place_column):
    along = lax.broadcasted_iota(jnp.int32, picked.shape, 1).astype(F32)
    single = jnp.where(along == place_column, picked, 0.0).astype(BF16)
    return jnp.dot(single, jnp.ones((picked.shape[1], 128), BF16), preferred_element_type=F32)


def relax_edges(planes, field_ref, once_ref, scaled_ref, coupling_ref, rim_ref, edge_ref, place_ref, spread_ref,
                far_ref, pair_ref, right_ref, out_ref, send_ref, plain_ref):
    even = lax.rem(lax.axis_index("slab"), 2) == 0
    both = list(zip(bands(far_ref, 8), bands(pair_ref, 8)))
    halo = [[jnp.where(even, far, pair) for far, pair in both], [jnp.where(even, pair, far) for far, pair in both]]
    row8 = lax.broadcasted_iota(jnp.int32, (8, field_ref.shape[-1]), 0)
    for c in range(3):
        once = {z: once_ref[c, 16 * z:16 * z + 16, :] for z in (1, 2, 5, 6)}
        once[0] = once_ref[c, 0:16, :] + coupling_ref[0:16, :] * halo[0][c]
        once[7] = once_ref[c, 112:128, :] + coupling_ref[112:128, :] * halo[1][c]
        once[-1] = halo[0][3 + c] + halo[0][6] * field_ref[c, 0:16, :]
        once[8] = halo[1][3 + c] + halo[1][6] * field_ref[c, 112:128, :]
        rims = []
        for side in range(2):
            at = 2 * c + side
            corner = jnp.where(row8 == 0, halo[0][7][at:at + 1], 0.0) + jnp.where(row8 == 7, halo[1][7][at:at + 1], 0.0)
            rims.append(rim_ref[6 * side + c] + rim_ref[6 * side + 3] * corner)
        for order, z in enumerate(EDGES):
            here = slice(16 * z, 16 * z + 16)
            total = once[z - 1] + once[z + 1] + x_sum(once[z])
            total = total + row_sum(once[z], rims[0][z:z + 1], rims[1][z:z + 1])
            result = KEEP * once[z] + scaled_ref[c, here, :] + coupling_ref[here, :] * total
            out_ref[c, 16 * order:16 * order + 16, :] = result
            at = 64 * c + 16 * order
            plain_ref[at:at + 16, :] = result.astype(BF16)

    picked = jnp.dot(edge_ref[...], plain_ref[...], preferred_element_type=F32)
    spread = spread_ref[...] + spread_of(picked, place_ref[:, 0:1])
    far = jnp.dot(right_ref[...], spread.astype(BF16), preferred_element_type=F32)
    ranks = 16
    lane = lax.broadcasted_iota(jnp.int32, (PLANE, 128), 1)
    parts = [jnp.zeros((PLANE, 128), F32) for _ in range(2)]
    for k in range(ranks):
        for z in range(planes):
            group = far[PLANE * (k * planes + z):PLANE * (k * planes + z + 1), :]
            at = z * ranks + k
            parts[at // 128] = jnp.where(lane == at % 128, group, parts[at // 128])
    down = lax.broadcasted_iota(jnp.int32, (128, 128), 0)
    across = lax.broadcasted_iota(jnp.int32, (128, 128), 1)
    traces = []
    for half in range(2):
        piece = jnp.where(down == across, spread[128 * half:128 * half + 128, :], 0.0)
        traces.append(jnp.sum(piece, axis=0, keepdims=True))
    tiles = send_ref.shape[0] // PLANE
    for to in range(PLANE):
        packet = stacked([parts[0][to:to + 1, :], parts[1][to:to + 1, :]] + traces, 4).astype(BF16)
        for tile in range(tiles):
            send_ref[to * tiles + tile] = packet


def assemble(inner_hbm, edges_ref, out_hbm, sems):
    del inner_hbm
    copies = []
    for c in range(3):
        for k, at in enumerate((0, 96)):
            target = out_hbm.at[c, pl.ds(at, 32), :]
            copies.append(pltpu.make_async_copy(edges_ref.at[c, pl.ds(32 * k, 32), :], target, sems.at[2 * c + k]))
    for copy in copies:
        copy.start()
    for copy in copies:
        copy.wait()


def middle(tiles, got_ref, send_ref):
    across = lax.rem(lax.axis_index("slab"), PLANE)
    tile = lax.axis_index("tile")
    total = jnp.sum(got_ref[...].astype(F32), axis=0)
    other = jnp.where(across == 0, PLANE - 1, 0)
    relay = []
    for b in range(3):
        wanted = tile + b - 1
        inside = (wanted >= 0) & (wanted < tiles)
        packet = got_ref[other * tiles + jnp.clip(wanted, 0, tiles - 1)].astype(F32)
        packet = jnp.where(inside, packet, 0.0)
        relay += [packet[2:3, :], packet[3:4, :]]
    high = total.astype(BF16).astype(F32)
    low = total - high
    for half in range(2):
        packet = stacked([high[half:half + 1, :], low[half:half + 1, :]] + relay, 8).astype(BF16)
        for z in range(8 * half, min(8 * half + 8, send_ref.shape[0])):
            send_ref[z] = packet


def masked_rows(rows, factors):
    lines = [jnp.concatenate(row, axis=1) * factor.astype(F32) for row, factor in zip(rows, factors)]
    return stacked(lines, 16).astype(BF16)


def products(rows, blocks, count):
    every = lax.dot_general(rows, blocks, (((1,), (1,)), ((), ())), preferred_element_type=F32)
    result = every[0:1, 0:256]
    for k in range(1, count):
        result = result + every[k:k + 1, 256 * k:256 * k + 256]
    return result


def near_inside(tiles, mask_ref, got_ref, near_ref, out_ref):
    across = lax.rem(lax.axis_index("slab"), PLANE)
    tile = lax.axis_index("tile")
    rows = []
    for a in range(-1, 2):
        for b in range(-1, 2):
            up, beside = across + a, tile + b
            inside = (up >= 0) & (up < PLANE) & (beside >= 0) & (beside < tiles)
            packet = got_ref[jnp.clip(up, 0, PLANE - 1) * tiles + jnp.clip(beside, 0, tiles - 1)].astype(F32)
            packet = jnp.where(inside, packet, 0.0)
            rows.append((packet[2:3, :], packet[3:4, :]))
    out_ref[...] = products(masked_rows(rows, [mask_ref[0:1, q:q + 1] for q in range(9)]), near_ref[...], 9)


def finish(planes, mask_ref, rank_ref, part_ref, relay_ref, near_ref, left_ref, out_ref):
    slab = lax.axis_index("slab")
    across = lax.rem(slab, PLANE)
    plane = lax.div(slab, PLANE)
    upward = across == PLANE - 1
    start = jnp.where(upward, plane + 1, plane - 1)
    edge = ((across == 0) | upward) & (start >= 0) & (start < planes)
    packet = jnp.where(edge, relay_ref[jnp.clip(start, 0, planes - 1)].astype(F32), 0.0)
    rows = [(packet[2 + 2 * b:3 + 2 * b, :], packet[3 + 2 * b:4 + 2 * b, :]) for b in range(3)]
    first = jnp.where(upward, 6, 0)
    blocks = near_ref[pl.ds(pl.multiple_of(256 * first, 256), 768), :]
    factors = [jnp.where(upward, mask_ref[0:1, 6 + b:7 + b], mask_ref[0:1, b:b + 1]) for b in range(3)]
    near = products(masked_rows(rows, factors), blocks, 3)
    total = jnp.sum(relay_ref[...].astype(F32), axis=0)
    total = jnp.broadcast_to(total[0:1, :] + total[1:2, :], (8, 128))
    lane = lax.broadcasted_iota(jnp.int32, total.shape, 1)
    at = 16 * lax.rem(plane, 8)
    total = jnp.where((lane >= at) & (lane < at + rank_ref[...]), total, 0.0)
    high = total.astype(BF16).astype(F32)
    halves = jnp.concatenate([high, total - high], axis=0).astype(BF16)
    left = jnp.concatenate([left_ref[...]] * 8, axis=0)
    far = jnp.dot(halves, left, preferred_element_type=F32)
    out_ref[...] = part_ref[...] + near + far[0:1, :] + far[8:9, :]


def vmem():
    return pl.BlockSpec(memory_space=pltpu.VMEM)


def hbm():
    return pl.BlockSpec(memory_space=pltpu.HBM)


def exchange(first, last, axis):
    devices = lax.axis_size(axis)
    up = [(i, i + 1) for i in range(devices - 1)]
    down = [(j, i) for i, j in up]
    return lax.ppermute(last, axis, up), lax.ppermute(first, axis, down)


def swap(far, pair, axis):
    devices = lax.axis_size(axis)
    far = lax.ppermute(far, axis, [(i, i + 1 if i % 2 else i - 1) for i in range(1, devices - 1)])
    return far, lax.ppermute(pair, axis, [(i, i ^ 1) for i in range(devices)])


def local(initial_field, source, material, stiffness_table, mass_table, trace_cells, near_blocks, near_mask, far_left, far_right,
          block_ranks):
    slabs, tiles = lax.axis_size("slab"), lax.axis_size("tile")
    planes = slabs // PLANE
    volume = jax.ShapeDtypeStruct((3, 128, 384), F32)
    face = jax.ShapeDtypeStruct((64, 384), BF16)
    params = pltpu.CompilerParams(vmem_limit_bytes=24 * 1024 * 1024)
    first, last, table = pl.pallas_call(
        y_faces,
        out_shape=(face, face, jax.ShapeDtypeStruct((16, 384), F32)),
        in_specs=[hbm()] * 5,
        out_specs=(vmem(),) * 3,
        scratch_shapes=[
            pltpu.SMEM((8,), F32), pltpu.SMEM((8,), F32), pltpu.VMEM((4, 3, 8, 384), F32), pltpu.VMEM((2, 3, 8, 384), F32),
            pltpu.VMEM((2, 8, 384), jnp.int32), pltpu.SemaphoreType.DMA((10,)),
        ],
        compiler_params=pltpu.CompilerParams(vmem_limit_bytes=56000 * 1024),
    )(stiffness_table, mass_table, initial_field, source, material)
    field = initial_field.reshape(3, 128, 384)
    sources = source.reshape(3, 128, 384)
    cells = material.reshape(128, 384)
    before, after = exchange(first, last, "tile")
    face = jax.ShapeDtypeStruct((128, 384), BF16)
    far, pair = pl.pallas_call(
        z_faces,
        out_shape=(face, face),
        in_specs=[vmem()] * 6,
        out_specs=(vmem(), vmem()),
        compiler_params=params,
    )(table, field, sources, cells, before, after)
    far, pair = swap(far, pair, "slab")
    members = PLANE * tiles
    *state, inner, edge, place, spread = pl.pallas_call(
        relax_inner,
        out_shape=(
            volume, volume, jax.ShapeDtypeStruct((128, 384), F32), jax.ShapeDtypeStruct((12, 8, 384), F32),
            volume, jax.ShapeDtypeStruct((256, 192), BF16),
            jax.ShapeDtypeStruct((256, 128), F32), jax.ShapeDtypeStruct((256, 128), F32),
        ),
        in_specs=[vmem()] * 7,
        out_specs=(vmem(),) * 4 + (hbm(),) + (vmem(),) * 3,
        scratch_shapes=[pltpu.VMEM((192, 384), BF16), pltpu.VMEM((3, 64, 384), F32), pltpu.SemaphoreType.DMA((3,))],
        compiler_params=params,
        cost_estimate=pl.CostEstimate(flops=6_000_000, bytes_accessed=4_000_000, transcendentals=0),
    )(table, field, sources, cells, before, after, trace_cells.reshape(1, 256))
    edges, send = pl.pallas_call(
        functools.partial(relax_edges, planes),
        out_shape=(jax.ShapeDtypeStruct((3, 64, 384), F32), jax.ShapeDtypeStruct((members, 4, 128), BF16)),
        in_specs=[vmem()] * 11,
        out_specs=(vmem(), vmem()),
        scratch_shapes=[pltpu.VMEM((192, 384), BF16)],
        compiler_params=params,
    )(field, *state, edge, place, spread, far, pair, far_right.reshape(-1, 256))
    ids = np.arange(slabs * tiles).reshape(planes, members)
    got = lax.all_to_all(send, BOTH, 0, 0, axis_index_groups=ids.tolist(), tiled=True)
    send = pl.pallas_call(
        functools.partial(middle, tiles),
        out_shape=jax.ShapeDtypeStruct((planes, 8, 128), BF16),
        in_specs=[vmem()],
        out_specs=vmem(),
        compiler_params=params,
    )(got)
    relay = lax.all_to_all(send, BOTH, 0, 0, axis_index_groups=ids.T.tolist(), tiled=True)
    result = pl.pallas_call(
        assemble,
        out_shape=volume,
        in_specs=[hbm(), vmem()],
        out_specs=hbm(),
        input_output_aliases={0: 0},
        scratch_shapes=[pltpu.SemaphoreType.DMA((6,))],
        compiler_params=params,
        cost_estimate=pl.CostEstimate(flops=0, bytes_accessed=600_000, transcendentals=0),
    )(inner, edges)
    mask = near_mask.reshape(1, 9)
    blocks = near_blocks.reshape(-1, 256)
    part = pl.pallas_call(
        functools.partial(near_inside, tiles),
        out_shape=jax.ShapeDtypeStruct((1, 256), F32),
        in_specs=[vmem()] * 3,
        out_specs=vmem(),
        compiler_params=params,
        cost_estimate=pl.CostEstimate(flops=2 * 16 * 2304 * 256, bytes_accessed=2304 * 512, transcendentals=0),
    )(mask, got, blocks)
    boundary = pl.pallas_call(
        functools.partial(finish, planes),
        out_shape=jax.ShapeDtypeStruct((1, 256), F32),
        in_specs=[vmem()] * 6,
        out_specs=vmem(),
        compiler_params=params,
    )(mask, block_ranks.reshape(1, 1), part, relay, blocks, far_left.reshape(16, 256))
    return result.reshape(initial_field.shape), boundary.reshape(1, 1, 256)


def solution(mesh):
    placed = (
        P(None, "slab", "tile", None),
        P(None, "slab", "tile", None),
        P("slab", "tile", None),
        P(),
        P(),
        P("slab", "tile", None),
        P("slab", "tile", None, None, None),
        P("slab", "tile", None),
        P(None, "slab", "tile", None),
        P(None, None, "slab", "tile", None),
        P("slab"),
    )
    return jax.shard_map(
        local,
        mesh=mesh,
        in_specs=placed,
        out_specs=(P(None, "slab", "tile", None), P("slab", "tile", None)),
        check_vma=False,
    )
```

```python
import functools

import jax
import jax.numpy as jnp
import numpy as np
from jax import lax
from jax.experimental import pallas as pl
from jax.experimental.pallas import tpu as pltpu
from jax.sharding import PartitionSpec as P

RELAX = 0.8
KEEP = 1.0 - RELAX
PLANE = 8
F32 = jnp.float32
BF16 = jnp.bfloat16
BOTH = ("slab", "tile")


def table_rows(stiff_ref, mass_ref, width):
    stiffness = stiff_ref[...]
    weight = RELAX / (6.0 * stiffness + mass_ref[...])
    rows = []
    for table in (weight, stiffness * weight):
        rows += [jnp.broadcast_to(table[:, entry:entry + 1], (1, width)) for entry in range(8)]
    return rows


def lookup(material, rows):
    weight = jnp.broadcast_to(rows[0], material.shape)
    coupling = jnp.broadcast_to(rows[8], material.shape)
    for entry in range(1, 8):
        here = material == entry
        weight = jnp.where(here, rows[entry], weight)
        coupling = jnp.where(here, rows[8 + entry], coupling)
    return weight, coupling


def x_sum(value):
    width = value.shape[-1]
    lane = lax.broadcasted_iota(jnp.int32, value.shape, value.ndim - 1)
    before = jnp.where(lane == 0, 0.0, pltpu.roll(value, 1, value.ndim - 1))
    after = jnp.where(lane == width - 1, 0.0, pltpu.roll(value, width - 1, value.ndim - 1))
    return before + after


def row_sum(value, first, last):
    length = value.shape[0]
    row = lax.broadcasted_iota(jnp.int32, value.shape, 0)
    before = jnp.where(row == 0, first, pltpu.roll(value, 1, 0))
    after = jnp.where(row == length - 1, last, pltpu.roll(value, length - 1, 0))
    return before + after


def line_rows(ref, y, *lead):
    lines = [ref[(*lead, slice(16 * z + y, 16 * z + y + 1), slice(None))] for z in range(8)]
    row = lax.broadcasted_iota(jnp.int32, (8, lines[0].shape[1]), 0)
    value = jnp.broadcast_to(lines[0], row.shape)
    for z in range(1, 8):
        value = jnp.where(row == z, lines[z], value)
    return value


def y_faces(field_hbm, source_hbm, material_hbm, first_ref, last_ref, field_ref, source_ref, material_ref, sems):
    pairs = [(field_hbm.at[:, :, y, :], field_ref.at[k]) for k, y in enumerate((0, 15, 1, 14))]
    pairs += [(source_hbm.at[:, :, y, :], source_ref.at[k]) for k, y in enumerate((0, 15))]
    pairs += [(material_hbm.at[:, y, :], material_ref.at[k]) for k, y in enumerate((0, 15))]
    copies = [pltpu.make_async_copy(src, dst, sems.at[k]) for k, (src, dst) in enumerate(pairs)]
    for copy in copies:
        copy.start()
    for copy in copies:
        copy.wait()
    for k, out_ref in enumerate((first_ref, last_ref)):
        values = [field_ref[k, c] for c in range(3)]
        totals = [field_ref[2 + k, c] + row_sum(values[c], 0.0, 0.0) + x_sum(values[c]) for c in range(3)]
        planes = values + [source_ref[k, c] for c in range(3)] + totals + [1.0 + material_ref[k].astype(F32)]
        for pair in range(5):
            both = jnp.concatenate(planes[2 * pair:2 * pair + 2], axis=0)
            out_ref[16 * pair:16 * pair + 16, :] = both.astype(BF16)


def rim_rows(first, last):
    row = lax.broadcasted_iota(jnp.int32, (16, first.shape[1]), 0)
    return jnp.where(row == 0, first, jnp.where(row == 15, last, 0.0))


def z_faces(field_ref, base_ref, coupling_ref, before_ref, after_ref, far_ref, pair_ref):
    even = lax.rem(lax.axis_index("slab"), 2) == 0
    before = bands(before_ref, 2)
    after = bands(after_ref, 2)
    faces = []
    for z in (0, 7):
        here = slice(16 * z, 16 * z + 16)
        coupling = coupling_ref[here, :]
        lines, values, partials = [], [], []
        for c in range(3):
            at = 8 * (c % 2) + z
            lines += [before[c // 2][at:at + 1, :], after[c // 2][at:at + 1, :]]
            values.append(field_ref[c, here, :])
            partials.append(base_ref[c, here, :] + coupling * rim_rows(lines[2 * c], lines[2 * c + 1]))
        faces.append(values + partials + [coupling, stacked(lines, 16)])
    for k, (first, last) in enumerate(zip(*faces)):
        here = slice(16 * k, 16 * k + 16)
        far_ref[here, :] = jnp.where(even, first, last).astype(BF16)
        pair_ref[here, :] = jnp.where(even, last, first).astype(BF16)


def stacked(lines, height):
    row = lax.broadcasted_iota(jnp.int32, (height, lines[0].shape[1]), 0)
    value = jnp.zeros(row.shape, F32)
    for k in range(len(lines)):
        value = jnp.where(row == k, lines[k], value)
    return value


def column_of(row):
    length = row.shape[1]
    down = lax.broadcasted_iota(jnp.int32, (length, length), 0)
    along = lax.broadcasted_iota(jnp.int32, (length, length), 1)
    return jnp.sum(jnp.where(down == along, row, 0.0), axis=1, keepdims=True)


def bands(ref, count):
    return [ref[16 * k:16 * k + 16, :].astype(F32) for k in range(count)]


EDGES = (0, 1, 6, 7)


def no_halo(stiff_ref, mass_ref, field_ref, source_ref, material_ref, cells_ref,
            base_ref, scaled_ref, coupling_ref, edge_ref, chosen_ref, place_ref):
    rows = table_rows(stiff_ref, mass_ref, field_ref.shape[-1])
    for z in range(8):
        here = slice(16 * z, 16 * z + 16)
        weight, coupling = lookup(material_ref[here, :], rows)
        coupling_ref[here, :] = coupling
        for c in range(3):
            value = field_ref[c, here, :]
            total = row_sum(value, 0.0, 0.0) + x_sum(value)
            if z > 0:
                total = total + field_ref[c, 16 * z - 16:16 * z, :]
            if z < 7:
                total = total + field_ref[c, 16 * z + 16:16 * z + 32, :]
            scaled = weight * source_ref[c, here, :]
            scaled_ref[c, here, :] = scaled
            base_ref[c, here, :] = KEEP * value + scaled + coupling * total

    width = field_ref.shape[-1]
    count = cells_ref.shape[1]
    cells = cells_ref[...].astype(F32)
    line = jnp.floor((cells + 0.5) * (1.0 / width))
    place_ref[...] = jnp.broadcast_to(column_of(cells - width * line), (count, 128))
    line_column = column_of(line)
    along = lax.broadcasted_iota(jnp.int32, (count, 192), 1).astype(F32)
    part = jnp.floor(along * (1.0 / 64) + 0.001)
    shift = along - 64.0 * part
    inner = 128.0 * part + shift + 32.0
    outer = 128.0 * part + jnp.where(shift < 32.0, shift, shift + 64.0)
    edge_ref[...] = jnp.where(outer == line_column, 1.0, 0.0).astype(BF16)
    chosen_ref[...] = jnp.where(inner == line_column, 1.0, 0.0).astype(BF16)


def relax_inner(stiff_ref, mass_ref, field_ref, base_ref, scaled_ref, coupling_ref, before_ref, after_ref, chosen_ref, place_ref,
                once_ref, rim_ref, out_ref, spread_ref, plain_ref):
    rows = table_rows(stiff_ref, mass_ref, field_ref.shape[-1])
    lines = []
    for side, (ref, y) in enumerate(((before_ref, 0), (after_ref, 15))):
        halo = bands(ref, 5)
        planes = [halo[k // 2][8 * (k % 2):8 * (k % 2) + 8] for k in range(10)]
        weight, coupling = lookup(planes[9] - 1.0, rows)
        coupling = jnp.where(planes[9] > 0.0, coupling, 0.0)
        rim_ref[6 * side + 3] = coupling
        for c in range(3):
            total = planes[6 + c] + line_rows(field_ref, y, c)
            rim_ref[6 * side + c] = KEEP * planes[c] + weight * planes[3 + c] + coupling * total
        lines.append(planes[:3])
    for z in range(8):
        here = slice(16 * z, 16 * z + 16)
        for c in range(3):
            halo = rim_rows(lines[0][c][z:z + 1], lines[1][c][z:z + 1])
            once_ref[c, here, :] = base_ref[c, here, :] + coupling_ref[here, :] * halo
    for z in range(2, 6):
        here = slice(16 * z, 16 * z + 16)
        for c in range(3):
            value = once_ref[c, here, :]
            total = once_ref[c, 16 * z - 16:16 * z, :] + once_ref[c, 16 * z + 16:16 * z + 32, :] + x_sum(value)
            total = total + row_sum(value, rim_ref[c, z:z + 1, :], rim_ref[6 + c, z:z + 1, :])
            result = KEEP * value + scaled_ref[c, here, :] + coupling_ref[here, :] * total
            out_ref[c, 16 * z - 32:16 * z - 16, :] = result
            at = 64 * c + 16 * z - 32
            plain_ref[at:at + 16, :] = result.astype(BF16)
    picked = jnp.dot(chosen_ref[...], plain_ref[...], preferred_element_type=F32)
    spread_ref[...] = spread_of(picked, place_ref[:, 0:1])


def spread_of(picked, place_column):
    along = lax.broadcasted_iota(jnp.int32, picked.shape, 1).astype(F32)
    single = jnp.where(along == place_column, picked, 0.0).astype(BF16)
    return jnp.dot(single, jnp.ones((picked.shape[1], 128), BF16), preferred_element_type=F32)


def relax_edges(planes, field_ref, once_ref, scaled_ref, coupling_ref, rim_ref, edge_ref, place_ref, spread_ref,
                far_ref, pair_ref, right_ref, out_ref, send_ref, plain_ref):
    even = lax.rem(lax.axis_index("slab"), 2) == 0
    both = list(zip(bands(far_ref, 8), bands(pair_ref, 8)))
    halo = [[jnp.where(even, far, pair) for far, pair in both], [jnp.where(even, pair, far) for far, pair in both]]
    row8 = lax.broadcasted_iota(jnp.int32, (8, field_ref.shape[-1]), 0)
    for c in range(3):
        once = {z: once_ref[c, 16 * z:16 * z + 16, :] for z in (1, 2, 5, 6)}
        once[0] = once_ref[c, 0:16, :] + coupling_ref[0:16, :] * halo[0][c]
        once[7] = once_ref[c, 112:128, :] + coupling_ref[112:128, :] * halo[1][c]
        once[-1] = halo[0][3 + c] + halo[0][6] * field_ref[c, 0:16, :]
        once[8] = halo[1][3 + c] + halo[1][6] * field_ref[c, 112:128, :]
        rims = []
        for side in range(2):
            at = 2 * c + side
            corner = jnp.where(row8 == 0, halo[0][7][at:at + 1], 0.0) + jnp.where(row8 == 7, halo[1][7][at:at + 1], 0.0)
            rims.append(rim_ref[6 * side + c] + rim_ref[6 * side + 3] * corner)
        for order, z in enumerate(EDGES):
            here = slice(16 * z, 16 * z + 16)
            total = once[z - 1] + once[z + 1] + x_sum(once[z])
            total = total + row_sum(once[z], rims[0][z:z + 1], rims[1][z:z + 1])
            result = KEEP * once[z] + scaled_ref[c, here, :] + coupling_ref[here, :] * total
            out_ref[c, 16 * order:16 * order + 16, :] = result
            at = 64 * c + 16 * order
            plain_ref[at:at + 16, :] = result.astype(BF16)

    picked = jnp.dot(edge_ref[...], plain_ref[...], preferred_element_type=F32)
    spread = spread_ref[...] + spread_of(picked, place_ref[:, 0:1])
    far = jnp.dot(right_ref[...], spread.astype(BF16), preferred_element_type=F32)
    ranks = 16
    lane = lax.broadcasted_iota(jnp.int32, (PLANE, 128), 1)
    parts = [jnp.zeros((PLANE, 128), F32) for _ in range(2)]
    for k in range(ranks):
        for z in range(planes):
            group = far[PLANE * (k * planes + z):PLANE * (k * planes + z + 1), :]
            at = z * ranks + k
            parts[at // 128] = jnp.where(lane == at % 128, group, parts[at // 128])
    down = lax.broadcasted_iota(jnp.int32, (128, 128), 0)
    across = lax.broadcasted_iota(jnp.int32, (128, 128), 1)
    traces = []
    for half in range(2):
        piece = jnp.where(down == across, spread[128 * half:128 * half + 128, :], 0.0)
        traces.append(jnp.sum(piece, axis=0, keepdims=True))
    tiles = send_ref.shape[0] // PLANE
    for to in range(PLANE):
        packet = stacked([parts[0][to:to + 1, :], parts[1][to:to + 1, :]] + traces, 4).astype(BF16)
        for tile in range(tiles):
            send_ref[to * tiles + tile] = packet


def assemble(inner_ref, edges_ref, out_hbm, sems):
    copies = []
    for c in range(3):
        for source, target in ((edges_ref.at[c, 0:32], (0, 32)), (inner_ref.at[c], (32, 64)), (edges_ref.at[c, 32:64], (96, 32))):
            copies.append(pltpu.make_async_copy(source, out_hbm.at[c, pl.ds(*target), :], sems.at[len(copies)]))
    for copy in copies:
        copy.start()
    for copy in copies:
        copy.wait()


def middle(tiles, got_ref, send_ref):
    across = lax.rem(lax.axis_index("slab"), PLANE)
    tile = lax.axis_index("tile")
    total = jnp.sum(got_ref[...].astype(F32), axis=0)
    other = jnp.where(across == 0, PLANE - 1, 0)
    relay = []
    for b in range(3):
        wanted = tile + b - 1
        inside = (wanted >= 0) & (wanted < tiles)
        packet = got_ref[other * tiles + jnp.clip(wanted, 0, tiles - 1)].astype(F32)
        packet = jnp.where(inside, packet, 0.0)
        relay += [packet[2:3, :], packet[3:4, :]]
    high = total.astype(BF16).astype(F32)
    low = total - high
    for half in range(2):
        packet = stacked([high[half:half + 1, :], low[half:half + 1, :]] + relay, 8).astype(BF16)
        for z in range(8 * half, min(8 * half + 8, send_ref.shape[0])):
            send_ref[z] = packet


def masked_rows(rows, factors):
    lines = [jnp.concatenate(row, axis=1) * factor.astype(F32) for row, factor in zip(rows, factors)]
    return stacked(lines, 16).astype(BF16)


def products(rows, blocks, count):
    every = lax.dot_general(rows, blocks, (((1,), (1,)), ((), ())), preferred_element_type=F32)
    result = every[0:1, 0:256]
    for k in range(1, count):
        result = result + every[k:k + 1, 256 * k:256 * k + 256]
    return result


def near_inside(tiles, mask_ref, got_ref, near_ref, out_ref):
    across = lax.rem(lax.axis_index("slab"), PLANE)
    tile = lax.axis_index("tile")
    rows = []
    for a in range(-1, 2):
        for b in range(-1, 2):
            up, beside = across + a, tile + b
            inside = (up >= 0) & (up < PLANE) & (beside >= 0) & (beside < tiles)
            packet = got_ref[jnp.clip(up, 0, PLANE - 1) * tiles + jnp.clip(beside, 0, tiles - 1)].astype(F32)
            packet = jnp.where(inside, packet, 0.0)
            rows.append((packet[2:3, :], packet[3:4, :]))
    out_ref[...] = products(masked_rows(rows, [mask_ref[0:1, q:q + 1] for q in range(9)]), near_ref[...], 9)


def finish(planes, mask_ref, rank_ref, part_ref, relay_ref, near_ref, left_ref, out_ref):
    slab = lax.axis_index("slab")
    across = lax.rem(slab, PLANE)
    plane = lax.div(slab, PLANE)
    upward = across == PLANE - 1
    start = jnp.where(upward, plane + 1, plane - 1)
    edge = ((across == 0) | upward) & (start >= 0) & (start < planes)
    packet = jnp.where(edge, relay_ref[jnp.clip(start, 0, planes - 1)].astype(F32), 0.0)
    rows = [(packet[2 + 2 * b:3 + 2 * b, :], packet[3 + 2 * b:4 + 2 * b, :]) for b in range(3)]
    first = jnp.where(upward, 6, 0)
    blocks = near_ref[pl.ds(pl.multiple_of(256 * first, 256), 768), :]
    factors = [jnp.where(upward, mask_ref[0:1, 6 + b:7 + b], mask_ref[0:1, b:b + 1]) for b in range(3)]
    near = products(masked_rows(rows, factors), blocks, 3)
    total = jnp.sum(relay_ref[...].astype(F32), axis=0)
    total = jnp.broadcast_to(total[0:1, :] + total[1:2, :], (8, 128))
    lane = lax.broadcasted_iota(jnp.int32, total.shape, 1)
    at = 16 * lax.rem(plane, 8)
    total = jnp.where((lane >= at) & (lane < at + rank_ref[...]), total, 0.0)
    high = total.astype(BF16).astype(F32)
    halves = jnp.concatenate([high, total - high], axis=0).astype(BF16)
    left = jnp.concatenate([left_ref[...]] * 8, axis=0)
    far = jnp.dot(halves, left, preferred_element_type=F32)
    out_ref[...] = part_ref[...] + near + far[0:1, :] + far[8:9, :]


def vmem():
    return pl.BlockSpec(memory_space=pltpu.VMEM)


def hbm():
    return pl.BlockSpec(memory_space=pltpu.HBM)


def exchange(first, last, axis):
    devices = lax.axis_size(axis)
    up = [(i, i + 1) for i in range(devices - 1)]
    down = [(j, i) for i, j in up]
    return lax.ppermute(last, axis, up), lax.ppermute(first, axis, down)


def swap(far, pair, axis):
    devices = lax.axis_size(axis)
    far = lax.ppermute(far, axis, [(i, i + 1 if i % 2 else i - 1) for i in range(1, devices - 1)])
    return far, lax.ppermute(pair, axis, [(i, i ^ 1) for i in range(devices)])


def local(initial_field, source, material, stiffness_table, mass_table, trace_cells, near_blocks, near_mask, far_left, far_right,
          block_ranks):
    slabs, tiles = lax.axis_size("slab"), lax.axis_size("tile")
    planes = slabs // PLANE
    volume = jax.ShapeDtypeStruct((3, 128, 384), F32)
    face = jax.ShapeDtypeStruct((80, 384), BF16)
    params = pltpu.CompilerParams(vmem_limit_bytes=24 * 1024 * 1024)
    first, last = pl.pallas_call(
        y_faces,
        out_shape=(face, face),
        in_specs=[hbm()] * 3,
        out_specs=(vmem(), vmem()),
        scratch_shapes=[
            pltpu.VMEM((4, 3, 8, 384), F32), pltpu.VMEM((2, 3, 8, 384), F32), pltpu.VMEM((2, 8, 384), jnp.int32),
            pltpu.SemaphoreType.DMA((8,)),
        ],
        compiler_params=pltpu.CompilerParams(vmem_limit_bytes=55050 * 1024),
    )(initial_field, source, material)
    tables = (stiffness_table.reshape(1, 8), mass_table.reshape(1, 8))
    field = initial_field.reshape(3, 128, 384)
    sources = source.reshape(3, 128, 384)
    cells = material.reshape(128, 384)
    before, after = exchange(first, last, "tile")
    index = jax.ShapeDtypeStruct((256, 192), BF16)
    column = jax.ShapeDtypeStruct((256, 128), F32)
    base, scaled, coupling, edge, chosen, place = pl.pallas_call(
        no_halo,
        out_shape=(volume, volume, jax.ShapeDtypeStruct((128, 384), F32), index, index, column),
        in_specs=[vmem()] * 6,
        out_specs=(vmem(),) * 6,
        compiler_params=params,
        cost_estimate=pl.CostEstimate(flops=6_000_000, bytes_accessed=3_000_000, transcendentals=0),
    )(*tables, field, sources, cells, trace_cells.reshape(1, 256))
    face = jax.ShapeDtypeStruct((128, 384), BF16)
    far, pair = pl.pallas_call(
        z_faces,
        out_shape=(face, face),
        in_specs=[vmem()] * 5,
        out_specs=(vmem(), vmem()),
        compiler_params=params,
    )(field, base, coupling, before, after)
    far, pair = swap(far, pair, "slab")
    members = PLANE * tiles
    once, rim, inner, spread = pl.pallas_call(
        relax_inner,
        out_shape=(volume, jax.ShapeDtypeStruct((12, 8, 384), F32), jax.ShapeDtypeStruct((3, 64, 384), F32), column),
        in_specs=[vmem()] * 10,
        out_specs=(vmem(),) * 4,
        scratch_shapes=[pltpu.VMEM((192, 384), BF16)],
        compiler_params=params,
        cost_estimate=pl.CostEstimate(flops=4_000_000, bytes_accessed=3_000_000, transcendentals=0),
    )(*tables, field, base, scaled, coupling, before, after, chosen, place)
    edges, send = pl.pallas_call(
        functools.partial(relax_edges, planes),
        out_shape=(jax.ShapeDtypeStruct((3, 64, 384), F32), jax.ShapeDtypeStruct((members, 4, 128), BF16)),
        in_specs=[vmem()] * 11,
        out_specs=(vmem(), vmem()),
        scratch_shapes=[pltpu.VMEM((192, 384), BF16)],
        compiler_params=params,
    )(field, once, scaled, coupling, rim, edge, place, spread, far, pair, far_right.reshape(-1, 256))
    ids = np.arange(slabs * tiles).reshape(planes, members)
    got = lax.all_to_all(send, BOTH, 0, 0, axis_index_groups=ids.tolist(), tiled=True)
    send = pl.pallas_call(
        functools.partial(middle, tiles),
        out_shape=jax.ShapeDtypeStruct((planes, 8, 128), BF16),
        in_specs=[vmem()],
        out_specs=vmem(),
        compiler_params=params,
    )(got)
    relay = lax.all_to_all(send, BOTH, 0, 0, axis_index_groups=ids.T.tolist(), tiled=True)
    result = pl.pallas_call(
        assemble,
        out_shape=volume,
        in_specs=[vmem(), vmem()],
        out_specs=hbm(),
        scratch_shapes=[pltpu.SemaphoreType.DMA((9,))],
        compiler_params=params,
        cost_estimate=pl.CostEstimate(flops=0, bytes_accessed=600_000, transcendentals=0),
    )(inner, edges)
    mask = near_mask.reshape(1, 9)
    blocks = near_blocks.reshape(-1, 256)
    part = pl.pallas_call(
        functools.partial(near_inside, tiles),
        out_shape=jax.ShapeDtypeStruct((1, 256), F32),
        in_specs=[vmem()] * 3,
        out_specs=vmem(),
        compiler_params=params,
        cost_estimate=pl.CostEstimate(flops=2 * 16 * 2304 * 256, bytes_accessed=2304 * 512, transcendentals=0),
    )(mask, got, blocks)
    boundary = pl.pallas_call(
        functools.partial(finish, planes),
        out_shape=jax.ShapeDtypeStruct((1, 256), F32),
        in_specs=[vmem()] * 6,
        out_specs=vmem(),
        compiler_params=params,
    )(mask, block_ranks.reshape(1, 1), part, relay, blocks, far_left.reshape(16, 256))
    return result.reshape(initial_field.shape), boundary.reshape(1, 1, 256)


def solution(mesh):
    placed = (
        P(None, "slab", "tile", None),
        P(None, "slab", "tile", None),
        P("slab", "tile", None),
        P(),
        P(),
        P("slab", "tile", None),
        P("slab", "tile", None, None, None),
        P("slab", "tile", None),
        P(None, "slab", "tile", None),
        P(None, None, "slab", "tile", None),
        P("slab"),
    )
    return jax.shard_map(
        local,
        mesh=mesh,
        in_specs=placed,
        out_specs=(P(None, "slab", "tile", None), P("slab", "tile", None)),
        check_vma=False,
    )
```

```python
import functools

import jax
import jax.numpy as jnp
import numpy as np
from jax import lax
from jax.experimental import pallas as pl
from jax.experimental.pallas import tpu as pltpu
from jax.sharding import PartitionSpec as P

RELAX = 0.8
KEEP = 1.0 - RELAX
PLANE = 8
F32 = jnp.float32
BF16 = jnp.bfloat16
BOTH = ("slab", "tile")


def table_rows(stiff_ref, mass_ref, width):
    stiffness = stiff_ref[...]
    weight = RELAX / (6.0 * stiffness + mass_ref[...])
    rows = []
    for table in (weight, stiffness * weight):
        rows += [jnp.broadcast_to(table[:, entry:entry + 1], (1, width)) for entry in range(8)]
    return rows


def lookup(material, rows):
    weight = jnp.broadcast_to(rows[0], material.shape)
    coupling = jnp.broadcast_to(rows[8], material.shape)
    for entry in range(1, 8):
        here = material == entry
        weight = jnp.where(here, rows[entry], weight)
        coupling = jnp.where(here, rows[8 + entry], coupling)
    return weight, coupling


def x_sum(value):
    width = value.shape[-1]
    lane = lax.broadcasted_iota(jnp.int32, value.shape, value.ndim - 1)
    before = jnp.where(lane == 0, 0.0, pltpu.roll(value, 1, value.ndim - 1))
    after = jnp.where(lane == width - 1, 0.0, pltpu.roll(value, width - 1, value.ndim - 1))
    return before + after


def row_sum(value, first, last):
    length = value.shape[0]
    row = lax.broadcasted_iota(jnp.int32, value.shape, 0)
    before = jnp.where(row == 0, first, pltpu.roll(value, 1, 0))
    after = jnp.where(row == length - 1, last, pltpu.roll(value, length - 1, 0))
    return before + after


def line_rows(ref, y, *lead):
    lines = [ref[(*lead, slice(16 * z + y, 16 * z + y + 1), slice(None))] for z in range(8)]
    row = lax.broadcasted_iota(jnp.int32, (8, lines[0].shape[1]), 0)
    value = jnp.broadcast_to(lines[0], row.shape)
    for z in range(1, 8):
        value = jnp.where(row == z, lines[z], value)
    return value


def y_faces(field_hbm, source_hbm, material_hbm, first_ref, last_ref, field_ref, source_ref, material_ref, sems):
    pairs = [(field_hbm.at[:, :, y, :], field_ref.at[k]) for k, y in enumerate((0, 15, 1, 14))]
    pairs += [(source_hbm.at[:, :, y, :], source_ref.at[k]) for k, y in enumerate((0, 15))]
    pairs += [(material_hbm.at[:, y, :], material_ref.at[k]) for k, y in enumerate((0, 15))]
    copies = [pltpu.make_async_copy(src, dst, sems.at[k]) for k, (src, dst) in enumerate(pairs)]
    for copy in copies:
        copy.start()
    for copy in copies:
        copy.wait()
    for k, out_ref in enumerate((first_ref, last_ref)):
        values = [field_ref[k, c] for c in range(3)]
        totals = [field_ref[2 + k, c] + row_sum(values[c], 0.0, 0.0) + x_sum(values[c]) for c in range(3)]
        planes = values + [source_ref[k, c] for c in range(3)] + totals + [1.0 + material_ref[k].astype(F32)]
        for pair in range(5):
            both = jnp.concatenate(planes[2 * pair:2 * pair + 2], axis=0)
            out_ref[16 * pair:16 * pair + 16, :] = both.astype(BF16)


def rim_rows(first, last):
    row = lax.broadcasted_iota(jnp.int32, (16, first.shape[1]), 0)
    return jnp.where(row == 0, first, jnp.where(row == 15, last, 0.0))


def z_faces(field_ref, base_ref, coupling_ref, before_ref, after_ref, far_ref, pair_ref):
    even = lax.rem(lax.axis_index("slab"), 2) == 0
    before = bands(before_ref, 2)
    after = bands(after_ref, 2)
    faces = []
    for z in (0, 7):
        here = slice(16 * z, 16 * z + 16)
        coupling = coupling_ref[here, :]
        lines, values, partials = [], [], []
        for c in range(3):
            at = 8 * (c % 2) + z
            lines += [before[c // 2][at:at + 1, :], after[c // 2][at:at + 1, :]]
            values.append(field_ref[c, here, :])
            partials.append(base_ref[c, here, :] + coupling * rim_rows(lines[2 * c], lines[2 * c + 1]))
        faces.append(values + partials + [coupling, stacked(lines, 16)])
    for k, (first, last) in enumerate(zip(*faces)):
        here = slice(16 * k, 16 * k + 16)
        far_ref[here, :] = jnp.where(even, first, last).astype(BF16)
        pair_ref[here, :] = jnp.where(even, last, first).astype(BF16)


def stacked(lines, height):
    row = lax.broadcasted_iota(jnp.int32, (height, lines[0].shape[1]), 0)
    value = jnp.zeros(row.shape, F32)
    for k in range(len(lines)):
        value = jnp.where(row == k, lines[k], value)
    return value


def column_of(row):
    length = row.shape[1]
    down = lax.broadcasted_iota(jnp.int32, (length, length), 0)
    along = lax.broadcasted_iota(jnp.int32, (length, length), 1)
    return jnp.sum(jnp.where(down == along, row, 0.0), axis=1, keepdims=True)


def bands(ref, count):
    return [ref[16 * k:16 * k + 16, :].astype(F32) for k in range(count)]


EDGES = (0, 1, 6, 7)


def no_halo(stiff_ref, mass_ref, field_ref, source_ref, material_ref, cells_ref,
            base_ref, scaled_ref, coupling_ref, edge_ref, chosen_ref, place_ref):
    rows = table_rows(stiff_ref, mass_ref, field_ref.shape[-1])
    for z in range(8):
        here = slice(16 * z, 16 * z + 16)
        weight, coupling = lookup(material_ref[here, :], rows)
        coupling_ref[here, :] = coupling
        for c in range(3):
            value = field_ref[c, here, :]
            total = row_sum(value, 0.0, 0.0) + x_sum(value)
            if z > 0:
                total = total + field_ref[c, 16 * z - 16:16 * z, :]
            if z < 7:
                total = total + field_ref[c, 16 * z + 16:16 * z + 32, :]
            scaled = weight * source_ref[c, here, :]
            scaled_ref[c, here, :] = scaled
            base_ref[c, here, :] = KEEP * value + scaled + coupling * total

    width = field_ref.shape[-1]
    count = cells_ref.shape[1]
    cells = cells_ref[...].astype(F32)
    line = jnp.floor((cells + 0.5) * (1.0 / width))
    place_ref[...] = jnp.broadcast_to(column_of(cells - width * line), (count, 128))
    line_column = column_of(line)
    along = lax.broadcasted_iota(jnp.int32, (count, 192), 1).astype(F32)
    part = jnp.floor(along * (1.0 / 64) + 0.001)
    shift = along - 64.0 * part
    inner = 128.0 * part + shift + 32.0
    outer = 128.0 * part + jnp.where(shift < 32.0, shift, shift + 64.0)
    edge_ref[...] = jnp.where(outer == line_column, 1.0, 0.0).astype(BF16)
    chosen_ref[...] = jnp.where(inner == line_column, 1.0, 0.0).astype(BF16)


def relax_inner(stiff_ref, mass_ref, field_ref, base_ref, scaled_ref, coupling_ref, before_ref, after_ref, chosen_ref, place_ref,
                once_ref, rim_ref, out_ref, spread_ref, plain_ref):
    rows = table_rows(stiff_ref, mass_ref, field_ref.shape[-1])
    lines = []
    for side, (ref, y) in enumerate(((before_ref, 0), (after_ref, 15))):
        halo = bands(ref, 5)
        planes = [halo[k // 2][8 * (k % 2):8 * (k % 2) + 8] for k in range(10)]
        weight, coupling = lookup(planes[9] - 1.0, rows)
        coupling = jnp.where(planes[9] > 0.0, coupling, 0.0)
        rim_ref[6 * side + 3] = coupling
        for c in range(3):
            total = planes[6 + c] + line_rows(field_ref, y, c)
            rim_ref[6 * side + c] = KEEP * planes[c] + weight * planes[3 + c] + coupling * total
        lines.append(planes[:3])
    for z in range(8):
        here = slice(16 * z, 16 * z + 16)
        for c in range(3):
            halo = rim_rows(lines[0][c][z:z + 1], lines[1][c][z:z + 1])
            once_ref[c, here, :] = base_ref[c, here, :] + coupling_ref[here, :] * halo
    for z in range(2, 6):
        here = slice(16 * z, 16 * z + 16)
        for c in range(3):
            value = once_ref[c, here, :]
            total = once_ref[c, 16 * z - 16:16 * z, :] + once_ref[c, 16 * z + 16:16 * z + 32, :] + x_sum(value)
            total = total + row_sum(value, rim_ref[c, z:z + 1, :], rim_ref[6 + c, z:z + 1, :])
            result = KEEP * value + scaled_ref[c, here, :] + coupling_ref[here, :] * total
            out_ref[c, 16 * z - 32:16 * z - 16, :] = result
            at = 64 * c + 16 * z - 32
            plain_ref[at:at + 16, :] = result.astype(BF16)
    picked = jnp.dot(chosen_ref[...], plain_ref[...], preferred_element_type=F32)
    spread_ref[...] = spread_of(picked, place_ref[:, 0:1])


def spread_of(picked, place_column):
    along = lax.broadcasted_iota(jnp.int32, picked.shape, 1).astype(F32)
    single = jnp.where(along == place_column, picked, 0.0).astype(BF16)
    return jnp.dot(single, jnp.ones((picked.shape[1], 128), BF16), preferred_element_type=F32)


def relax_edges(planes, field_ref, once_ref, scaled_ref, coupling_ref, rim_ref, edge_ref, place_ref, spread_ref,
                far_ref, pair_ref, right_ref, out_ref, send_ref, plain_ref):
    even = lax.rem(lax.axis_index("slab"), 2) == 0
    both = list(zip(bands(far_ref, 8), bands(pair_ref, 8)))
    halo = [[jnp.where(even, far, pair) for far, pair in both], [jnp.where(even, pair, far) for far, pair in both]]
    row8 = lax.broadcasted_iota(jnp.int32, (8, field_ref.shape[-1]), 0)
    for c in range(3):
        once = {z: once_ref[c, 16 * z:16 * z + 16, :] for z in (1, 2, 5, 6)}
        once[0] = once_ref[c, 0:16, :] + coupling_ref[0:16, :] * halo[0][c]
        once[7] = once_ref[c, 112:128, :] + coupling_ref[112:128, :] * halo[1][c]
        once[-1] = halo[0][3 + c] + halo[0][6] * field_ref[c, 0:16, :]
        once[8] = halo[1][3 + c] + halo[1][6] * field_ref[c, 112:128, :]
        rims = []
        for side in range(2):
            at = 2 * c + side
            corner = jnp.where(row8 == 0, halo[0][7][at:at + 1], 0.0) + jnp.where(row8 == 7, halo[1][7][at:at + 1], 0.0)
            rims.append(rim_ref[6 * side + c] + rim_ref[6 * side + 3] * corner)
        for order, z in enumerate(EDGES):
            here = slice(16 * z, 16 * z + 16)
            total = once[z - 1] + once[z + 1] + x_sum(once[z])
            total = total + row_sum(once[z], rims[0][z:z + 1], rims[1][z:z + 1])
            result = KEEP * once[z] + scaled_ref[c, here, :] + coupling_ref[here, :] * total
            out_ref[c, 16 * order:16 * order + 16, :] = result
            at = 64 * c + 16 * order
            plain_ref[at:at + 16, :] = result.astype(BF16)

    picked = jnp.dot(edge_ref[...], plain_ref[...], preferred_element_type=F32)
    spread = spread_ref[...] + spread_of(picked, place_ref[:, 0:1])
    far = jnp.dot(right_ref[...], spread.astype(BF16), preferred_element_type=F32)
    ranks = 16
    lane = lax.broadcasted_iota(jnp.int32, (PLANE, 128), 1)
    parts = [jnp.zeros((PLANE, 128), F32) for _ in range(2)]
    for k in range(ranks):
        for z in range(planes):
            group = far[PLANE * (k * planes + z):PLANE * (k * planes + z + 1), :]
            at = z * ranks + k
            parts[at // 128] = jnp.where(lane == at % 128, group, parts[at // 128])
    down = lax.broadcasted_iota(jnp.int32, (128, 128), 0)
    across = lax.broadcasted_iota(jnp.int32, (128, 128), 1)
    traces = []
    for half in range(2):
        piece = jnp.where(down == across, spread[128 * half:128 * half + 128, :], 0.0)
        traces.append(jnp.sum(piece, axis=0, keepdims=True))
    tiles = send_ref.shape[0] // PLANE
    for to in range(PLANE):
        packet = stacked([parts[0][to:to + 1, :], parts[1][to:to + 1, :]] + traces, 4).astype(BF16)
        for tile in range(tiles):
            send_ref[to * tiles + tile] = packet


def assemble(inner_ref, edges_ref, out_hbm, sems):
    copies = []
    for c in range(3):
        for source, target in ((edges_ref.at[c, 0:32], (0, 32)), (inner_ref.at[c], (32, 64)), (edges_ref.at[c, 32:64], (96, 32))):
            copies.append(pltpu.make_async_copy(source, out_hbm.at[c, pl.ds(*target), :], sems.at[len(copies)]))
    for copy in copies:
        copy.start()
    for copy in copies:
        copy.wait()


def seat(z, planes):
    return (z + planes - planes // 2) % planes


def middle(tiles, got_ref, send_ref):
    across = lax.rem(lax.axis_index("slab"), PLANE)
    tile = lax.axis_index("tile")
    total = jnp.sum(got_ref[...].astype(F32), axis=0)
    other = jnp.where(across == 0, PLANE - 1, 0)
    relay = []
    for b in range(3):
        wanted = tile + b - 1
        inside = (wanted >= 0) & (wanted < tiles)
        packet = got_ref[other * tiles + jnp.clip(wanted, 0, tiles - 1)].astype(F32)
        packet = jnp.where(inside, packet, 0.0)
        relay += [packet[2:3, :], packet[3:4, :]]
    high = total.astype(BF16).astype(F32)
    low = total - high
    for half in range(2):
        packet = stacked([high[half:half + 1, :], low[half:half + 1, :]] + relay, 8).astype(BF16)
        for z in range(8 * half, min(8 * half + 8, send_ref.shape[0])):
            send_ref[seat(z, send_ref.shape[0])] = packet


def masked_rows(rows, factors):
    lines = [jnp.concatenate(row, axis=1) * factor.astype(F32) for row, factor in zip(rows, factors)]
    return stacked(lines, 16).astype(BF16)


def products(rows, blocks, count):
    every = lax.dot_general(rows, blocks, (((1,), (1,)), ((), ())), preferred_element_type=F32)
    result = every[0:1, 0:256]
    for k in range(1, count):
        result = result + every[k:k + 1, 256 * k:256 * k + 256]
    return result


def near_inside(tiles, mask_ref, got_ref, near_ref, out_ref):
    across = lax.rem(lax.axis_index("slab"), PLANE)
    tile = lax.axis_index("tile")
    rows = []
    for a in range(-1, 2):
        for b in range(-1, 2):
            up, beside = across + a, tile + b
            inside = (up >= 0) & (up < PLANE) & (beside >= 0) & (beside < tiles)
            packet = got_ref[jnp.clip(up, 0, PLANE - 1) * tiles + jnp.clip(beside, 0, tiles - 1)].astype(F32)
            packet = jnp.where(inside, packet, 0.0)
            rows.append((packet[2:3, :], packet[3:4, :]))
    out_ref[...] = products(masked_rows(rows, [mask_ref[0:1, q:q + 1] for q in range(9)]), near_ref[...], 9)


def finish(planes, mask_ref, rank_ref, part_ref, relay_ref, near_ref, left_ref, out_ref):
    slab = lax.axis_index("slab")
    across = lax.rem(slab, PLANE)
    plane = lax.div(slab, PLANE)
    upward = across == PLANE - 1
    start = jnp.where(upward, plane + 1, plane - 1)
    edge = ((across == 0) | upward) & (start >= 0) & (start < planes)
    packet = jnp.where(edge, relay_ref[lax.rem(jnp.clip(start, 0, planes - 1) + planes - planes // 2, planes)].astype(F32), 0.0)
    rows = [(packet[2 + 2 * b:3 + 2 * b, :], packet[3 + 2 * b:4 + 2 * b, :]) for b in range(3)]
    first = jnp.where(upward, 6, 0)
    blocks = near_ref[pl.ds(pl.multiple_of(256 * first, 256), 768), :]
    factors = [jnp.where(upward, mask_ref[0:1, 6 + b:7 + b], mask_ref[0:1, b:b + 1]) for b in range(3)]
    near = products(masked_rows(rows, factors), blocks, 3)
    total = jnp.sum(relay_ref[...].astype(F32), axis=0)
    total = jnp.broadcast_to(total[0:1, :] + total[1:2, :], (8, 128))
    lane = lax.broadcasted_iota(jnp.int32, total.shape, 1)
    at = 16 * lax.rem(plane, 8)
    total = jnp.where((lane >= at) & (lane < at + rank_ref[...]), total, 0.0)
    high = total.astype(BF16).astype(F32)
    halves = jnp.concatenate([high, total - high], axis=0).astype(BF16)
    left = jnp.concatenate([left_ref[...]] * 8, axis=0)
    far = jnp.dot(halves, left, preferred_element_type=F32)
    out_ref[...] = part_ref[...] + near + far[0:1, :] + far[8:9, :]


def vmem():
    return pl.BlockSpec(memory_space=pltpu.VMEM)


def hbm():
    return pl.BlockSpec(memory_space=pltpu.HBM)


def exchange(first, last, axis):
    devices = lax.axis_size(axis)
    up = [(i, i + 1) for i in range(devices - 1)]
    down = [(j, i) for i, j in up]
    return lax.ppermute(last, axis, up), lax.ppermute(first, axis, down)


def swap(far, pair, axis):
    devices = lax.axis_size(axis)
    far = lax.ppermute(far, axis, [(i, i + 1 if i % 2 else i - 1) for i in range(1, devices - 1)])
    return far, lax.ppermute(pair, axis, [(i, i ^ 1) for i in range(devices)])


def local(initial_field, source, material, stiffness_table, mass_table, trace_cells, near_blocks, near_mask, far_left, far_right,
          block_ranks):
    slabs, tiles = lax.axis_size("slab"), lax.axis_size("tile")
    planes = slabs // PLANE
    volume = jax.ShapeDtypeStruct((3, 128, 384), F32)
    face = jax.ShapeDtypeStruct((80, 384), BF16)
    params = pltpu.CompilerParams(vmem_limit_bytes=24 * 1024 * 1024)
    first, last = pl.pallas_call(
        y_faces,
        out_shape=(face, face),
        in_specs=[hbm()] * 3,
        out_specs=(vmem(), vmem()),
        scratch_shapes=[
            pltpu.VMEM((4, 3, 8, 384), F32), pltpu.VMEM((2, 3, 8, 384), F32), pltpu.VMEM((2, 8, 384), jnp.int32),
            pltpu.SemaphoreType.DMA((8,)),
        ],
        compiler_params=pltpu.CompilerParams(vmem_limit_bytes=55050 * 1024),
    )(initial_field, source, material)
    tables = (stiffness_table.reshape(1, 8), mass_table.reshape(1, 8))
    field = initial_field.reshape(3, 128, 384)
    sources = source.reshape(3, 128, 384)
    cells = material.reshape(128, 384)
    before, after = exchange(first, last, "tile")
    index = jax.ShapeDtypeStruct((256, 192), BF16)
    column = jax.ShapeDtypeStruct((256, 128), F32)
    base, scaled, coupling, edge, chosen, place = pl.pallas_call(
        no_halo,
        out_shape=(volume, volume, jax.ShapeDtypeStruct((128, 384), F32), index, index, column),
        in_specs=[vmem()] * 6,
        out_specs=(vmem(),) * 6,
        compiler_params=params,
        cost_estimate=pl.CostEstimate(flops=6_000_000, bytes_accessed=3_000_000, transcendentals=0),
    )(*tables, field, sources, cells, trace_cells.reshape(1, 256))
    face = jax.ShapeDtypeStruct((128, 384), BF16)
    far, pair = pl.pallas_call(
        z_faces,
        out_shape=(face, face),
        in_specs=[vmem()] * 5,
        out_specs=(vmem(), vmem()),
        compiler_params=params,
    )(field, base, coupling, before, after)
    far, pair = swap(far, pair, "slab")
    members = PLANE * tiles
    once, rim, inner, spread = pl.pallas_call(
        relax_inner,
        out_shape=(volume, jax.ShapeDtypeStruct((12, 8, 384), F32), jax.ShapeDtypeStruct((3, 64, 384), F32), column),
        in_specs=[vmem()] * 10,
        out_specs=(vmem(),) * 4,
        scratch_shapes=[pltpu.VMEM((192, 384), BF16)],
        compiler_params=params,
        cost_estimate=pl.CostEstimate(flops=4_000_000, bytes_accessed=3_000_000, transcendentals=0),
    )(*tables, field, base, scaled, coupling, before, after, chosen, place)
    edges, send = pl.pallas_call(
        functools.partial(relax_edges, planes),
        out_shape=(jax.ShapeDtypeStruct((3, 64, 384), F32), jax.ShapeDtypeStruct((members, 4, 128), BF16)),
        in_specs=[vmem()] * 11,
        out_specs=(vmem(), vmem()),
        scratch_shapes=[pltpu.VMEM((192, 384), BF16)],
        compiler_params=params,
    )(field, once, scaled, coupling, rim, edge, place, spread, far, pair, far_right.reshape(-1, 256))
    ids = np.arange(slabs * tiles).reshape(planes, members)
    got = lax.all_to_all(send, BOTH, 0, 0, axis_index_groups=ids.tolist(), tiled=True)
    send = pl.pallas_call(
        functools.partial(middle, tiles),
        out_shape=jax.ShapeDtypeStruct((planes, 8, 128), BF16),
        in_specs=[vmem()],
        out_specs=vmem(),
        compiler_params=params,
    )(got)
    relay = lax.all_to_all(send, BOTH, 0, 0, axis_index_groups=np.roll(ids, -(planes // 2), axis=0).T.tolist(), tiled=True)
    result = pl.pallas_call(
        assemble,
        out_shape=volume,
        in_specs=[vmem(), vmem()],
        out_specs=hbm(),
        scratch_shapes=[pltpu.SemaphoreType.DMA((9,))],
        compiler_params=params,
        cost_estimate=pl.CostEstimate(flops=0, bytes_accessed=600_000, transcendentals=0),
    )(inner, edges)
    mask = near_mask.reshape(1, 9)
    blocks = near_blocks.reshape(-1, 256)
    part = pl.pallas_call(
        functools.partial(near_inside, tiles),
        out_shape=jax.ShapeDtypeStruct((1, 256), F32),
        in_specs=[vmem()] * 3,
        out_specs=vmem(),
        compiler_params=params,
        cost_estimate=pl.CostEstimate(flops=2 * 16 * 2304 * 256, bytes_accessed=2304 * 512, transcendentals=0),
    )(mask, got, blocks)
    boundary = pl.pallas_call(
        functools.partial(finish, planes),
        out_shape=jax.ShapeDtypeStruct((1, 256), F32),
        in_specs=[vmem()] * 6,
        out_specs=vmem(),
        compiler_params=params,
    )(mask, block_ranks.reshape(1, 1), part, relay, blocks, far_left.reshape(16, 256))
    return result.reshape(initial_field.shape), boundary.reshape(1, 1, 256)


def solution(mesh):
    placed = (
        P(None, "slab", "tile", None),
        P(None, "slab", "tile", None),
        P("slab", "tile", None),
        P(),
        P(),
        P("slab", "tile", None),
        P("slab", "tile", None, None, None),
        P("slab", "tile", None),
        P(None, "slab", "tile", None),
        P(None, None, "slab", "tile", None),
        P("slab"),
    )
    return jax.shard_map(
        local,
        mesh=mesh,
        in_specs=placed,
        out_specs=(P(None, "slab", "tile", None), P("slab", "tile", None)),
        check_vma=False,
    )
```

```python
import functools

import jax
import jax.numpy as jnp
import numpy as np
from jax import lax
from jax.experimental import pallas as pl
from jax.experimental.pallas import tpu as pltpu
from jax.sharding import PartitionSpec as P

RELAX = 0.8
KEEP = 1.0 - RELAX
PLANE = 8
F32 = jnp.float32
BF16 = jnp.bfloat16
BOTH = ("slab", "tile")


def seat(member, count):
    return (member + count - count // 2) % count


def seated(member, count):
    return lax.rem(jnp.clip(member, 0, count - 1) + count - count // 2, count)


def table_rows(stiff_ref, mass_ref, width):
    stiffness = stiff_ref[...]
    weight = RELAX / (6.0 * stiffness + mass_ref[...])
    rows = []
    for table in (weight, stiffness * weight):
        rows += [jnp.broadcast_to(table[:, entry:entry + 1], (1, width)) for entry in range(8)]
    return rows


def lookup(material, rows):
    weight = jnp.broadcast_to(rows[0], material.shape)
    coupling = jnp.broadcast_to(rows[8], material.shape)
    for entry in range(1, 8):
        here = material == entry
        weight = jnp.where(here, rows[entry], weight)
        coupling = jnp.where(here, rows[8 + entry], coupling)
    return weight, coupling


def x_sum(value):
    width = value.shape[-1]
    lane = lax.broadcasted_iota(jnp.int32, value.shape, value.ndim - 1)
    before = jnp.where(lane == 0, 0.0, pltpu.roll(value, 1, value.ndim - 1))
    after = jnp.where(lane == width - 1, 0.0, pltpu.roll(value, width - 1, value.ndim - 1))
    return before + after


def row_sum(value, first, last):
    length = value.shape[0]
    row = lax.broadcasted_iota(jnp.int32, value.shape, 0)
    before = jnp.where(row == 0, first, pltpu.roll(value, 1, 0))
    after = jnp.where(row == length - 1, last, pltpu.roll(value, length - 1, 0))
    return before + after


def line_rows(ref, y, *lead):
    lines = [ref[(*lead, slice(16 * z + y, 16 * z + y + 1), slice(None))] for z in range(8)]
    row = lax.broadcasted_iota(jnp.int32, (8, lines[0].shape[1]), 0)
    value = jnp.broadcast_to(lines[0], row.shape)
    for z in range(1, 8):
        value = jnp.where(row == z, lines[z], value)
    return value


def y_faces(field_hbm, source_hbm, material_hbm, first_ref, last_ref, field_ref, source_ref, material_ref, sems):
    pairs = [(field_hbm.at[:, :, y, :], field_ref.at[k]) for k, y in enumerate((0, 15, 1, 14))]
    pairs += [(source_hbm.at[:, :, y, :], source_ref.at[k]) for k, y in enumerate((0, 15))]
    pairs += [(material_hbm.at[:, y, :], material_ref.at[k]) for k, y in enumerate((0, 15))]
    copies = [pltpu.make_async_copy(src, dst, sems.at[k]) for k, (src, dst) in enumerate(pairs)]
    for copy in copies:
        copy.start()
    for copy in copies:
        copy.wait()
    for k, out_ref in enumerate((first_ref, last_ref)):
        values = [field_ref[k, c] for c in range(3)]
        totals = [field_ref[2 + k, c] + row_sum(values[c], 0.0, 0.0) + x_sum(values[c]) for c in range(3)]
        planes = values + [source_ref[k, c] for c in range(3)] + totals + [1.0 + material_ref[k].astype(F32)]
        for pair in range(5):
            both = jnp.concatenate(planes[2 * pair:2 * pair + 2], axis=0)
            out_ref[16 * pair:16 * pair + 16, :] = both.astype(BF16)


def rim_rows(first, last):
    row = lax.broadcasted_iota(jnp.int32, (16, first.shape[1]), 0)
    return jnp.where(row == 0, first, jnp.where(row == 15, last, 0.0))


def z_faces(field_ref, base_ref, coupling_ref, before_ref, after_ref, far_ref, pair_ref):
    even = lax.rem(lax.axis_index("slab"), 2) == 0
    before = bands(before_ref, 2)
    after = bands(after_ref, 2)
    faces = []
    for z in (0, 7):
        here = slice(16 * z, 16 * z + 16)
        coupling = coupling_ref[here, :]
        lines, values, partials = [], [], []
        for c in range(3):
            at = 8 * (c % 2) + z
            lines += [before[c // 2][at:at + 1, :], after[c // 2][at:at + 1, :]]
            values.append(field_ref[c, here, :])
            partials.append(base_ref[c, here, :] + coupling * rim_rows(lines[2 * c], lines[2 * c + 1]))
        faces.append(values + partials + [coupling, stacked(lines, 16)])
    for k, (first, last) in enumerate(zip(*faces)):
        here = slice(16 * k, 16 * k + 16)
        far_ref[here, :] = jnp.where(even, first, last).astype(BF16)
        pair_ref[here, :] = jnp.where(even, last, first).astype(BF16)


def stacked(lines, height):
    row = lax.broadcasted_iota(jnp.int32, (height, lines[0].shape[1]), 0)
    value = jnp.zeros(row.shape, F32)
    for k in range(len(lines)):
        value = jnp.where(row == k, lines[k], value)
    return value


def column_of(row):
    length = row.shape[1]
    down = lax.broadcasted_iota(jnp.int32, (length, length), 0)
    along = lax.broadcasted_iota(jnp.int32, (length, length), 1)
    return jnp.sum(jnp.where(down == along, row, 0.0), axis=1, keepdims=True)


def bands(ref, count):
    return [ref[16 * k:16 * k + 16, :].astype(F32) for k in range(count)]


EDGES = (0, 1, 6, 7)


def no_halo(stiff_ref, mass_ref, field_ref, source_ref, material_ref, cells_ref,
            base_ref, scaled_ref, coupling_ref, edge_ref, chosen_ref, place_ref):
    rows = table_rows(stiff_ref, mass_ref, field_ref.shape[-1])
    for z in range(8):
        here = slice(16 * z, 16 * z + 16)
        weight, coupling = lookup(material_ref[here, :], rows)
        coupling_ref[here, :] = coupling
        for c in range(3):
            value = field_ref[c, here, :]
            total = row_sum(value, 0.0, 0.0) + x_sum(value)
            if z > 0:
                total = total + field_ref[c, 16 * z - 16:16 * z, :]
            if z < 7:
                total = total + field_ref[c, 16 * z + 16:16 * z + 32, :]
            scaled = weight * source_ref[c, here, :]
            scaled_ref[c, here, :] = scaled
            base_ref[c, here, :] = KEEP * value + scaled + coupling * total

    width = field_ref.shape[-1]
    count = cells_ref.shape[1]
    cells = cells_ref[...].astype(F32)
    line = jnp.floor((cells + 0.5) * (1.0 / width))
    place_ref[...] = jnp.broadcast_to(column_of(cells - width * line), (count, 128))
    line_column = column_of(line)
    along = lax.broadcasted_iota(jnp.int32, (count, 192), 1).astype(F32)
    part = jnp.floor(along * (1.0 / 64) + 0.001)
    shift = along - 64.0 * part
    inner = 128.0 * part + shift + 32.0
    outer = 128.0 * part + jnp.where(shift < 32.0, shift, shift + 64.0)
    edge_ref[...] = jnp.where(outer == line_column, 1.0, 0.0).astype(BF16)
    chosen_ref[...] = jnp.where(inner == line_column, 1.0, 0.0).astype(BF16)


def relax_inner(stiff_ref, mass_ref, field_ref, base_ref, scaled_ref, coupling_ref, before_ref, after_ref, chosen_ref, place_ref,
                once_ref, rim_ref, out_ref, spread_ref, plain_ref):
    rows = table_rows(stiff_ref, mass_ref, field_ref.shape[-1])
    lines = []
    for side, (ref, y) in enumerate(((before_ref, 0), (after_ref, 15))):
        halo = bands(ref, 5)
        planes = [halo[k // 2][8 * (k % 2):8 * (k % 2) + 8] for k in range(10)]
        weight, coupling = lookup(planes[9] - 1.0, rows)
        coupling = jnp.where(planes[9] > 0.0, coupling, 0.0)
        rim_ref[6 * side + 3] = coupling
        for c in range(3):
            total = planes[6 + c] + line_rows(field_ref, y, c)
            rim_ref[6 * side + c] = KEEP * planes[c] + weight * planes[3 + c] + coupling * total
        lines.append(planes[:3])
    for z in range(8):
        here = slice(16 * z, 16 * z + 16)
        for c in range(3):
            halo = rim_rows(lines[0][c][z:z + 1], lines[1][c][z:z + 1])
            once_ref[c, here, :] = base_ref[c, here, :] + coupling_ref[here, :] * halo
    for z in range(2, 6):
        here = slice(16 * z, 16 * z + 16)
        for c in range(3):
            value = once_ref[c, here, :]
            total = once_ref[c, 16 * z - 16:16 * z, :] + once_ref[c, 16 * z + 16:16 * z + 32, :] + x_sum(value)
            total = total + row_sum(value, rim_ref[c, z:z + 1, :], rim_ref[6 + c, z:z + 1, :])
            result = KEEP * value + scaled_ref[c, here, :] + coupling_ref[here, :] * total
            out_ref[c, 16 * z - 32:16 * z - 16, :] = result
            at = 64 * c + 16 * z - 32
            plain_ref[at:at + 16, :] = result.astype(BF16)
    picked = jnp.dot(chosen_ref[...], plain_ref[...], preferred_element_type=F32)
    spread_ref[...] = spread_of(picked, place_ref[:, 0:1])


def spread_of(picked, place_column):
    along = lax.broadcasted_iota(jnp.int32, picked.shape, 1).astype(F32)
    single = jnp.where(along == place_column, picked, 0.0).astype(BF16)
    return jnp.dot(single, jnp.ones((picked.shape[1], 128), BF16), preferred_element_type=F32)


def relax_edges(planes, field_ref, once_ref, scaled_ref, coupling_ref, rim_ref, edge_ref, place_ref, spread_ref,
                far_ref, pair_ref, right_ref, out_ref, send_ref, plain_ref):
    even = lax.rem(lax.axis_index("slab"), 2) == 0
    both = list(zip(bands(far_ref, 8), bands(pair_ref, 8)))
    halo = [[jnp.where(even, far, pair) for far, pair in both], [jnp.where(even, pair, far) for far, pair in both]]
    row8 = lax.broadcasted_iota(jnp.int32, (8, field_ref.shape[-1]), 0)
    for c in range(3):
        once = {z: once_ref[c, 16 * z:16 * z + 16, :] for z in (1, 2, 5, 6)}
        once[0] = once_ref[c, 0:16, :] + coupling_ref[0:16, :] * halo[0][c]
        once[7] = once_ref[c, 112:128, :] + coupling_ref[112:128, :] * halo[1][c]
        once[-1] = halo[0][3 + c] + halo[0][6] * field_ref[c, 0:16, :]
        once[8] = halo[1][3 + c] + halo[1][6] * field_ref[c, 112:128, :]
        rims = []
        for side in range(2):
            at = 2 * c + side
            corner = jnp.where(row8 == 0, halo[0][7][at:at + 1], 0.0) + jnp.where(row8 == 7, halo[1][7][at:at + 1], 0.0)
            rims.append(rim_ref[6 * side + c] + rim_ref[6 * side + 3] * corner)
        for order, z in enumerate(EDGES):
            here = slice(16 * z, 16 * z + 16)
            total = once[z - 1] + once[z + 1] + x_sum(once[z])
            total = total + row_sum(once[z], rims[0][z:z + 1], rims[1][z:z + 1])
            result = KEEP * once[z] + scaled_ref[c, here, :] + coupling_ref[here, :] * total
            out_ref[c, 16 * order:16 * order + 16, :] = result
            at = 64 * c + 16 * order
            plain_ref[at:at + 16, :] = result.astype(BF16)

    picked = jnp.dot(edge_ref[...], plain_ref[...], preferred_element_type=F32)
    spread = spread_ref[...] + spread_of(picked, place_ref[:, 0:1])
    far = jnp.dot(right_ref[...], spread.astype(BF16), preferred_element_type=F32)
    ranks = 16
    lane = lax.broadcasted_iota(jnp.int32, (PLANE, 128), 1)
    parts = [jnp.zeros((PLANE, 128), F32) for _ in range(2)]
    for k in range(ranks):
        for z in range(planes):
            group = far[PLANE * (k * planes + z):PLANE * (k * planes + z + 1), :]
            at = z * ranks + k
            parts[at // 128] = jnp.where(lane == at % 128, group, parts[at // 128])
    down = lax.broadcasted_iota(jnp.int32, (128, 128), 0)
    across = lax.broadcasted_iota(jnp.int32, (128, 128), 1)
    traces = []
    for half in range(2):
        piece = jnp.where(down == across, spread[128 * half:128 * half + 128, :], 0.0)
        traces.append(jnp.sum(piece, axis=0, keepdims=True))
    tiles = send_ref.shape[0] // PLANE
    for to in range(PLANE):
        packet = stacked([parts[0][to:to + 1, :], parts[1][to:to + 1, :]] + traces, 4).astype(BF16)
        for tile in range(tiles):
            send_ref[seat(to, PLANE) * tiles + seat(tile, tiles)] = packet


def assemble(inner_ref, edges_ref, out_hbm, sems):
    copies = []
    for c in range(3):
        for source, target in ((edges_ref.at[c, 0:32], (0, 32)), (inner_ref.at[c], (32, 64)), (edges_ref.at[c, 32:64], (96, 32))):
            copies.append(pltpu.make_async_copy(source, out_hbm.at[c, pl.ds(*target), :], sems.at[len(copies)]))
    for copy in copies:
        copy.start()
    for copy in copies:
        copy.wait()


def middle(tiles, got_ref, send_ref):
    across = lax.rem(lax.axis_index("slab"), PLANE)
    tile = lax.axis_index("tile")
    total = jnp.sum(got_ref[...].astype(F32), axis=0)
    other = jnp.where(across == 0, PLANE - 1, 0)
    relay = []
    for b in range(3):
        wanted = tile + b - 1
        inside = (wanted >= 0) & (wanted < tiles)
        packet = got_ref[seated(other, PLANE) * tiles + seated(wanted, tiles)].astype(F32)
        packet = jnp.where(inside, packet, 0.0)
        relay += [packet[2:3, :], packet[3:4, :]]
    high = total.astype(BF16).astype(F32)
    low = total - high
    for half in range(2):
        packet = stacked([high[half:half + 1, :], low[half:half + 1, :]] + relay, 8).astype(BF16)
        for z in range(8 * half, min(8 * half + 8, send_ref.shape[0])):
            send_ref[seat(z, send_ref.shape[0])] = packet


def masked_rows(rows, factors):
    lines = [jnp.concatenate(row, axis=1) * factor.astype(F32) for row, factor in zip(rows, factors)]
    return stacked(lines, 16).astype(BF16)


def products(rows, blocks, count):
    every = lax.dot_general(rows, blocks, (((1,), (1,)), ((), ())), preferred_element_type=F32)
    result = every[0:1, 0:256]
    for k in range(1, count):
        result = result + every[k:k + 1, 256 * k:256 * k + 256]
    return result


def near_inside(tiles, mask_ref, got_ref, near_ref, out_ref):
    across = lax.rem(lax.axis_index("slab"), PLANE)
    tile = lax.axis_index("tile")
    rows = []
    for a in range(-1, 2):
        for b in range(-1, 2):
            up, beside = across + a, tile + b
            inside = (up >= 0) & (up < PLANE) & (beside >= 0) & (beside < tiles)
            packet = got_ref[seated(up, PLANE) * tiles + seated(beside, tiles)].astype(F32)
            packet = jnp.where(inside, packet, 0.0)
            rows.append((packet[2:3, :], packet[3:4, :]))
    out_ref[...] = products(masked_rows(rows, [mask_ref[0:1, q:q + 1] for q in range(9)]), near_ref[...], 9)


def finish(planes, mask_ref, rank_ref, part_ref, relay_ref, near_ref, left_ref, out_ref):
    slab = lax.axis_index("slab")
    across = lax.rem(slab, PLANE)
    plane = lax.div(slab, PLANE)
    upward = across == PLANE - 1
    start = jnp.where(upward, plane + 1, plane - 1)
    edge = ((across == 0) | upward) & (start >= 0) & (start < planes)
    packet = jnp.where(edge, relay_ref[seated(start, planes)].astype(F32), 0.0)
    rows = [(packet[2 + 2 * b:3 + 2 * b, :], packet[3 + 2 * b:4 + 2 * b, :]) for b in range(3)]
    first = jnp.where(upward, 6, 0)
    blocks = near_ref[pl.ds(pl.multiple_of(256 * first, 256), 768), :]
    factors = [jnp.where(upward, mask_ref[0:1, 6 + b:7 + b], mask_ref[0:1, b:b + 1]) for b in range(3)]
    near = products(masked_rows(rows, factors), blocks, 3)
    total = jnp.sum(relay_ref[...].astype(F32), axis=0)
    total = jnp.broadcast_to(total[0:1, :] + total[1:2, :], (8, 128))
    lane = lax.broadcasted_iota(jnp.int32, total.shape, 1)
    at = 16 * lax.rem(plane, 8)
    total = jnp.where((lane >= at) & (lane < at + rank_ref[...]), total, 0.0)
    high = total.astype(BF16).astype(F32)
    halves = jnp.concatenate([high, total - high], axis=0).astype(BF16)
    left = jnp.concatenate([left_ref[...]] * 8, axis=0)
    far = jnp.dot(halves, left, preferred_element_type=F32)
    out_ref[...] = part_ref[...] + near + far[0:1, :] + far[8:9, :]


def vmem():
    return pl.BlockSpec(memory_space=pltpu.VMEM)


def hbm():
    return pl.BlockSpec(memory_space=pltpu.HBM)


def exchange(first, last, axis):
    devices = lax.axis_size(axis)
    up = [(i, i + 1) for i in range(devices - 1)]
    down = [(j, i) for i, j in up]
    return lax.ppermute(last, axis, up), lax.ppermute(first, axis, down)


def swap(far, pair, axis):
    devices = lax.axis_size(axis)
    far = lax.ppermute(far, axis, [(i, i + 1 if i % 2 else i - 1) for i in range(1, devices - 1)])
    return far, lax.ppermute(pair, axis, [(i, i ^ 1) for i in range(devices)])


def local(initial_field, source, material, stiffness_table, mass_table, trace_cells, near_blocks, near_mask, far_left, far_right,
          block_ranks):
    slabs, tiles = lax.axis_size("slab"), lax.axis_size("tile")
    planes = slabs // PLANE
    volume = jax.ShapeDtypeStruct((3, 128, 384), F32)
    face = jax.ShapeDtypeStruct((80, 384), BF16)
    params = pltpu.CompilerParams(vmem_limit_bytes=24 * 1024 * 1024)
    first, last = pl.pallas_call(
        y_faces,
        out_shape=(face, face),
        in_specs=[hbm()] * 3,
        out_specs=(vmem(), vmem()),
        scratch_shapes=[
            pltpu.VMEM((4, 3, 8, 384), F32), pltpu.VMEM((2, 3, 8, 384), F32), pltpu.VMEM((2, 8, 384), jnp.int32),
            pltpu.SemaphoreType.DMA((8,)),
        ],
        compiler_params=pltpu.CompilerParams(vmem_limit_bytes=55050 * 1024),
    )(initial_field, source, material)
    tables = (stiffness_table.reshape(1, 8), mass_table.reshape(1, 8))
    field = initial_field.reshape(3, 128, 384)
    sources = source.reshape(3, 128, 384)
    cells = material.reshape(128, 384)
    before, after = exchange(first, last, "tile")
    index = jax.ShapeDtypeStruct((256, 192), BF16)
    column = jax.ShapeDtypeStruct((256, 128), F32)
    base, scaled, coupling, edge, chosen, place = pl.pallas_call(
        no_halo,
        out_shape=(volume, volume, jax.ShapeDtypeStruct((128, 384), F32), index, index, column),
        in_specs=[vmem()] * 6,
        out_specs=(vmem(),) * 6,
        compiler_params=params,
        cost_estimate=pl.CostEstimate(flops=6_000_000, bytes_accessed=3_000_000, transcendentals=0),
    )(*tables, field, sources, cells, trace_cells.reshape(1, 256))
    face = jax.ShapeDtypeStruct((128, 384), BF16)
    far, pair = pl.pallas_call(
        z_faces,
        out_shape=(face, face),
        in_specs=[vmem()] * 5,
        out_specs=(vmem(), vmem()),
        compiler_params=params,
    )(field, base, coupling, before, after)
    far, pair = swap(far, pair, "slab")
    members = PLANE * tiles
    once, rim, inner, spread = pl.pallas_call(
        relax_inner,
        out_shape=(volume, jax.ShapeDtypeStruct((12, 8, 384), F32), jax.ShapeDtypeStruct((3, 64, 384), F32), column),
        in_specs=[vmem()] * 10,
        out_specs=(vmem(),) * 4,
        scratch_shapes=[pltpu.VMEM((192, 384), BF16)],
        compiler_params=params,
        cost_estimate=pl.CostEstimate(flops=4_000_000, bytes_accessed=3_000_000, transcendentals=0),
    )(*tables, field, base, scaled, coupling, before, after, chosen, place)
    edges, send = pl.pallas_call(
        functools.partial(relax_edges, planes),
        out_shape=(jax.ShapeDtypeStruct((3, 64, 384), F32), jax.ShapeDtypeStruct((members, 4, 128), BF16)),
        in_specs=[vmem()] * 11,
        out_specs=(vmem(), vmem()),
        scratch_shapes=[pltpu.VMEM((192, 384), BF16)],
        compiler_params=params,
    )(field, once, scaled, coupling, rim, edge, place, spread, far, pair, far_right.reshape(-1, 256))
    ids = np.arange(slabs * tiles).reshape(planes, PLANE, tiles)
    ids = np.roll(ids, (-(planes // 2), -(PLANE // 2), -(tiles // 2)), axis=(0, 1, 2)).reshape(planes, members)
    got = lax.all_to_all(send, BOTH, 0, 0, axis_index_groups=ids.tolist(), tiled=True)
    send = pl.pallas_call(
        functools.partial(middle, tiles),
        out_shape=jax.ShapeDtypeStruct((planes, 8, 128), BF16),
        in_specs=[vmem()],
        out_specs=vmem(),
        compiler_params=params,
    )(got)
    relay = lax.all_to_all(send, BOTH, 0, 0, axis_index_groups=ids.T.tolist(), tiled=True)
    result = pl.pallas_call(
        assemble,
        out_shape=volume,
        in_specs=[vmem(), vmem()],
        out_specs=hbm(),
        scratch_shapes=[pltpu.SemaphoreType.DMA((9,))],
        compiler_params=params,
        cost_estimate=pl.CostEstimate(flops=0, bytes_accessed=600_000, transcendentals=0),
    )(inner, edges)
    mask = near_mask.reshape(1, 9)
    blocks = near_blocks.reshape(-1, 256)
    part = pl.pallas_call(
        functools.partial(near_inside, tiles),
        out_shape=jax.ShapeDtypeStruct((1, 256), F32),
        in_specs=[vmem()] * 3,
        out_specs=vmem(),
        compiler_params=params,
        cost_estimate=pl.CostEstimate(flops=2 * 16 * 2304 * 256, bytes_accessed=2304 * 512, transcendentals=0),
    )(mask, got, blocks)
    boundary = pl.pallas_call(
        functools.partial(finish, planes),
        out_shape=jax.ShapeDtypeStruct((1, 256), F32),
        in_specs=[vmem()] * 6,
        out_specs=vmem(),
        compiler_params=params,
    )(mask, block_ranks.reshape(1, 1), part, relay, blocks, far_left.reshape(16, 256))
    return result.reshape(initial_field.shape), boundary.reshape(1, 1, 256)


def solution(mesh):
    placed = (
        P(None, "slab", "tile", None),
        P(None, "slab", "tile", None),
        P("slab", "tile", None),
        P(),
        P(),
        P("slab", "tile", None),
        P("slab", "tile", None, None, None),
        P("slab", "tile", None),
        P(None, "slab", "tile", None),
        P(None, None, "slab", "tile", None),
        P("slab"),
    )
    return jax.shard_map(
        local,
        mesh=mesh,
        in_specs=placed,
        out_specs=(P(None, "slab", "tile", None), P("slab", "tile", None)),
        check_vma=False,
    )
```

```python
import functools

import jax
import jax.numpy as jnp
import numpy as np
from jax import lax
from jax.experimental import pallas as pl
from jax.experimental.pallas import tpu as pltpu
from jax.sharding import PartitionSpec as P

RELAX = 0.8
KEEP = 1.0 - RELAX
PLANE = 8
F32 = jnp.float32
BF16 = jnp.bfloat16
BOTH = ("slab", "tile")


def seat(member, count):
    away = member - count // 2
    return 2 * abs(away) - (away < 0)


def seated(member, count):
    away = jnp.clip(member, 0, count - 1) - count // 2
    return 2 * jnp.abs(away) - jnp.where(away < 0, 1, 0)


def seating(count):
    return np.argsort([seat(member, count) for member in range(count)])


def table_rows(stiff_ref, mass_ref, width):
    stiffness = stiff_ref[...]
    weight = RELAX / (6.0 * stiffness + mass_ref[...])
    rows = []
    for table in (weight, stiffness * weight):
        rows += [jnp.broadcast_to(table[:, entry:entry + 1], (1, width)) for entry in range(8)]
    return rows


def lookup(material, rows):
    weight = jnp.broadcast_to(rows[0], material.shape)
    coupling = jnp.broadcast_to(rows[8], material.shape)
    for entry in range(1, 8):
        here = material == entry
        weight = jnp.where(here, rows[entry], weight)
        coupling = jnp.where(here, rows[8 + entry], coupling)
    return weight, coupling


def x_sum(value):
    width = value.shape[-1]
    lane = lax.broadcasted_iota(jnp.int32, value.shape, value.ndim - 1)
    before = jnp.where(lane == 0, 0.0, pltpu.roll(value, 1, value.ndim - 1))
    after = jnp.where(lane == width - 1, 0.0, pltpu.roll(value, width - 1, value.ndim - 1))
    return before + after


def row_sum(value, first, last):
    length = value.shape[0]
    row = lax.broadcasted_iota(jnp.int32, value.shape, 0)
    before = jnp.where(row == 0, first, pltpu.roll(value, 1, 0))
    after = jnp.where(row == length - 1, last, pltpu.roll(value, length - 1, 0))
    return before + after


def line_rows(ref, y, *lead):
    lines = [ref[(*lead, slice(16 * z + y, 16 * z + y + 1), slice(None))] for z in range(8)]
    row = lax.broadcasted_iota(jnp.int32, (8, lines[0].shape[1]), 0)
    value = jnp.broadcast_to(lines[0], row.shape)
    for z in range(1, 8):
        value = jnp.where(row == z, lines[z], value)
    return value


def y_faces(field_hbm, source_hbm, material_hbm, first_ref, last_ref, field_ref, source_ref, material_ref, sems):
    pairs = [(field_hbm.at[:, :, y, :], field_ref.at[k]) for k, y in enumerate((0, 15, 1, 14))]
    pairs += [(source_hbm.at[:, :, y, :], source_ref.at[k]) for k, y in enumerate((0, 15))]
    pairs += [(material_hbm.at[:, y, :], material_ref.at[k]) for k, y in enumerate((0, 15))]
    copies = [pltpu.make_async_copy(src, dst, sems.at[k]) for k, (src, dst) in enumerate(pairs)]
    for copy in copies:
        copy.start()
    for copy in copies:
        copy.wait()
    for k, out_ref in enumerate((first_ref, last_ref)):
        values = [field_ref[k, c] for c in range(3)]
        totals = [field_ref[2 + k, c] + row_sum(values[c], 0.0, 0.0) + x_sum(values[c]) for c in range(3)]
        planes = values + [source_ref[k, c] for c in range(3)] + totals + [1.0 + material_ref[k].astype(F32)]
        for pair in range(5):
            both = jnp.concatenate(planes[2 * pair:2 * pair + 2], axis=0)
            out_ref[16 * pair:16 * pair + 16, :] = both.astype(BF16)


def rim_rows(first, last):
    row = lax.broadcasted_iota(jnp.int32, (16, first.shape[1]), 0)
    return jnp.where(row == 0, first, jnp.where(row == 15, last, 0.0))


def z_faces(field_ref, base_ref, coupling_ref, before_ref, after_ref, far_ref, pair_ref):
    even = lax.rem(lax.axis_index("slab"), 2) == 0
    before = bands(before_ref, 2)
    after = bands(after_ref, 2)
    faces = []
    for z in (0, 7):
        here = slice(16 * z, 16 * z + 16)
        coupling = coupling_ref[here, :]
        lines, values, partials = [], [], []
        for c in range(3):
            at = 8 * (c % 2) + z
            lines += [before[c // 2][at:at + 1, :], after[c // 2][at:at + 1, :]]
            values.append(field_ref[c, here, :])
            partials.append(base_ref[c, here, :] + coupling * rim_rows(lines[2 * c], lines[2 * c + 1]))
        faces.append(values + partials + [coupling, stacked(lines, 16)])
    for k, (first, last) in enumerate(zip(*faces)):
        here = slice(16 * k, 16 * k + 16)
        far_ref[here, :] = jnp.where(even, first, last).astype(BF16)
        pair_ref[here, :] = jnp.where(even, last, first).astype(BF16)


def stacked(lines, height):
    row = lax.broadcasted_iota(jnp.int32, (height, lines[0].shape[1]), 0)
    value = jnp.zeros(row.shape, F32)
    for k in range(len(lines)):
        value = jnp.where(row == k, lines[k], value)
    return value


def column_of(row):
    length = row.shape[1]
    down = lax.broadcasted_iota(jnp.int32, (length, length), 0)
    along = lax.broadcasted_iota(jnp.int32, (length, length), 1)
    return jnp.sum(jnp.where(down == along, row, 0.0), axis=1, keepdims=True)


def bands(ref, count):
    return [ref[16 * k:16 * k + 16, :].astype(F32) for k in range(count)]


EDGES = (0, 1, 6, 7)


def no_halo(stiff_ref, mass_ref, field_ref, source_ref, material_ref, cells_ref,
            base_ref, scaled_ref, coupling_ref, edge_ref, chosen_ref, place_ref):
    rows = table_rows(stiff_ref, mass_ref, field_ref.shape[-1])
    for z in range(8):
        here = slice(16 * z, 16 * z + 16)
        weight, coupling = lookup(material_ref[here, :], rows)
        coupling_ref[here, :] = coupling
        for c in range(3):
            value = field_ref[c, here, :]
            total = row_sum(value, 0.0, 0.0) + x_sum(value)
            if z > 0:
                total = total + field_ref[c, 16 * z - 16:16 * z, :]
            if z < 7:
                total = total + field_ref[c, 16 * z + 16:16 * z + 32, :]
            scaled = weight * source_ref[c, here, :]
            scaled_ref[c, here, :] = scaled
            base_ref[c, here, :] = KEEP * value + scaled + coupling * total

    width = field_ref.shape[-1]
    count = cells_ref.shape[1]
    cells = cells_ref[...].astype(F32)
    line = jnp.floor((cells + 0.5) * (1.0 / width))
    place_ref[...] = jnp.broadcast_to(column_of(cells - width * line), (count, 128))
    line_column = column_of(line)
    along = lax.broadcasted_iota(jnp.int32, (count, 192), 1).astype(F32)
    part = jnp.floor(along * (1.0 / 64) + 0.001)
    shift = along - 64.0 * part
    inner = 128.0 * part + shift + 32.0
    outer = 128.0 * part + jnp.where(shift < 32.0, shift, shift + 64.0)
    edge_ref[...] = jnp.where(outer == line_column, 1.0, 0.0).astype(BF16)
    chosen_ref[...] = jnp.where(inner == line_column, 1.0, 0.0).astype(BF16)


def relax_inner(stiff_ref, mass_ref, field_ref, base_ref, scaled_ref, coupling_ref, before_ref, after_ref, chosen_ref, place_ref,
                once_ref, rim_ref, out_ref, spread_ref, plain_ref):
    rows = table_rows(stiff_ref, mass_ref, field_ref.shape[-1])
    lines = []
    for side, (ref, y) in enumerate(((before_ref, 0), (after_ref, 15))):
        halo = bands(ref, 5)
        planes = [halo[k // 2][8 * (k % 2):8 * (k % 2) + 8] for k in range(10)]
        weight, coupling = lookup(planes[9] - 1.0, rows)
        coupling = jnp.where(planes[9] > 0.0, coupling, 0.0)
        rim_ref[6 * side + 3] = coupling
        for c in range(3):
            total = planes[6 + c] + line_rows(field_ref, y, c)
            rim_ref[6 * side + c] = KEEP * planes[c] + weight * planes[3 + c] + coupling * total
        lines.append(planes[:3])
    for z in range(8):
        here = slice(16 * z, 16 * z + 16)
        for c in range(3):
            halo = rim_rows(lines[0][c][z:z + 1], lines[1][c][z:z + 1])
            once_ref[c, here, :] = base_ref[c, here, :] + coupling_ref[here, :] * halo
    for z in range(2, 6):
        here = slice(16 * z, 16 * z + 16)
        for c in range(3):
            value = once_ref[c, here, :]
            total = once_ref[c, 16 * z - 16:16 * z, :] + once_ref[c, 16 * z + 16:16 * z + 32, :] + x_sum(value)
            total = total + row_sum(value, rim_ref[c, z:z + 1, :], rim_ref[6 + c, z:z + 1, :])
            result = KEEP * value + scaled_ref[c, here, :] + coupling_ref[here, :] * total
            out_ref[c, 16 * z - 32:16 * z - 16, :] = result
            at = 64 * c + 16 * z - 32
            plain_ref[at:at + 16, :] = result.astype(BF16)
    picked = jnp.dot(chosen_ref[...], plain_ref[...], preferred_element_type=F32)
    spread_ref[...] = spread_of(picked, place_ref[:, 0:1])


def spread_of(picked, place_column):
    along = lax.broadcasted_iota(jnp.int32, picked.shape, 1).astype(F32)
    single = jnp.where(along == place_column, picked, 0.0).astype(BF16)
    return jnp.dot(single, jnp.ones((picked.shape[1], 128), BF16), preferred_element_type=F32)


def relax_edges(planes, field_ref, once_ref, scaled_ref, coupling_ref, rim_ref, edge_ref, place_ref, spread_ref,
                far_ref, pair_ref, right_ref, out_ref, send_ref, plain_ref):
    even = lax.rem(lax.axis_index("slab"), 2) == 0
    both = list(zip(bands(far_ref, 8), bands(pair_ref, 8)))
    halo = [[jnp.where(even, far, pair) for far, pair in both], [jnp.where(even, pair, far) for far, pair in both]]
    row8 = lax.broadcasted_iota(jnp.int32, (8, field_ref.shape[-1]), 0)
    for c in range(3):
        once = {z: once_ref[c, 16 * z:16 * z + 16, :] for z in (1, 2, 5, 6)}
        once[0] = once_ref[c, 0:16, :] + coupling_ref[0:16, :] * halo[0][c]
        once[7] = once_ref[c, 112:128, :] + coupling_ref[112:128, :] * halo[1][c]
        once[-1] = halo[0][3 + c] + halo[0][6] * field_ref[c, 0:16, :]
        once[8] = halo[1][3 + c] + halo[1][6] * field_ref[c, 112:128, :]
        rims = []
        for side in range(2):
            at = 2 * c + side
            corner = jnp.where(row8 == 0, halo[0][7][at:at + 1], 0.0) + jnp.where(row8 == 7, halo[1][7][at:at + 1], 0.0)
            rims.append(rim_ref[6 * side + c] + rim_ref[6 * side + 3] * corner)
        for order, z in enumerate(EDGES):
            here = slice(16 * z, 16 * z + 16)
            total = once[z - 1] + once[z + 1] + x_sum(once[z])
            total = total + row_sum(once[z], rims[0][z:z + 1], rims[1][z:z + 1])
            result = KEEP * once[z] + scaled_ref[c, here, :] + coupling_ref[here, :] * total
            out_ref[c, 16 * order:16 * order + 16, :] = result
            at = 64 * c + 16 * order
            plain_ref[at:at + 16, :] = result.astype(BF16)

    picked = jnp.dot(edge_ref[...], plain_ref[...], preferred_element_type=F32)
    spread = spread_ref[...] + spread_of(picked, place_ref[:, 0:1])
    far = jnp.dot(right_ref[...], spread.astype(BF16), preferred_element_type=F32)
    ranks = 16
    lane = lax.broadcasted_iota(jnp.int32, (PLANE, 128), 1)
    parts = [jnp.zeros((PLANE, 128), F32) for _ in range(2)]
    for k in range(ranks):
        for z in range(planes):
            group = far[PLANE * (k * planes + z):PLANE * (k * planes + z + 1), :]
            at = z * ranks + k
            parts[at // 128] = jnp.where(lane == at % 128, group, parts[at // 128])
    down = lax.broadcasted_iota(jnp.int32, (128, 128), 0)
    across = lax.broadcasted_iota(jnp.int32, (128, 128), 1)
    traces = []
    for half in range(2):
        piece = jnp.where(down == across, spread[128 * half:128 * half + 128, :], 0.0)
        traces.append(jnp.sum(piece, axis=0, keepdims=True))
    tiles = send_ref.shape[0] // PLANE
    for to in range(PLANE):
        packet = stacked([parts[0][to:to + 1, :], parts[1][to:to + 1, :]] + traces, 4).astype(BF16)
        for tile in range(tiles):
            send_ref[seat(to, PLANE) * tiles + seat(tile, tiles)] = packet


def assemble(inner_ref, edges_ref, out_hbm, sems):
    copies = []
    for c in range(3):
        for source, target in ((edges_ref.at[c, 0:32], (0, 32)), (inner_ref.at[c], (32, 64)), (edges_ref.at[c, 32:64], (96, 32))):
            copies.append(pltpu.make_async_copy(source, out_hbm.at[c, pl.ds(*target), :], sems.at[len(copies)]))
    for copy in copies:
        copy.start()
    for copy in copies:
        copy.wait()


def middle(tiles, got_ref, send_ref):
    across = lax.rem(lax.axis_index("slab"), PLANE)
    tile = lax.axis_index("tile")
    total = jnp.sum(got_ref[...].astype(F32), axis=0)
    other = jnp.where(across == 0, PLANE - 1, 0)
    relay = []
    for b in range(3):
        wanted = tile + b - 1
        inside = (wanted >= 0) & (wanted < tiles)
        packet = got_ref[seated(other, PLANE) * tiles + seated(wanted, tiles)].astype(F32)
        packet = jnp.where(inside, packet, 0.0)
        relay += [packet[2:3, :], packet[3:4, :]]
    high = total.astype(BF16).astype(F32)
    low = total - high
    for half in range(2):
        packet = stacked([high[half:half + 1, :], low[half:half + 1, :]] + relay, 8).astype(BF16)
        for z in range(8 * half, min(8 * half + 8, send_ref.shape[0])):
            send_ref[seat(z, send_ref.shape[0])] = packet


def masked_rows(rows, factors):
    lines = [jnp.concatenate(row, axis=1) * factor.astype(F32) for row, factor in zip(rows, factors)]
    return stacked(lines, 16).astype(BF16)


def products(rows, blocks, count):
    every = lax.dot_general(rows, blocks, (((1,), (1,)), ((), ())), preferred_element_type=F32)
    result = every[0:1, 0:256]
    for k in range(1, count):
        result = result + every[k:k + 1, 256 * k:256 * k + 256]
    return result


def near_inside(tiles, mask_ref, got_ref, near_ref, out_ref):
    across = lax.rem(lax.axis_index("slab"), PLANE)
    tile = lax.axis_index("tile")
    rows = []
    for a in range(-1, 2):
        for b in range(-1, 2):
            up, beside = across + a, tile + b
            inside = (up >= 0) & (up < PLANE) & (beside >= 0) & (beside < tiles)
            packet = got_ref[seated(up, PLANE) * tiles + seated(beside, tiles)].astype(F32)
            packet = jnp.where(inside, packet, 0.0)
            rows.append((packet[2:3, :], packet[3:4, :]))
    out_ref[...] = products(masked_rows(rows, [mask_ref[0:1, q:q + 1] for q in range(9)]), near_ref[...], 9)


def finish(planes, mask_ref, rank_ref, part_ref, relay_ref, near_ref, left_ref, out_ref):
    slab = lax.axis_index("slab")
    across = lax.rem(slab, PLANE)
    plane = lax.div(slab, PLANE)
    upward = across == PLANE - 1
    start = jnp.where(upward, plane + 1, plane - 1)
    edge = ((across == 0) | upward) & (start >= 0) & (start < planes)
    packet = jnp.where(edge, relay_ref[seated(start, planes)].astype(F32), 0.0)
    rows = [(packet[2 + 2 * b:3 + 2 * b, :], packet[3 + 2 * b:4 + 2 * b, :]) for b in range(3)]
    first = jnp.where(upward, 6, 0)
    blocks = near_ref[pl.ds(pl.multiple_of(256 * first, 256), 768), :]
    factors = [jnp.where(upward, mask_ref[0:1, 6 + b:7 + b], mask_ref[0:1, b:b + 1]) for b in range(3)]
    near = products(masked_rows(rows, factors), blocks, 3)
    total = jnp.sum(relay_ref[...].astype(F32), axis=0)
    total = jnp.broadcast_to(total[0:1, :] + total[1:2, :], (8, 128))
    lane = lax.broadcasted_iota(jnp.int32, total.shape, 1)
    at = 16 * lax.rem(plane, 8)
    total = jnp.where((lane >= at) & (lane < at + rank_ref[...]), total, 0.0)
    high = total.astype(BF16).astype(F32)
    halves = jnp.concatenate([high, total - high], axis=0).astype(BF16)
    left = jnp.concatenate([left_ref[...]] * 8, axis=0)
    far = jnp.dot(halves, left, preferred_element_type=F32)
    out_ref[...] = part_ref[...] + near + far[0:1, :] + far[8:9, :]


def vmem():
    return pl.BlockSpec(memory_space=pltpu.VMEM)


def hbm():
    return pl.BlockSpec(memory_space=pltpu.HBM)


def exchange(first, last, axis):
    devices = lax.axis_size(axis)
    up = [(i, i + 1) for i in range(devices - 1)]
    down = [(j, i) for i, j in up]
    return lax.ppermute(last, axis, up), lax.ppermute(first, axis, down)


def swap(far, pair, axis):
    devices = lax.axis_size(axis)
    far = lax.ppermute(far, axis, [(i, i + 1 if i % 2 else i - 1) for i in range(1, devices - 1)])
    return far, lax.ppermute(pair, axis, [(i, i ^ 1) for i in range(devices)])


def local(initial_field, source, material, stiffness_table, mass_table, trace_cells, near_blocks, near_mask, far_left, far_right,
          block_ranks):
    slabs, tiles = lax.axis_size("slab"), lax.axis_size("tile")
    planes = slabs // PLANE
    volume = jax.ShapeDtypeStruct((3, 128, 384), F32)
    face = jax.ShapeDtypeStruct((80, 384), BF16)
    params = pltpu.CompilerParams(vmem_limit_bytes=24 * 1024 * 1024)
    first, last = pl.pallas_call(
        y_faces,
        out_shape=(face, face),
        in_specs=[hbm()] * 3,
        out_specs=(vmem(), vmem()),
        scratch_shapes=[
            pltpu.VMEM((4, 3, 8, 384), F32), pltpu.VMEM((2, 3, 8, 384), F32), pltpu.VMEM((2, 8, 384), jnp.int32),
            pltpu.SemaphoreType.DMA((8,)),
        ],
        compiler_params=pltpu.CompilerParams(vmem_limit_bytes=55050 * 1024),
    )(initial_field, source, material)
    tables = (stiffness_table.reshape(1, 8), mass_table.reshape(1, 8))
    field = initial_field.reshape(3, 128, 384)
    sources = source.reshape(3, 128, 384)
    cells = material.reshape(128, 384)
    before, after = exchange(first, last, "tile")
    index = jax.ShapeDtypeStruct((256, 192), BF16)
    column = jax.ShapeDtypeStruct((256, 128), F32)
    base, scaled, coupling, edge, chosen, place = pl.pallas_call(
        no_halo,
        out_shape=(volume, volume, jax.ShapeDtypeStruct((128, 384), F32), index, index, column),
        in_specs=[vmem()] * 6,
        out_specs=(vmem(),) * 6,
        compiler_params=params,
        cost_estimate=pl.CostEstimate(flops=6_000_000, bytes_accessed=3_000_000, transcendentals=0),
    )(*tables, field, sources, cells, trace_cells.reshape(1, 256))
    face = jax.ShapeDtypeStruct((128, 384), BF16)
    far, pair = pl.pallas_call(
        z_faces,
        out_shape=(face, face),
        in_specs=[vmem()] * 5,
        out_specs=(vmem(), vmem()),
        compiler_params=params,
    )(field, base, coupling, before, after)
    far, pair = swap(far, pair, "slab")
    members = PLANE * tiles
    once, rim, inner, spread = pl.pallas_call(
        relax_inner,
        out_shape=(volume, jax.ShapeDtypeStruct((12, 8, 384), F32), jax.ShapeDtypeStruct((3, 64, 384), F32), column),
        in_specs=[vmem()] * 10,
        out_specs=(vmem(),) * 4,
        scratch_shapes=[pltpu.VMEM((192, 384), BF16)],
        compiler_params=params,
        cost_estimate=pl.CostEstimate(flops=4_000_000, bytes_accessed=3_000_000, transcendentals=0),
    )(*tables, field, base, scaled, coupling, before, after, chosen, place)
    edges, send = pl.pallas_call(
        functools.partial(relax_edges, planes),
        out_shape=(jax.ShapeDtypeStruct((3, 64, 384), F32), jax.ShapeDtypeStruct((members, 4, 128), BF16)),
        in_specs=[vmem()] * 11,
        out_specs=(vmem(), vmem()),
        scratch_shapes=[pltpu.VMEM((192, 384), BF16)],
        compiler_params=params,
    )(field, once, scaled, coupling, rim, edge, place, spread, far, pair, far_right.reshape(-1, 256))
    ids = np.arange(slabs * tiles).reshape(planes, PLANE, tiles)
    ids = ids[np.ix_(seating(planes), seating(PLANE), seating(tiles))].reshape(planes, members)
    got = lax.all_to_all(send, BOTH, 0, 0, axis_index_groups=ids.tolist(), tiled=True)
    send = pl.pallas_call(
        functools.partial(middle, tiles),
        out_shape=jax.ShapeDtypeStruct((planes, 8, 128), BF16),
        in_specs=[vmem()],
        out_specs=vmem(),
        compiler_params=params,
    )(got)
    relay = lax.all_to_all(send, BOTH, 0, 0, axis_index_groups=ids.T.tolist(), tiled=True)
    result = pl.pallas_call(
        assemble,
        out_shape=volume,
        in_specs=[vmem(), vmem()],
        out_specs=hbm(),
        scratch_shapes=[pltpu.SemaphoreType.DMA((9,))],
        compiler_params=params,
        cost_estimate=pl.CostEstimate(flops=0, bytes_accessed=600_000, transcendentals=0),
    )(inner, edges)
    mask = near_mask.reshape(1, 9)
    blocks = near_blocks.reshape(-1, 256)
    part = pl.pallas_call(
        functools.partial(near_inside, tiles),
        out_shape=jax.ShapeDtypeStruct((1, 256), F32),
        in_specs=[vmem()] * 3,
        out_specs=vmem(),
        compiler_params=params,
        cost_estimate=pl.CostEstimate(flops=2 * 16 * 2304 * 256, bytes_accessed=2304 * 512, transcendentals=0),
    )(mask, got, blocks)
    boundary = pl.pallas_call(
        functools.partial(finish, planes),
        out_shape=jax.ShapeDtypeStruct((1, 256), F32),
        in_specs=[vmem()] * 6,
        out_specs=vmem(),
        compiler_params=params,
    )(mask, block_ranks.reshape(1, 1), part, relay, blocks, far_left.reshape(16, 256))
    return result.reshape(initial_field.shape), boundary.reshape(1, 1, 256)


def solution(mesh):
    placed = (
        P(None, "slab", "tile", None),
        P(None, "slab", "tile", None),
        P("slab", "tile", None),
        P(),
        P(),
        P("slab", "tile", None),
        P("slab", "tile", None, None, None),
        P("slab", "tile", None),
        P(None, "slab", "tile", None),
        P(None, None, "slab", "tile", None),
        P("slab"),
    )
    return jax.shard_map(
        local,
        mesh=mesh,
        in_specs=placed,
        out_specs=(P(None, "slab", "tile", None), P("slab", "tile", None)),
        check_vma=False,
    )
```

```python
import functools

import jax
import jax.numpy as jnp
import numpy as np
from jax import lax
from jax.experimental import pallas as pl
from jax.experimental.pallas import tpu as pltpu
from jax.sharding import PartitionSpec as P

RELAX = 0.8
KEEP = 1.0 - RELAX
PLANE = 8
F32 = jnp.float32
BF16 = jnp.bfloat16
BOTH = ("slab", "tile")


def seat(member, count):
    return (member + count - count // 2) % count


def seated(member, count):
    return lax.rem(jnp.clip(member, 0, count - 1) + count - count // 2, count)


def table_rows(stiff_ref, mass_ref, width):
    stiffness = stiff_ref[...]
    weight = RELAX / (6.0 * stiffness + mass_ref[...])
    rows = []
    for table in (weight, stiffness * weight):
        rows += [jnp.broadcast_to(table[:, entry:entry + 1], (1, width)) for entry in range(8)]
    return rows


def lookup(material, rows):
    weight = jnp.broadcast_to(rows[0], material.shape)
    coupling = jnp.broadcast_to(rows[8], material.shape)
    for entry in range(1, 8):
        here = material == entry
        weight = jnp.where(here, rows[entry], weight)
        coupling = jnp.where(here, rows[8 + entry], coupling)
    return weight, coupling


def x_sum(value):
    width = value.shape[-1]
    lane = lax.broadcasted_iota(jnp.int32, value.shape, value.ndim - 1)
    before = jnp.where(lane == 0, 0.0, pltpu.roll(value, 1, value.ndim - 1))
    after = jnp.where(lane == width - 1, 0.0, pltpu.roll(value, width - 1, value.ndim - 1))
    return before + after


def row_sum(value, first, last):
    length = value.shape[0]
    row = lax.broadcasted_iota(jnp.int32, value.shape, 0)
    before = jnp.where(row == 0, first, pltpu.roll(value, 1, 0))
    after = jnp.where(row == length - 1, last, pltpu.roll(value, length - 1, 0))
    return before + after


def line_rows(ref, y, *lead):
    lines = [ref[(*lead, slice(16 * z + y, 16 * z + y + 1), slice(None))] for z in range(8)]
    row = lax.broadcasted_iota(jnp.int32, (8, lines[0].shape[1]), 0)
    value = jnp.broadcast_to(lines[0], row.shape)
    for z in range(1, 8):
        value = jnp.where(row == z, lines[z], value)
    return value


def even_slab():
    return lax.rem(lax.axis_index("slab"), 2) == 0


def in_order(one_ref, two_ref, count):
    even = even_slab()
    both = list(zip(bands(one_ref, count), bands(two_ref, count)))
    return [jnp.where(even, one, two) for one, two in both], [jnp.where(even, two, one) for one, two in both]


def y_faces(field_hbm, source_hbm, material_hbm, one_ref, two_ref, field_ref, source_ref, material_ref, sems):
    pairs = [(field_hbm.at[:, :, y, :], field_ref.at[k]) for k, y in enumerate((0, 15, 1, 14))]
    pairs += [(source_hbm.at[:, :, y, :], source_ref.at[k]) for k, y in enumerate((0, 15))]
    pairs += [(material_hbm.at[:, y, :], material_ref.at[k]) for k, y in enumerate((0, 15))]
    copies = [pltpu.make_async_copy(src, dst, sems.at[k]) for k, (src, dst) in enumerate(pairs)]
    for copy in copies:
        copy.start()
    for copy in copies:
        copy.wait()
    faces = []
    for k in range(2):
        values = [field_ref[k, c] for c in range(3)]
        totals = [field_ref[2 + k, c] + row_sum(values[c], 0.0, 0.0) + x_sum(values[c]) for c in range(3)]
        planes = values + [source_ref[k, c] for c in range(3)] + totals + [1.0 + material_ref[k].astype(F32)]
        faces.append([jnp.concatenate(planes[2 * pair:2 * pair + 2], axis=0) for pair in range(5)])
    even = even_slab()
    for pair, (first, last) in enumerate(zip(*faces)):
        here = slice(16 * pair, 16 * pair + 16)
        one_ref[here, :] = jnp.where(even, last, first).astype(BF16)
        two_ref[here, :] = jnp.where(even, first, last).astype(BF16)


def rim_rows(first, last):
    row = lax.broadcasted_iota(jnp.int32, (16, first.shape[1]), 0)
    return jnp.where(row == 0, first, jnp.where(row == 15, last, 0.0))


def z_faces(field_ref, base_ref, coupling_ref, one_ref, two_ref, far_ref, pair_ref):
    even = even_slab()
    before, after = in_order(one_ref, two_ref, 2)
    faces = []
    for z in (0, 7):
        here = slice(16 * z, 16 * z + 16)
        coupling = coupling_ref[here, :]
        lines, values, partials = [], [], []
        for c in range(3):
            at = 8 * (c % 2) + z
            lines += [before[c // 2][at:at + 1, :], after[c // 2][at:at + 1, :]]
            values.append(field_ref[c, here, :])
            partials.append(base_ref[c, here, :] + coupling * rim_rows(lines[2 * c], lines[2 * c + 1]))
        faces.append(values + partials + [coupling, stacked(lines, 16)])
    for k, (first, last) in enumerate(zip(*faces)):
        here = slice(16 * k, 16 * k + 16)
        far_ref[here, :] = jnp.where(even, first, last).astype(BF16)
        pair_ref[here, :] = jnp.where(even, last, first).astype(BF16)


def stacked(lines, height):
    row = lax.broadcasted_iota(jnp.int32, (height, lines[0].shape[1]), 0)
    value = jnp.zeros(row.shape, F32)
    for k in range(len(lines)):
        value = jnp.where(row == k, lines[k], value)
    return value


def column_of(row):
    length = row.shape[1]
    down = lax.broadcasted_iota(jnp.int32, (length, length), 0)
    along = lax.broadcasted_iota(jnp.int32, (length, length), 1)
    return jnp.sum(jnp.where(down == along, row, 0.0), axis=1, keepdims=True)


def bands(ref, count):
    return [ref[16 * k:16 * k + 16, :].astype(F32) for k in range(count)]


EDGES = (0, 1, 6, 7)


def no_halo(stiff_ref, mass_ref, field_ref, source_ref, material_ref, cells_ref,
            base_ref, scaled_ref, coupling_ref, edge_ref, chosen_ref, place_ref):
    rows = table_rows(stiff_ref, mass_ref, field_ref.shape[-1])
    for z in range(8):
        here = slice(16 * z, 16 * z + 16)
        weight, coupling = lookup(material_ref[here, :], rows)
        coupling_ref[here, :] = coupling
        for c in range(3):
            value = field_ref[c, here, :]
            total = row_sum(value, 0.0, 0.0) + x_sum(value)
            if z > 0:
                total = total + field_ref[c, 16 * z - 16:16 * z, :]
            if z < 7:
                total = total + field_ref[c, 16 * z + 16:16 * z + 32, :]
            scaled = weight * source_ref[c, here, :]
            scaled_ref[c, here, :] = scaled
            base_ref[c, here, :] = KEEP * value + scaled + coupling * total

    width = field_ref.shape[-1]
    count = cells_ref.shape[1]
    cells = cells_ref[...].astype(F32)
    line = jnp.floor((cells + 0.5) * (1.0 / width))
    place_ref[...] = jnp.broadcast_to(column_of(cells - width * line), (count, 128))
    line_column = column_of(line)
    along = lax.broadcasted_iota(jnp.int32, (count, 192), 1).astype(F32)
    part = jnp.floor(along * (1.0 / 64) + 0.001)
    shift = along - 64.0 * part
    inner = 128.0 * part + shift + 32.0
    outer = 128.0 * part + jnp.where(shift < 32.0, shift, shift + 64.0)
    edge_ref[...] = jnp.where(outer == line_column, 1.0, 0.0).astype(BF16)
    chosen_ref[...] = jnp.where(inner == line_column, 1.0, 0.0).astype(BF16)


def relax_inner(stiff_ref, mass_ref, field_ref, base_ref, scaled_ref, coupling_ref, one_ref, two_ref, chosen_ref, place_ref,
                once_ref, rim_ref, out_ref, spread_ref, plain_ref):
    rows = table_rows(stiff_ref, mass_ref, field_ref.shape[-1])
    lines = []
    for side, (halo, y) in enumerate(zip(in_order(one_ref, two_ref, 5), (0, 15))):
        planes = [halo[k // 2][8 * (k % 2):8 * (k % 2) + 8] for k in range(10)]
        weight, coupling = lookup(planes[9] - 1.0, rows)
        coupling = jnp.where(planes[9] > 0.0, coupling, 0.0)
        rim_ref[6 * side + 3] = coupling
        for c in range(3):
            total = planes[6 + c] + line_rows(field_ref, y, c)
            rim_ref[6 * side + c] = KEEP * planes[c] + weight * planes[3 + c] + coupling * total
        lines.append(planes[:3])
    for z in range(8):
        here = slice(16 * z, 16 * z + 16)
        for c in range(3):
            halo = rim_rows(lines[0][c][z:z + 1], lines[1][c][z:z + 1])
            once_ref[c, here, :] = base_ref[c, here, :] + coupling_ref[here, :] * halo
    for z in range(2, 6):
        here = slice(16 * z, 16 * z + 16)
        for c in range(3):
            value = once_ref[c, here, :]
            total = once_ref[c, 16 * z - 16:16 * z, :] + once_ref[c, 16 * z + 16:16 * z + 32, :] + x_sum(value)
            total = total + row_sum(value, rim_ref[c, z:z + 1, :], rim_ref[6 + c, z:z + 1, :])
            result = KEEP * value + scaled_ref[c, here, :] + coupling_ref[here, :] * total
            out_ref[c, 16 * z - 32:16 * z - 16, :] = result
            at = 64 * c + 16 * z - 32
            plain_ref[at:at + 16, :] = result.astype(BF16)
    picked = jnp.dot(chosen_ref[...], plain_ref[...], preferred_element_type=F32)
    spread_ref[...] = spread_of(picked, place_ref[:, 0:1])


def spread_of(picked, place_column):
    along = lax.broadcasted_iota(jnp.int32, picked.shape, 1).astype(F32)
    single = jnp.where(along == place_column, picked, 0.0).astype(BF16)
    return jnp.dot(single, jnp.ones((picked.shape[1], 128), BF16), preferred_element_type=F32)


def relax_edges(planes, field_ref, once_ref, scaled_ref, coupling_ref, rim_ref, edge_ref, place_ref, spread_ref,
                far_ref, pair_ref, right_ref, out_ref, send_ref, plain_ref):
    halo = in_order(far_ref, pair_ref, 8)
    row8 = lax.broadcasted_iota(jnp.int32, (8, field_ref.shape[-1]), 0)
    for c in range(3):
        once = {z: once_ref[c, 16 * z:16 * z + 16, :] for z in (1, 2, 5, 6)}
        once[0] = once_ref[c, 0:16, :] + coupling_ref[0:16, :] * halo[0][c]
        once[7] = once_ref[c, 112:128, :] + coupling_ref[112:128, :] * halo[1][c]
        once[-1] = halo[0][3 + c] + halo[0][6] * field_ref[c, 0:16, :]
        once[8] = halo[1][3 + c] + halo[1][6] * field_ref[c, 112:128, :]
        rims = []
        for side in range(2):
            at = 2 * c + side
            corner = jnp.where(row8 == 0, halo[0][7][at:at + 1], 0.0) + jnp.where(row8 == 7, halo[1][7][at:at + 1], 0.0)
            rims.append(rim_ref[6 * side + c] + rim_ref[6 * side + 3] * corner)
        for order, z in enumerate(EDGES):
            here = slice(16 * z, 16 * z + 16)
            total = once[z - 1] + once[z + 1] + x_sum(once[z])
            total = total + row_sum(once[z], rims[0][z:z + 1], rims[1][z:z + 1])
            result = KEEP * once[z] + scaled_ref[c, here, :] + coupling_ref[here, :] * total
            out_ref[c, 16 * order:16 * order + 16, :] = result
            at = 64 * c + 16 * order
            plain_ref[at:at + 16, :] = result.astype(BF16)

    picked = jnp.dot(edge_ref[...], plain_ref[...], preferred_element_type=F32)
    spread = spread_ref[...] + spread_of(picked, place_ref[:, 0:1])
    far = jnp.dot(right_ref[...], spread.astype(BF16), preferred_element_type=F32)
    ranks = 16
    lane = lax.broadcasted_iota(jnp.int32, (PLANE, 128), 1)
    parts = [jnp.zeros((PLANE, 128), F32) for _ in range(2)]
    for k in range(ranks):
        for z in range(planes):
            group = far[PLANE * (k * planes + z):PLANE * (k * planes + z + 1), :]
            at = z * ranks + k
            parts[at // 128] = jnp.where(lane == at % 128, group, parts[at // 128])
    down = lax.broadcasted_iota(jnp.int32, (128, 128), 0)
    across = lax.broadcasted_iota(jnp.int32, (128, 128), 1)
    traces = []
    for half in range(2):
        piece = jnp.where(down == across, spread[128 * half:128 * half + 128, :], 0.0)
        traces.append(jnp.sum(piece, axis=0, keepdims=True))
    tiles = send_ref.shape[0] // PLANE
    for to in range(PLANE):
        packet = stacked([parts[0][to:to + 1, :], parts[1][to:to + 1, :]] + traces, 4).astype(BF16)
        for tile in range(tiles):
            send_ref[seat(to, PLANE) * tiles + seat(tile, tiles)] = packet


def assemble(inner_ref, edges_ref, out_hbm, sems):
    copies = []
    for c in range(3):
        for source, target in ((edges_ref.at[c, 0:32], (0, 32)), (inner_ref.at[c], (32, 64)), (edges_ref.at[c, 32:64], (96, 32))):
            copies.append(pltpu.make_async_copy(source, out_hbm.at[c, pl.ds(*target), :], sems.at[len(copies)]))
    for copy in copies:
        copy.start()
    for copy in copies:
        copy.wait()


def middle(tiles, got_ref, send_ref):
    across = lax.rem(lax.axis_index("slab"), PLANE)
    tile = lax.axis_index("tile")
    total = jnp.sum(got_ref[...].astype(F32), axis=0)
    other = jnp.where(across == 0, PLANE - 1, 0)
    relay = []
    for b in range(3):
        wanted = tile + b - 1
        inside = (wanted >= 0) & (wanted < tiles)
        packet = got_ref[seated(other, PLANE) * tiles + seated(wanted, tiles)].astype(F32)
        packet = jnp.where(inside, packet, 0.0)
        relay += [packet[2:3, :], packet[3:4, :]]
    high = total.astype(BF16).astype(F32)
    low = total - high
    for half in range(2):
        packet = stacked([high[half:half + 1, :], low[half:half + 1, :]] + relay, 8).astype(BF16)
        for z in range(8 * half, min(8 * half + 8, send_ref.shape[0])):
            send_ref[seat(z, send_ref.shape[0])] = packet


def masked_rows(rows, factors):
    lines = [jnp.concatenate(row, axis=1) * factor.astype(F32) for row, factor in zip(rows, factors)]
    return stacked(lines, 16).astype(BF16)


def products(rows, blocks, count):
    every = lax.dot_general(rows, blocks, (((1,), (1,)), ((), ())), preferred_element_type=F32)
    result = every[0:1, 0:256]
    for k in range(1, count):
        result = result + every[k:k + 1, 256 * k:256 * k + 256]
    return result


def near_inside(tiles, mask_ref, got_ref, near_ref, out_ref):
    across = lax.rem(lax.axis_index("slab"), PLANE)
    tile = lax.axis_index("tile")
    rows = []
    for a in range(-1, 2):
        for b in range(-1, 2):
            up, beside = across + a, tile + b
            inside = (up >= 0) & (up < PLANE) & (beside >= 0) & (beside < tiles)
            packet = got_ref[seated(up, PLANE) * tiles + seated(beside, tiles)].astype(F32)
            packet = jnp.where(inside, packet, 0.0)
            rows.append((packet[2:3, :], packet[3:4, :]))
    out_ref[...] = products(masked_rows(rows, [mask_ref[0:1, q:q + 1] for q in range(9)]), near_ref[...], 9)


def finish(planes, mask_ref, rank_ref, part_ref, relay_ref, near_ref, left_ref, out_ref):
    slab = lax.axis_index("slab")
    across = lax.rem(slab, PLANE)
    plane = lax.div(slab, PLANE)
    upward = across == PLANE - 1
    start = jnp.where(upward, plane + 1, plane - 1)
    edge = ((across == 0) | upward) & (start >= 0) & (start < planes)
    packet = jnp.where(edge, relay_ref[seated(start, planes)].astype(F32), 0.0)
    rows = [(packet[2 + 2 * b:3 + 2 * b, :], packet[3 + 2 * b:4 + 2 * b, :]) for b in range(3)]
    first = jnp.where(upward, 6, 0)
    blocks = near_ref[pl.ds(pl.multiple_of(256 * first, 256), 768), :]
    factors = [jnp.where(upward, mask_ref[0:1, 6 + b:7 + b], mask_ref[0:1, b:b + 1]) for b in range(3)]
    near = products(masked_rows(rows, factors), blocks, 3)
    total = jnp.sum(relay_ref[...].astype(F32), axis=0)
    total = jnp.broadcast_to(total[0:1, :] + total[1:2, :], (8, 128))
    lane = lax.broadcasted_iota(jnp.int32, total.shape, 1)
    at = 16 * lax.rem(plane, 8)
    total = jnp.where((lane >= at) & (lane < at + rank_ref[...]), total, 0.0)
    high = total.astype(BF16).astype(F32)
    halves = jnp.concatenate([high, total - high], axis=0).astype(BF16)
    left = jnp.concatenate([left_ref[...]] * 8, axis=0)
    far = jnp.dot(halves, left, preferred_element_type=F32)
    out_ref[...] = part_ref[...] + near + far[0:1, :] + far[8:9, :]


def vmem():
    return pl.BlockSpec(memory_space=pltpu.VMEM)


def hbm():
    return pl.BlockSpec(memory_space=pltpu.HBM)


def exchange(one, two):
    slabs, tiles = lax.axis_size("slab"), lax.axis_size("tile")
    sent = []
    for value, sign in ((one, 1), (two, -1)):
        pairs = []
        for i in range(slabs):
            step = sign if i % 2 == 0 else -sign
            pairs += [(i * tiles + j, i * tiles + j + step) for j in range(tiles) if 0 <= j + step < tiles]
        sent.append(lax.ppermute(value, BOTH, pairs))
    return sent


def swap(far, pair, axis):
    devices = lax.axis_size(axis)
    far = lax.ppermute(far, axis, [(i, i + 1 if i % 2 else i - 1) for i in range(1, devices - 1)])
    return far, lax.ppermute(pair, axis, [(i, i ^ 1) for i in range(devices)])


def local(initial_field, source, material, stiffness_table, mass_table, trace_cells, near_blocks, near_mask, far_left, far_right,
          block_ranks):
    slabs, tiles = lax.axis_size("slab"), lax.axis_size("tile")
    planes = slabs // PLANE
    volume = jax.ShapeDtypeStruct((3, 128, 384), F32)
    face = jax.ShapeDtypeStruct((80, 384), BF16)
    params = pltpu.CompilerParams(vmem_limit_bytes=24 * 1024 * 1024)
    one, two = pl.pallas_call(
        y_faces,
        out_shape=(face, face),
        in_specs=[hbm()] * 3,
        out_specs=(vmem(), vmem()),
        scratch_shapes=[
            pltpu.VMEM((4, 3, 8, 384), F32), pltpu.VMEM((2, 3, 8, 384), F32), pltpu.VMEM((2, 8, 384), jnp.int32),
            pltpu.SemaphoreType.DMA((8,)),
        ],
        compiler_params=pltpu.CompilerParams(vmem_limit_bytes=55050 * 1024),
    )(initial_field, source, material)
    tables = (stiffness_table.reshape(1, 8), mass_table.reshape(1, 8))
    field = initial_field.reshape(3, 128, 384)
    sources = source.reshape(3, 128, 384)
    cells = material.reshape(128, 384)
    one, two = exchange(one, two)
    index = jax.ShapeDtypeStruct((256, 192), BF16)
    column = jax.ShapeDtypeStruct((256, 128), F32)
    base, scaled, coupling, edge, chosen, place = pl.pallas_call(
        no_halo,
        out_shape=(volume, volume, jax.ShapeDtypeStruct((128, 384), F32), index, index, column),
        in_specs=[vmem()] * 6,
        out_specs=(vmem(),) * 6,
        compiler_params=params,
        cost_estimate=pl.CostEstimate(flops=6_000_000, bytes_accessed=3_000_000, transcendentals=0),
    )(*tables, field, sources, cells, trace_cells.reshape(1, 256))
    face = jax.ShapeDtypeStruct((128, 384), BF16)
    far, pair = pl.pallas_call(
        z_faces,
        out_shape=(face, face),
        in_specs=[vmem()] * 5,
        out_specs=(vmem(), vmem()),
        compiler_params=params,
    )(field, base, coupling, one, two)
    far, pair = swap(far, pair, "slab")
    members = PLANE * tiles
    once, rim, inner, spread = pl.pallas_call(
        relax_inner,
        out_shape=(volume, jax.ShapeDtypeStruct((12, 8, 384), F32), jax.ShapeDtypeStruct((3, 64, 384), F32), column),
        in_specs=[vmem()] * 10,
        out_specs=(vmem(),) * 4,
        scratch_shapes=[pltpu.VMEM((192, 384), BF16)],
        compiler_params=params,
        cost_estimate=pl.CostEstimate(flops=4_000_000, bytes_accessed=3_000_000, transcendentals=0),
    )(*tables, field, base, scaled, coupling, one, two, chosen, place)
    edges, send = pl.pallas_call(
        functools.partial(relax_edges, planes),
        out_shape=(jax.ShapeDtypeStruct((3, 64, 384), F32), jax.ShapeDtypeStruct((members, 4, 128), BF16)),
        in_specs=[vmem()] * 11,
        out_specs=(vmem(), vmem()),
        scratch_shapes=[pltpu.VMEM((192, 384), BF16)],
        compiler_params=params,
    )(field, once, scaled, coupling, rim, edge, place, spread, far, pair, far_right.reshape(-1, 256))
    ids = np.arange(slabs * tiles).reshape(planes, PLANE, tiles)
    ids = np.roll(ids, (-(planes // 2), -(PLANE // 2), -(tiles // 2)), axis=(0, 1, 2)).reshape(planes, members)
    got = lax.all_to_all(send, BOTH, 0, 0, axis_index_groups=ids.tolist(), tiled=True)
    send = pl.pallas_call(
        functools.partial(middle, tiles),
        out_shape=jax.ShapeDtypeStruct((planes, 8, 128), BF16),
        in_specs=[vmem()],
        out_specs=vmem(),
        compiler_params=params,
    )(got)
    relay = lax.all_to_all(send, BOTH, 0, 0, axis_index_groups=ids.T.tolist(), tiled=True)
    result = pl.pallas_call(
        assemble,
        out_shape=volume,
        in_specs=[vmem(), vmem()],
        out_specs=hbm(),
        scratch_shapes=[pltpu.SemaphoreType.DMA((9,))],
        compiler_params=params,
        cost_estimate=pl.CostEstimate(flops=0, bytes_accessed=600_000, transcendentals=0),
    )(inner, edges)
    mask = near_mask.reshape(1, 9)
    blocks = near_blocks.reshape(-1, 256)
    part = pl.pallas_call(
        functools.partial(near_inside, tiles),
        out_shape=jax.ShapeDtypeStruct((1, 256), F32),
        in_specs=[vmem()] * 3,
        out_specs=vmem(),
        compiler_params=params,
        cost_estimate=pl.CostEstimate(flops=2 * 16 * 2304 * 256, bytes_accessed=2304 * 512, transcendentals=0),
    )(mask, got, blocks)
    boundary = pl.pallas_call(
        functools.partial(finish, planes),
        out_shape=jax.ShapeDtypeStruct((1, 256), F32),
        in_specs=[vmem()] * 6,
        out_specs=vmem(),
        compiler_params=params,
    )(mask, block_ranks.reshape(1, 1), part, relay, blocks, far_left.reshape(16, 256))
    return result.reshape(initial_field.shape), boundary.reshape(1, 1, 256)


def solution(mesh):
    placed = (
        P(None, "slab", "tile", None),
        P(None, "slab", "tile", None),
        P("slab", "tile", None),
        P(),
        P(),
        P("slab", "tile", None),
        P("slab", "tile", None, None, None),
        P("slab", "tile", None),
        P(None, "slab", "tile", None),
        P(None, None, "slab", "tile", None),
        P("slab"),
    )
    return jax.shard_map(
        local,
        mesh=mesh,
        in_specs=placed,
        out_specs=(P(None, "slab", "tile", None), P("slab", "tile", None)),
        check_vma=False,
    )
```

```python
import functools

import jax
import jax.numpy as jnp
import numpy as np
from jax import lax
from jax.experimental import pallas as pl
from jax.experimental.pallas import tpu as pltpu
from jax.sharding import PartitionSpec as P

RELAX = 0.8
KEEP = 1.0 - RELAX
PLANE = 8
F32 = jnp.float32
BF16 = jnp.bfloat16
BOTH = ("slab", "tile")


def seat(member, count):
    return (member + count - count // 2) % count


def seated(member, count):
    return lax.rem(jnp.clip(member, 0, count - 1) + count - count // 2, count)


def table_rows(stiff_ref, mass_ref, width):
    stiffness = stiff_ref[...]
    weight = RELAX / (6.0 * stiffness + mass_ref[...])
    rows = []
    for table in (weight, stiffness * weight):
        rows += [jnp.broadcast_to(table[:, entry:entry + 1], (1, width)) for entry in range(8)]
    return rows


def lookup(material, rows):
    weight = jnp.broadcast_to(rows[0], material.shape)
    coupling = jnp.broadcast_to(rows[8], material.shape)
    for entry in range(1, 8):
        here = material == entry
        weight = jnp.where(here, rows[entry], weight)
        coupling = jnp.where(here, rows[8 + entry], coupling)
    return weight, coupling


def x_sum(value):
    width = value.shape[-1]
    lane = lax.broadcasted_iota(jnp.int32, value.shape, value.ndim - 1)
    before = jnp.where(lane == 0, 0.0, pltpu.roll(value, 1, value.ndim - 1))
    after = jnp.where(lane == width - 1, 0.0, pltpu.roll(value, width - 1, value.ndim - 1))
    return before + after


def row_sum(value, first, last):
    length = value.shape[0]
    row = lax.broadcasted_iota(jnp.int32, value.shape, 0)
    before = jnp.where(row == 0, first, pltpu.roll(value, 1, 0))
    after = jnp.where(row == length - 1, last, pltpu.roll(value, length - 1, 0))
    return before + after


def line_rows(ref, y, *lead):
    lines = [ref[(*lead, slice(16 * z + y, 16 * z + y + 1), slice(None))] for z in range(8)]
    row = lax.broadcasted_iota(jnp.int32, (8, lines[0].shape[1]), 0)
    value = jnp.broadcast_to(lines[0], row.shape)
    for z in range(1, 8):
        value = jnp.where(row == z, lines[z], value)
    return value


def y_faces(field_hbm, source_hbm, material_hbm, first_ref, last_ref, field_ref, source_ref, material_ref, sems):
    pairs = [(field_hbm.at[:, :, y, :], field_ref.at[k]) for k, y in enumerate((0, 15, 1, 14))]
    pairs += [(source_hbm.at[:, :, y, :], source_ref.at[k]) for k, y in enumerate((0, 15))]
    pairs += [(material_hbm.at[:, y, :], material_ref.at[k]) for k, y in enumerate((0, 15))]
    copies = [pltpu.make_async_copy(src, dst, sems.at[k]) for k, (src, dst) in enumerate(pairs)]
    for copy in copies:
        copy.start()
    for copy in copies:
        copy.wait()
    for k, out_ref in enumerate((first_ref, last_ref)):
        values = [field_ref[k, c] for c in range(3)]
        totals = [field_ref[2 + k, c] + row_sum(values[c], 0.0, 0.0) + x_sum(values[c]) for c in range(3)]
        planes = values + [source_ref[k, c] for c in range(3)] + totals + [1.0 + material_ref[k].astype(F32)]
        for pair in range(5):
            both = jnp.concatenate(planes[2 * pair:2 * pair + 2], axis=0)
            out_ref[16 * pair:16 * pair + 16, :] = both.astype(BF16)


def rim_rows(first, last):
    row = lax.broadcasted_iota(jnp.int32, (16, first.shape[1]), 0)
    return jnp.where(row == 0, first, jnp.where(row == 15, last, 0.0))


def z_faces(field_ref, base_ref, coupling_ref, before_ref, after_ref, far_ref, pair_ref):
    even = lax.rem(lax.axis_index("slab"), 2) == 0
    before = bands(before_ref, 2)
    after = bands(after_ref, 2)
    faces = []
    for z in (0, 7):
        here = slice(16 * z, 16 * z + 16)
        coupling = coupling_ref[here, :]
        lines, values, partials = [], [], []
        for c in range(3):
            at = 8 * (c % 2) + z
            lines += [before[c // 2][at:at + 1, :], after[c // 2][at:at + 1, :]]
            values.append(field_ref[c, here, :])
            partials.append(base_ref[c, here, :] + coupling * rim_rows(lines[2 * c], lines[2 * c + 1]))
        faces.append(values + partials + [coupling, stacked(lines, 16)])
    for k, (first, last) in enumerate(zip(*faces)):
        here = slice(16 * k, 16 * k + 16)
        far_ref[here, :] = jnp.where(even, first, last).astype(BF16)
        pair_ref[here, :] = jnp.where(even, last, first).astype(BF16)


def stacked(lines, height):
    row = lax.broadcasted_iota(jnp.int32, (height, lines[0].shape[1]), 0)
    value = jnp.zeros(row.shape, F32)
    for k in range(len(lines)):
        value = jnp.where(row == k, lines[k], value)
    return value


def column_of(row):
    length = row.shape[1]
    down = lax.broadcasted_iota(jnp.int32, (length, length), 0)
    along = lax.broadcasted_iota(jnp.int32, (length, length), 1)
    return jnp.sum(jnp.where(down == along, row, 0.0), axis=1, keepdims=True)


def bands(ref, count):
    return [ref[16 * k:16 * k + 16, :].astype(F32) for k in range(count)]


EDGES = (0, 1, 6, 7)


def no_halo(stiff_ref, mass_ref, field_ref, source_ref, material_ref, cells_ref,
            base_ref, scaled_ref, coupling_ref, edge_ref, chosen_ref, place_ref):
    rows = table_rows(stiff_ref, mass_ref, field_ref.shape[-1])
    for z in range(8):
        here = slice(16 * z, 16 * z + 16)
        weight, coupling = lookup(material_ref[here, :], rows)
        coupling_ref[here, :] = coupling
        for c in range(3):
            value = field_ref[c, here, :]
            total = row_sum(value, 0.0, 0.0) + x_sum(value)
            if z > 0:
                total = total + field_ref[c, 16 * z - 16:16 * z, :]
            if z < 7:
                total = total + field_ref[c, 16 * z + 16:16 * z + 32, :]
            scaled = weight * source_ref[c, here, :]
            scaled_ref[c, here, :] = scaled
            base_ref[c, here, :] = KEEP * value + scaled + coupling * total

    width = field_ref.shape[-1]
    count = cells_ref.shape[1]
    cells = cells_ref[...].astype(F32)
    line = jnp.floor((cells + 0.5) * (1.0 / width))
    place_ref[...] = jnp.broadcast_to(column_of(cells - width * line), (count, 128))
    line_column = column_of(line)
    along = lax.broadcasted_iota(jnp.int32, (count, 192), 1).astype(F32)
    part = jnp.floor(along * (1.0 / 64) + 0.001)
    shift = along - 64.0 * part
    inner = 128.0 * part + shift + 32.0
    outer = 128.0 * part + jnp.where(shift < 32.0, shift, shift + 64.0)
    edge_ref[...] = jnp.where(outer == line_column, 1.0, 0.0).astype(BF16)
    chosen_ref[...] = jnp.where(inner == line_column, 1.0, 0.0).astype(BF16)


def relax_inner(stiff_ref, mass_ref, field_ref, base_ref, scaled_ref, coupling_ref, before_ref, after_ref, chosen_ref, place_ref,
                once_ref, rim_ref, out_ref, spread_ref, plain_ref):
    rows = table_rows(stiff_ref, mass_ref, field_ref.shape[-1])
    lines = []
    for side, (ref, y) in enumerate(((before_ref, 0), (after_ref, 15))):
        halo = bands(ref, 5)
        planes = [halo[k // 2][8 * (k % 2):8 * (k % 2) + 8] for k in range(10)]
        weight, coupling = lookup(planes[9] - 1.0, rows)
        coupling = jnp.where(planes[9] > 0.0, coupling, 0.0)
        rim_ref[6 * side + 3] = coupling
        for c in range(3):
            total = planes[6 + c] + line_rows(field_ref, y, c)
            rim_ref[6 * side + c] = KEEP * planes[c] + weight * planes[3 + c] + coupling * total
        lines.append(planes[:3])
    for z in range(8):
        here = slice(16 * z, 16 * z + 16)
        for c in range(3):
            halo = rim_rows(lines[0][c][z:z + 1], lines[1][c][z:z + 1])
            once_ref[c, here, :] = base_ref[c, here, :] + coupling_ref[here, :] * halo
    for z in range(2, 6):
        here = slice(16 * z, 16 * z + 16)
        for c in range(3):
            value = once_ref[c, here, :]
            total = once_ref[c, 16 * z - 16:16 * z, :] + once_ref[c, 16 * z + 16:16 * z + 32, :] + x_sum(value)
            total = total + row_sum(value, rim_ref[c, z:z + 1, :], rim_ref[6 + c, z:z + 1, :])
            result = KEEP * value + scaled_ref[c, here, :] + coupling_ref[here, :] * total
            out_ref[c, 16 * z - 32:16 * z - 16, :] = result
            at = 64 * c + 16 * z - 32
            plain_ref[at:at + 16, :] = result.astype(BF16)
    picked = jnp.dot(chosen_ref[...], plain_ref[...], preferred_element_type=F32)
    spread_ref[...] = spread_of(picked, place_ref[:, 0:1])


def spread_of(picked, place_column):
    along = lax.broadcasted_iota(jnp.int32, picked.shape, 1).astype(F32)
    single = jnp.where(along == place_column, picked, 0.0).astype(BF16)
    return jnp.dot(single, jnp.ones((picked.shape[1], 128), BF16), preferred_element_type=F32)


def relax_edges(planes, field_ref, once_ref, scaled_ref, coupling_ref, rim_ref, edge_ref, place_ref, spread_ref,
                far_ref, pair_ref, right_ref, out_ref, send_ref, plain_ref):
    even = lax.rem(lax.axis_index("slab"), 2) == 0
    both = list(zip(bands(far_ref, 8), bands(pair_ref, 8)))
    halo = [[jnp.where(even, far, pair) for far, pair in both], [jnp.where(even, pair, far) for far, pair in both]]
    row8 = lax.broadcasted_iota(jnp.int32, (8, field_ref.shape[-1]), 0)
    for c in range(3):
        once = {z: once_ref[c, 16 * z:16 * z + 16, :] for z in (1, 2, 5, 6)}
        once[0] = once_ref[c, 0:16, :] + coupling_ref[0:16, :] * halo[0][c]
        once[7] = once_ref[c, 112:128, :] + coupling_ref[112:128, :] * halo[1][c]
        once[-1] = halo[0][3 + c] + halo[0][6] * field_ref[c, 0:16, :]
        once[8] = halo[1][3 + c] + halo[1][6] * field_ref[c, 112:128, :]
        rims = []
        for side in range(2):
            at = 2 * c + side
            corner = jnp.where(row8 == 0, halo[0][7][at:at + 1], 0.0) + jnp.where(row8 == 7, halo[1][7][at:at + 1], 0.0)
            rims.append(rim_ref[6 * side + c] + rim_ref[6 * side + 3] * corner)
        for order, z in enumerate(EDGES):
            here = slice(16 * z, 16 * z + 16)
            total = once[z - 1] + once[z + 1] + x_sum(once[z])
            total = total + row_sum(once[z], rims[0][z:z + 1], rims[1][z:z + 1])
            result = KEEP * once[z] + scaled_ref[c, here, :] + coupling_ref[here, :] * total
            out_ref[c, 16 * order:16 * order + 16, :] = result
            at = 64 * c + 16 * order
            plain_ref[at:at + 16, :] = result.astype(BF16)

    picked = jnp.dot(edge_ref[...], plain_ref[...], preferred_element_type=F32)
    spread = spread_ref[...] + spread_of(picked, place_ref[:, 0:1])
    far = jnp.dot(right_ref[...], spread.astype(BF16), preferred_element_type=F32)
    ranks = 16
    lane = lax.broadcasted_iota(jnp.int32, (PLANE, 128), 1)
    parts = [jnp.zeros((PLANE, 128), F32) for _ in range(2)]
    for k in range(ranks):
        for z in range(planes):
            group = far[PLANE * (k * planes + z):PLANE * (k * planes + z + 1), :]
            at = z * ranks + k
            parts[at // 128] = jnp.where(lane == at % 128, group, parts[at // 128])
    down = lax.broadcasted_iota(jnp.int32, (128, 128), 0)
    across = lax.broadcasted_iota(jnp.int32, (128, 128), 1)
    traces = []
    for half in range(2):
        piece = jnp.where(down == across, spread[128 * half:128 * half + 128, :], 0.0)
        traces.append(jnp.sum(piece, axis=0, keepdims=True))
    tiles = send_ref.shape[0] // PLANE
    for to in range(PLANE):
        packet = stacked([parts[0][to:to + 1, :], parts[1][to:to + 1, :]] + traces, 4).astype(BF16)
        for tile in range(tiles):
            send_ref[to * tiles + seat(tile, tiles)] = packet


def assemble(inner_ref, edges_ref, out_hbm, sems):
    copies = []
    for c in range(3):
        for source, target in ((edges_ref.at[c, 0:32], (0, 32)), (inner_ref.at[c], (32, 64)), (edges_ref.at[c, 32:64], (96, 32))):
            copies.append(pltpu.make_async_copy(source, out_hbm.at[c, pl.ds(*target), :], sems.at[len(copies)]))
    for copy in copies:
        copy.start()
    for copy in copies:
        copy.wait()


def middle(tiles, got_ref, send_ref):
    across = lax.rem(lax.axis_index("slab"), PLANE)
    tile = lax.axis_index("tile")
    total = jnp.sum(got_ref[...].astype(F32), axis=0)
    other = jnp.where(across == 0, PLANE - 1, 0)
    relay = []
    for b in range(3):
        wanted = tile + b - 1
        inside = (wanted >= 0) & (wanted < tiles)
        packet = got_ref[other * tiles + seated(wanted, tiles)].astype(F32)
        packet = jnp.where(inside, packet, 0.0)
        relay += [packet[2:3, :], packet[3:4, :]]
    high = total.astype(BF16).astype(F32)
    low = total - high
    for half in range(2):
        packet = stacked([high[half:half + 1, :], low[half:half + 1, :]] + relay, 8).astype(BF16)
        for z in range(8 * half, min(8 * half + 8, send_ref.shape[0])):
            send_ref[seat(z, send_ref.shape[0])] = packet


def masked_rows(rows, factors):
    lines = [jnp.concatenate(row, axis=1) * factor.astype(F32) for row, factor in zip(rows, factors)]
    return stacked(lines, 16).astype(BF16)


def products(rows, blocks, count):
    every = lax.dot_general(rows, blocks, (((1,), (1,)), ((), ())), preferred_element_type=F32)
    result = every[0:1, 0:256]
    for k in range(1, count):
        result = result + every[k:k + 1, 256 * k:256 * k + 256]
    return result


def near_inside(tiles, mask_ref, got_ref, near_ref, out_ref):
    across = lax.rem(lax.axis_index("slab"), PLANE)
    tile = lax.axis_index("tile")
    rows = []
    for a in range(-1, 2):
        for b in range(-1, 2):
            up, beside = across + a, tile + b
            inside = (up >= 0) & (up < PLANE) & (beside >= 0) & (beside < tiles)
            packet = got_ref[jnp.clip(up, 0, PLANE - 1) * tiles + seated(beside, tiles)].astype(F32)
            packet = jnp.where(inside, packet, 0.0)
            rows.append((packet[2:3, :], packet[3:4, :]))
    out_ref[...] = products(masked_rows(rows, [mask_ref[0:1, q:q + 1] for q in range(9)]), near_ref[...], 9)


def finish(planes, mask_ref, rank_ref, part_ref, relay_ref, near_ref, left_ref, out_ref):
    slab = lax.axis_index("slab")
    across = lax.rem(slab, PLANE)
    plane = lax.div(slab, PLANE)
    upward = across == PLANE - 1
    start = jnp.where(upward, plane + 1, plane - 1)
    edge = ((across == 0) | upward) & (start >= 0) & (start < planes)
    packet = jnp.where(edge, relay_ref[seated(start, planes)].astype(F32), 0.0)
    rows = [(packet[2 + 2 * b:3 + 2 * b, :], packet[3 + 2 * b:4 + 2 * b, :]) for b in range(3)]
    first = jnp.where(upward, 6, 0)
    blocks = near_ref[pl.ds(pl.multiple_of(256 * first, 256), 768), :]
    factors = [jnp.where(upward, mask_ref[0:1, 6 + b:7 + b], mask_ref[0:1, b:b + 1]) for b in range(3)]
    near = products(masked_rows(rows, factors), blocks, 3)
    total = jnp.sum(relay_ref[...].astype(F32), axis=0)
    total = jnp.broadcast_to(total[0:1, :] + total[1:2, :], (8, 128))
    lane = lax.broadcasted_iota(jnp.int32, total.shape, 1)
    at = 16 * lax.rem(plane, 8)
    total = jnp.where((lane >= at) & (lane < at + rank_ref[...]), total, 0.0)
    high = total.astype(BF16).astype(F32)
    halves = jnp.concatenate([high, total - high], axis=0).astype(BF16)
    left = jnp.concatenate([left_ref[...]] * 8, axis=0)
    far = jnp.dot(halves, left, preferred_element_type=F32)
    out_ref[...] = part_ref[...] + near + far[0:1, :] + far[8:9, :]


def vmem():
    return pl.BlockSpec(memory_space=pltpu.VMEM)


def hbm():
    return pl.BlockSpec(memory_space=pltpu.HBM)


def exchange(first, last, axis):
    devices = lax.axis_size(axis)
    up = [(i, i + 1) for i in range(devices - 1)]
    down = [(j, i) for i, j in up]
    return lax.ppermute(last, axis, up), lax.ppermute(first, axis, down)


def swap(far, pair, axis):
    devices = lax.axis_size(axis)
    far = lax.ppermute(far, axis, [(i, i + 1 if i % 2 else i - 1) for i in range(1, devices - 1)])
    return far, lax.ppermute(pair, axis, [(i, i ^ 1) for i in range(devices)])


def local(initial_field, source, material, stiffness_table, mass_table, trace_cells, near_blocks, near_mask, far_left, far_right,
          block_ranks):
    slabs, tiles = lax.axis_size("slab"), lax.axis_size("tile")
    planes = slabs // PLANE
    volume = jax.ShapeDtypeStruct((3, 128, 384), F32)
    face = jax.ShapeDtypeStruct((80, 384), BF16)
    params = pltpu.CompilerParams(vmem_limit_bytes=24 * 1024 * 1024)
    first, last = pl.pallas_call(
        y_faces,
        out_shape=(face, face),
        in_specs=[hbm()] * 3,
        out_specs=(vmem(), vmem()),
        scratch_shapes=[
            pltpu.VMEM((4, 3, 8, 384), F32), pltpu.VMEM((2, 3, 8, 384), F32), pltpu.VMEM((2, 8, 384), jnp.int32),
            pltpu.SemaphoreType.DMA((8,)),
        ],
        compiler_params=pltpu.CompilerParams(vmem_limit_bytes=55050 * 1024),
    )(initial_field, source, material)
    tables = (stiffness_table.reshape(1, 8), mass_table.reshape(1, 8))
    field = initial_field.reshape(3, 128, 384)
    sources = source.reshape(3, 128, 384)
    cells = material.reshape(128, 384)
    before, after = exchange(first, last, "tile")
    index = jax.ShapeDtypeStruct((256, 192), BF16)
    column = jax.ShapeDtypeStruct((256, 128), F32)
    base, scaled, coupling, edge, chosen, place = pl.pallas_call(
        no_halo,
        out_shape=(volume, volume, jax.ShapeDtypeStruct((128, 384), F32), index, index, column),
        in_specs=[vmem()] * 6,
        out_specs=(vmem(),) * 6,
        compiler_params=params,
        cost_estimate=pl.CostEstimate(flops=6_000_000, bytes_accessed=3_000_000, transcendentals=0),
    )(*tables, field, sources, cells, trace_cells.reshape(1, 256))
    face = jax.ShapeDtypeStruct((128, 384), BF16)
    far, pair = pl.pallas_call(
        z_faces,
        out_shape=(face, face),
        in_specs=[vmem()] * 5,
        out_specs=(vmem(), vmem()),
        compiler_params=params,
    )(field, base, coupling, before, after)
    far, pair = swap(far, pair, "slab")
    members = PLANE * tiles
    once, rim, inner, spread = pl.pallas_call(
        relax_inner,
        out_shape=(volume, jax.ShapeDtypeStruct((12, 8, 384), F32), jax.ShapeDtypeStruct((3, 64, 384), F32), column),
        in_specs=[vmem()] * 10,
        out_specs=(vmem(),) * 4,
        scratch_shapes=[pltpu.VMEM((192, 384), BF16)],
        compiler_params=params,
        cost_estimate=pl.CostEstimate(flops=4_000_000, bytes_accessed=3_000_000, transcendentals=0),
    )(*tables, field, base, scaled, coupling, before, after, chosen, place)
    edges, send = pl.pallas_call(
        functools.partial(relax_edges, planes),
        out_shape=(jax.ShapeDtypeStruct((3, 64, 384), F32), jax.ShapeDtypeStruct((members, 4, 128), BF16)),
        in_specs=[vmem()] * 11,
        out_specs=(vmem(), vmem()),
        scratch_shapes=[pltpu.VMEM((192, 384), BF16)],
        compiler_params=params,
    )(field, once, scaled, coupling, rim, edge, place, spread, far, pair, far_right.reshape(-1, 256))
    ids = np.arange(slabs * tiles).reshape(planes, PLANE, tiles)
    ids = np.roll(ids, (-(planes // 2), -(tiles // 2)), axis=(0, 2)).reshape(planes, members)
    got = lax.all_to_all(send, BOTH, 0, 0, axis_index_groups=ids.tolist(), tiled=True)
    send = pl.pallas_call(
        functools.partial(middle, tiles),
        out_shape=jax.ShapeDtypeStruct((planes, 8, 128), BF16),
        in_specs=[vmem()],
        out_specs=vmem(),
        compiler_params=params,
    )(got)
    relay = lax.all_to_all(send, BOTH, 0, 0, axis_index_groups=ids.T.tolist(), tiled=True)
    result = pl.pallas_call(
        assemble,
        out_shape=volume,
        in_specs=[vmem(), vmem()],
        out_specs=hbm(),
        scratch_shapes=[pltpu.SemaphoreType.DMA((9,))],
        compiler_params=params,
        cost_estimate=pl.CostEstimate(flops=0, bytes_accessed=600_000, transcendentals=0),
    )(inner, edges)
    mask = near_mask.reshape(1, 9)
    blocks = near_blocks.reshape(-1, 256)
    part = pl.pallas_call(
        functools.partial(near_inside, tiles),
        out_shape=jax.ShapeDtypeStruct((1, 256), F32),
        in_specs=[vmem()] * 3,
        out_specs=vmem(),
        compiler_params=params,
        cost_estimate=pl.CostEstimate(flops=2 * 16 * 2304 * 256, bytes_accessed=2304 * 512, transcendentals=0),
    )(mask, got, blocks)
    boundary = pl.pallas_call(
        functools.partial(finish, planes),
        out_shape=jax.ShapeDtypeStruct((1, 256), F32),
        in_specs=[vmem()] * 6,
        out_specs=vmem(),
        compiler_params=params,
    )(mask, block_ranks.reshape(1, 1), part, relay, blocks, far_left.reshape(16, 256))
    return result.reshape(initial_field.shape), boundary.reshape(1, 1, 256)


def solution(mesh):
    placed = (
        P(None, "slab", "tile", None),
        P(None, "slab", "tile", None),
        P("slab", "tile", None),
        P(),
        P(),
        P("slab", "tile", None),
        P("slab", "tile", None, None, None),
        P("slab", "tile", None),
        P(None, "slab", "tile", None),
        P(None, None, "slab", "tile", None),
        P("slab"),
    )
    return jax.shard_map(
        local,
        mesh=mesh,
        in_specs=placed,
        out_specs=(P(None, "slab", "tile", None), P("slab", "tile", None)),
        check_vma=False,
    )
```

```python
import functools

import jax
import jax.numpy as jnp
import numpy as np
from jax import lax
from jax.experimental import pallas as pl
from jax.experimental.pallas import tpu as pltpu
from jax.sharding import PartitionSpec as P

RELAX = 0.8
KEEP = 1.0 - RELAX
PLANE = 8
F32 = jnp.float32
BF16 = jnp.bfloat16
BOTH = ("slab", "tile")


def seat(member, count):
    return (member + count - count // 2) % count


def seated(member, count):
    return lax.rem(jnp.clip(member, 0, count - 1) + count - count // 2, count)


def table_rows(stiff_ref, mass_ref, width):
    stiffness = stiff_ref[...]
    weight = RELAX / (6.0 * stiffness + mass_ref[...])
    rows = []
    for table in (weight, stiffness * weight):
        rows += [jnp.broadcast_to(table[:, entry:entry + 1], (1, width)) for entry in range(8)]
    return rows


def lookup(material, rows):
    weight = jnp.broadcast_to(rows[0], material.shape)
    coupling = jnp.broadcast_to(rows[8], material.shape)
    for entry in range(1, 8):
        here = material == entry
        weight = jnp.where(here, rows[entry], weight)
        coupling = jnp.where(here, rows[8 + entry], coupling)
    return weight, coupling


def x_sum(value):
    width = value.shape[-1]
    lane = lax.broadcasted_iota(jnp.int32, value.shape, value.ndim - 1)
    before = jnp.where(lane == 0, 0.0, pltpu.roll(value, 1, value.ndim - 1))
    after = jnp.where(lane == width - 1, 0.0, pltpu.roll(value, width - 1, value.ndim - 1))
    return before + after


def row_sum(value, first, last):
    length = value.shape[0]
    row = lax.broadcasted_iota(jnp.int32, value.shape, 0)
    before = jnp.where(row == 0, first, pltpu.roll(value, 1, 0))
    after = jnp.where(row == length - 1, last, pltpu.roll(value, length - 1, 0))
    return before + after


def line_rows(ref, y, *lead):
    lines = [ref[(*lead, slice(16 * z + y, 16 * z + y + 1), slice(None))] for z in range(8)]
    row = lax.broadcasted_iota(jnp.int32, (8, lines[0].shape[1]), 0)
    value = jnp.broadcast_to(lines[0], row.shape)
    for z in range(1, 8):
        value = jnp.where(row == z, lines[z], value)
    return value


def y_faces(field_hbm, source_hbm, material_hbm, first_ref, last_ref, field_ref, source_ref, material_ref, sems):
    pairs = [(field_hbm.at[:, :, y, :], field_ref.at[k]) for k, y in enumerate((0, 15, 1, 14))]
    pairs += [(source_hbm.at[:, :, y, :], source_ref.at[k]) for k, y in enumerate((0, 15))]
    pairs += [(material_hbm.at[:, y, :], material_ref.at[k]) for k, y in enumerate((0, 15))]
    copies = [pltpu.make_async_copy(src, dst, sems.at[k]) for k, (src, dst) in enumerate(pairs)]
    for copy in copies:
        copy.start()
    for copy in copies:
        copy.wait()
    for k, out_ref in enumerate((first_ref, last_ref)):
        values = [field_ref[k, c] for c in range(3)]
        totals = [field_ref[2 + k, c] + row_sum(values[c], 0.0, 0.0) + x_sum(values[c]) for c in range(3)]
        planes = values + [source_ref[k, c] for c in range(3)] + totals + [1.0 + material_ref[k].astype(F32)]
        for pair in range(5):
            both = jnp.concatenate(planes[2 * pair:2 * pair + 2], axis=0)
            out_ref[16 * pair:16 * pair + 16, :] = both.astype(BF16)


def rim_rows(first, last):
    row = lax.broadcasted_iota(jnp.int32, (16, first.shape[1]), 0)
    return jnp.where(row == 0, first, jnp.where(row == 15, last, 0.0))


def z_faces(field_ref, base_ref, coupling_ref, before_ref, after_ref, far_ref, pair_ref):
    even = lax.rem(lax.axis_index("slab"), 2) == 0
    before = bands(before_ref, 2)
    after = bands(after_ref, 2)
    faces = []
    for z in (0, 7):
        here = slice(16 * z, 16 * z + 16)
        coupling = coupling_ref[here, :]
        lines, values, partials = [], [], []
        for c in range(3):
            at = 8 * (c % 2) + z
            lines += [before[c // 2][at:at + 1, :], after[c // 2][at:at + 1, :]]
            values.append(field_ref[c, here, :])
            partials.append(base_ref[c, here, :] + coupling * rim_rows(lines[2 * c], lines[2 * c + 1]))
        faces.append(values + partials + [coupling, stacked(lines, 16)])
    for k, (first, last) in enumerate(zip(*faces)):
        here = slice(16 * k, 16 * k + 16)
        far_ref[here, :] = jnp.where(even, first, last).astype(BF16)
        pair_ref[here, :] = jnp.where(even, last, first).astype(BF16)


def stacked(lines, height):
    row = lax.broadcasted_iota(jnp.int32, (height, lines[0].shape[1]), 0)
    value = jnp.zeros(row.shape, F32)
    for k in range(len(lines)):
        value = jnp.where(row == k, lines[k], value)
    return value


def column_of(row):
    length = row.shape[1]
    down = lax.broadcasted_iota(jnp.int32, (length, length), 0)
    along = lax.broadcasted_iota(jnp.int32, (length, length), 1)
    return jnp.sum(jnp.where(down == along, row, 0.0), axis=1, keepdims=True)


def bands(ref, count):
    return [ref[16 * k:16 * k + 16, :].astype(F32) for k in range(count)]


EDGES = (0, 1, 6, 7)


def no_halo(stiff_ref, mass_ref, field_ref, source_ref, material_ref, cells_ref,
            base_ref, scaled_ref, coupling_ref, edge_ref, chosen_ref, place_ref):
    rows = table_rows(stiff_ref, mass_ref, field_ref.shape[-1])
    for z in range(8):
        here = slice(16 * z, 16 * z + 16)
        weight, coupling = lookup(material_ref[here, :], rows)
        coupling_ref[here, :] = coupling
        for c in range(3):
            value = field_ref[c, here, :]
            total = row_sum(value, 0.0, 0.0) + x_sum(value)
            if z > 0:
                total = total + field_ref[c, 16 * z - 16:16 * z, :]
            if z < 7:
                total = total + field_ref[c, 16 * z + 16:16 * z + 32, :]
            scaled = weight * source_ref[c, here, :]
            scaled_ref[c, here, :] = scaled
            base_ref[c, here, :] = KEEP * value + scaled + coupling * total

    width = field_ref.shape[-1]
    count = cells_ref.shape[1]
    cells = cells_ref[...].astype(F32)
    line = jnp.floor((cells + 0.5) * (1.0 / width))
    place_ref[...] = jnp.broadcast_to(column_of(cells - width * line), (count, 128))
    line_column = column_of(line)
    along = lax.broadcasted_iota(jnp.int32, (count, 192), 1).astype(F32)
    part = jnp.floor(along * (1.0 / 64) + 0.001)
    shift = along - 64.0 * part
    inner = 128.0 * part + shift + 32.0
    outer = 128.0 * part + jnp.where(shift < 32.0, shift, shift + 64.0)
    edge_ref[...] = jnp.where(outer == line_column, 1.0, 0.0).astype(BF16)
    chosen_ref[...] = jnp.where(inner == line_column, 1.0, 0.0).astype(BF16)


def relax_inner(stiff_ref, mass_ref, field_ref, base_ref, scaled_ref, coupling_ref, before_ref, after_ref, chosen_ref, place_ref,
                once_ref, rim_ref, out_ref, spread_ref, plain_ref):
    rows = table_rows(stiff_ref, mass_ref, field_ref.shape[-1])
    lines = []
    for side, (ref, y) in enumerate(((before_ref, 0), (after_ref, 15))):
        halo = bands(ref, 5)
        planes = [halo[k // 2][8 * (k % 2):8 * (k % 2) + 8] for k in range(10)]
        weight, coupling = lookup(planes[9] - 1.0, rows)
        coupling = jnp.where(planes[9] > 0.0, coupling, 0.0)
        rim_ref[6 * side + 3] = coupling
        for c in range(3):
            total = planes[6 + c] + line_rows(field_ref, y, c)
            rim_ref[6 * side + c] = KEEP * planes[c] + weight * planes[3 + c] + coupling * total
        lines.append(planes[:3])
    for z in range(8):
        here = slice(16 * z, 16 * z + 16)
        for c in range(3):
            halo = rim_rows(lines[0][c][z:z + 1], lines[1][c][z:z + 1])
            once_ref[c, here, :] = base_ref[c, here, :] + coupling_ref[here, :] * halo
    for z in range(2, 6):
        here = slice(16 * z, 16 * z + 16)
        for c in range(3):
            value = once_ref[c, here, :]
            total = once_ref[c, 16 * z - 16:16 * z, :] + once_ref[c, 16 * z + 16:16 * z + 32, :] + x_sum(value)
            total = total + row_sum(value, rim_ref[c, z:z + 1, :], rim_ref[6 + c, z:z + 1, :])
            result = KEEP * value + scaled_ref[c, here, :] + coupling_ref[here, :] * total
            out_ref[c, 16 * z - 32:16 * z - 16, :] = result
            at = 64 * c + 16 * z - 32
            plain_ref[at:at + 16, :] = result.astype(BF16)
    picked = jnp.dot(chosen_ref[...], plain_ref[...], preferred_element_type=F32)
    spread_ref[...] = spread_of(picked, place_ref[:, 0:1])


def spread_of(picked, place_column):
    along = lax.broadcasted_iota(jnp.int32, picked.shape, 1).astype(F32)
    single = jnp.where(along == place_column, picked, 0.0).astype(BF16)
    return jnp.dot(single, jnp.ones((picked.shape[1], 128), BF16), preferred_element_type=F32)


def relax_edges(planes, field_ref, once_ref, scaled_ref, coupling_ref, rim_ref, edge_ref, place_ref, spread_ref,
                far_ref, pair_ref, right_ref, out_ref, send_ref, plain_ref):
    even = lax.rem(lax.axis_index("slab"), 2) == 0
    both = list(zip(bands(far_ref, 8), bands(pair_ref, 8)))
    halo = [[jnp.where(even, far, pair) for far, pair in both], [jnp.where(even, pair, far) for far, pair in both]]
    row8 = lax.broadcasted_iota(jnp.int32, (8, field_ref.shape[-1]), 0)
    for c in range(3):
        once = {z: once_ref[c, 16 * z:16 * z + 16, :] for z in (1, 2, 5, 6)}
        once[0] = once_ref[c, 0:16, :] + coupling_ref[0:16, :] * halo[0][c]
        once[7] = once_ref[c, 112:128, :] + coupling_ref[112:128, :] * halo[1][c]
        once[-1] = halo[0][3 + c] + halo[0][6] * field_ref[c, 0:16, :]
        once[8] = halo[1][3 + c] + halo[1][6] * field_ref[c, 112:128, :]
        rims = []
        for side in range(2):
            at = 2 * c + side
            corner = jnp.where(row8 == 0, halo[0][7][at:at + 1], 0.0) + jnp.where(row8 == 7, halo[1][7][at:at + 1], 0.0)
            rims.append(rim_ref[6 * side + c] + rim_ref[6 * side + 3] * corner)
        for order, z in enumerate(EDGES):
            here = slice(16 * z, 16 * z + 16)
            total = once[z - 1] + once[z + 1] + x_sum(once[z])
            total = total + row_sum(once[z], rims[0][z:z + 1], rims[1][z:z + 1])
            result = KEEP * once[z] + scaled_ref[c, here, :] + coupling_ref[here, :] * total
            out_ref[c, 16 * order:16 * order + 16, :] = result
            at = 64 * c + 16 * order
            plain_ref[at:at + 16, :] = result.astype(BF16)

    picked = jnp.dot(edge_ref[...], plain_ref[...], preferred_element_type=F32)
    spread = spread_ref[...] + spread_of(picked, place_ref[:, 0:1])
    far = jnp.dot(right_ref[...], spread.astype(BF16), preferred_element_type=F32)
    ranks = 16
    lane = lax.broadcasted_iota(jnp.int32, (PLANE, 128), 1)
    parts = [jnp.zeros((PLANE, 128), F32) for _ in range(2)]
    for k in range(ranks):
        for z in range(planes):
            group = far[PLANE * (k * planes + z):PLANE * (k * planes + z + 1), :]
            at = z * ranks + k
            parts[at // 128] = jnp.where(lane == at % 128, group, parts[at // 128])
    down = lax.broadcasted_iota(jnp.int32, (128, 128), 0)
    across = lax.broadcasted_iota(jnp.int32, (128, 128), 1)
    traces = []
    for half in range(2):
        piece = jnp.where(down == across, spread[128 * half:128 * half + 128, :], 0.0)
        traces.append(jnp.sum(piece, axis=0, keepdims=True))
    tiles = send_ref.shape[0] // PLANE
    for to in range(PLANE):
        packet = stacked([parts[0][to:to + 1, :], parts[1][to:to + 1, :]] + traces, 4).astype(BF16)
        for tile in range(tiles):
            send_ref[seat(to, PLANE) * tiles + seat(tile, tiles)] = packet


def assemble(inner_ref, edges_ref, out_hbm, sems):
    copies = []
    for c in range(3):
        for source, target in ((edges_ref.at[c, 0:32], (0, 32)), (inner_ref.at[c], (32, 64)), (edges_ref.at[c, 32:64], (96, 32))):
            copies.append(pltpu.make_async_copy(source, out_hbm.at[c, pl.ds(*target), :], sems.at[len(copies)]))
    for copy in copies:
        copy.start()
    for copy in copies:
        copy.wait()


def middle(tiles, got_ref, send_ref):
    across = lax.rem(lax.axis_index("slab"), PLANE)
    tile = lax.axis_index("tile")
    total = jnp.sum(got_ref[...].astype(F32), axis=0)
    other = jnp.where(across == 0, PLANE - 1, 0)
    relay = []
    for b in range(3):
        wanted = tile + b - 1
        inside = (wanted >= 0) & (wanted < tiles)
        packet = got_ref[seated(other, PLANE) * tiles + seated(wanted, tiles)].astype(F32)
        packet = jnp.where(inside, packet, 0.0)
        relay += [packet[2:3, :], packet[3:4, :]]
    high = total.astype(BF16).astype(F32)
    low = total - high
    for half in range(2):
        packet = stacked([high[half:half + 1, :], low[half:half + 1, :]] + relay, 8).astype(BF16)
        for z in range(8 * half, min(8 * half + 8, send_ref.shape[0])):
            send_ref[seat(z - 1, send_ref.shape[0])] = packet


def masked_rows(rows, factors):
    lines = [jnp.concatenate(row, axis=1) * factor.astype(F32) for row, factor in zip(rows, factors)]
    return stacked(lines, 16).astype(BF16)


def products(rows, blocks, count):
    every = lax.dot_general(rows, blocks, (((1,), (1,)), ((), ())), preferred_element_type=F32)
    result = every[0:1, 0:256]
    for k in range(1, count):
        result = result + every[k:k + 1, 256 * k:256 * k + 256]
    return result


def near_inside(tiles, mask_ref, got_ref, near_ref, out_ref):
    across = lax.rem(lax.axis_index("slab"), PLANE)
    tile = lax.axis_index("tile")
    rows = []
    for a in range(-1, 2):
        for b in range(-1, 2):
            up, beside = across + a, tile + b
            inside = (up >= 0) & (up < PLANE) & (beside >= 0) & (beside < tiles)
            packet = got_ref[seated(up, PLANE) * tiles + seated(beside, tiles)].astype(F32)
            packet = jnp.where(inside, packet, 0.0)
            rows.append((packet[2:3, :], packet[3:4, :]))
    out_ref[...] = products(masked_rows(rows, [mask_ref[0:1, q:q + 1] for q in range(9)]), near_ref[...], 9)


def finish(planes, mask_ref, rank_ref, part_ref, relay_ref, near_ref, left_ref, out_ref):
    slab = lax.axis_index("slab")
    across = lax.rem(slab, PLANE)
    plane = lax.div(slab, PLANE)
    upward = across == PLANE - 1
    start = jnp.where(upward, plane + 1, plane - 1)
    edge = ((across == 0) | upward) & (start >= 0) & (start < planes)
    packet = jnp.where(edge, relay_ref[lax.rem(seated(start, planes) + planes - 1, planes)].astype(F32), 0.0)
    rows = [(packet[2 + 2 * b:3 + 2 * b, :], packet[3 + 2 * b:4 + 2 * b, :]) for b in range(3)]
    first = jnp.where(upward, 6, 0)
    blocks = near_ref[pl.ds(pl.multiple_of(256 * first, 256), 768), :]
    factors = [jnp.where(upward, mask_ref[0:1, 6 + b:7 + b], mask_ref[0:1, b:b + 1]) for b in range(3)]
    near = products(masked_rows(rows, factors), blocks, 3)
    total = jnp.sum(relay_ref[...].astype(F32), axis=0)
    total = jnp.broadcast_to(total[0:1, :] + total[1:2, :], (8, 128))
    lane = lax.broadcasted_iota(jnp.int32, total.shape, 1)
    at = 16 * lax.rem(plane, 8)
    total = jnp.where((lane >= at) & (lane < at + rank_ref[...]), total, 0.0)
    high = total.astype(BF16).astype(F32)
    halves = jnp.concatenate([high, total - high], axis=0).astype(BF16)
    left = jnp.concatenate([left_ref[...]] * 8, axis=0)
    far = jnp.dot(halves, left, preferred_element_type=F32)
    out_ref[...] = part_ref[...] + near + far[0:1, :] + far[8:9, :]


def vmem():
    return pl.BlockSpec(memory_space=pltpu.VMEM)


def hbm():
    return pl.BlockSpec(memory_space=pltpu.HBM)


def exchange(first, last, axis):
    devices = lax.axis_size(axis)
    up = [(i, i + 1) for i in range(devices - 1)]
    down = [(j, i) for i, j in up]
    return lax.ppermute(last, axis, up), lax.ppermute(first, axis, down)


def swap(far, pair, axis):
    devices = lax.axis_size(axis)
    far = lax.ppermute(far, axis, [(i, i + 1 if i % 2 else i - 1) for i in range(1, devices - 1)])
    return far, lax.ppermute(pair, axis, [(i, i ^ 1) for i in range(devices)])


def local(initial_field, source, material, stiffness_table, mass_table, trace_cells, near_blocks, near_mask, far_left, far_right,
          block_ranks):
    slabs, tiles = lax.axis_size("slab"), lax.axis_size("tile")
    planes = slabs // PLANE
    volume = jax.ShapeDtypeStruct((3, 128, 384), F32)
    face = jax.ShapeDtypeStruct((80, 384), BF16)
    params = pltpu.CompilerParams(vmem_limit_bytes=24 * 1024 * 1024)
    first, last = pl.pallas_call(
        y_faces,
        out_shape=(face, face),
        in_specs=[hbm()] * 3,
        out_specs=(vmem(), vmem()),
        scratch_shapes=[
            pltpu.VMEM((4, 3, 8, 384), F32), pltpu.VMEM((2, 3, 8, 384), F32), pltpu.VMEM((2, 8, 384), jnp.int32),
            pltpu.SemaphoreType.DMA((8,)),
        ],
        compiler_params=pltpu.CompilerParams(vmem_limit_bytes=55050 * 1024),
    )(initial_field, source, material)
    tables = (stiffness_table.reshape(1, 8), mass_table.reshape(1, 8))
    field = initial_field.reshape(3, 128, 384)
    sources = source.reshape(3, 128, 384)
    cells = material.reshape(128, 384)
    before, after = exchange(first, last, "tile")
    index = jax.ShapeDtypeStruct((256, 192), BF16)
    column = jax.ShapeDtypeStruct((256, 128), F32)
    base, scaled, coupling, edge, chosen, place = pl.pallas_call(
        no_halo,
        out_shape=(volume, volume, jax.ShapeDtypeStruct((128, 384), F32), index, index, column),
        in_specs=[vmem()] * 6,
        out_specs=(vmem(),) * 6,
        compiler_params=params,
        cost_estimate=pl.CostEstimate(flops=6_000_000, bytes_accessed=3_000_000, transcendentals=0),
    )(*tables, field, sources, cells, trace_cells.reshape(1, 256))
    face = jax.ShapeDtypeStruct((128, 384), BF16)
    far, pair = pl.pallas_call(
        z_faces,
        out_shape=(face, face),
        in_specs=[vmem()] * 5,
        out_specs=(vmem(), vmem()),
        compiler_params=params,
    )(field, base, coupling, before, after)
    far, pair = swap(far, pair, "slab")
    members = PLANE * tiles
    once, rim, inner, spread = pl.pallas_call(
        relax_inner,
        out_shape=(volume, jax.ShapeDtypeStruct((12, 8, 384), F32), jax.ShapeDtypeStruct((3, 64, 384), F32), column),
        in_specs=[vmem()] * 10,
        out_specs=(vmem(),) * 4,
        scratch_shapes=[pltpu.VMEM((192, 384), BF16)],
        compiler_params=params,
        cost_estimate=pl.CostEstimate(flops=4_000_000, bytes_accessed=3_000_000, transcendentals=0),
    )(*tables, field, base, scaled, coupling, before, after, chosen, place)
    edges, send = pl.pallas_call(
        functools.partial(relax_edges, planes),
        out_shape=(jax.ShapeDtypeStruct((3, 64, 384), F32), jax.ShapeDtypeStruct((members, 4, 128), BF16)),
        in_specs=[vmem()] * 11,
        out_specs=(vmem(), vmem()),
        scratch_shapes=[pltpu.VMEM((192, 384), BF16)],
        compiler_params=params,
    )(field, once, scaled, coupling, rim, edge, place, spread, far, pair, far_right.reshape(-1, 256))
    ids = np.arange(slabs * tiles).reshape(planes, PLANE, tiles)
    ids = np.roll(ids, (-(planes // 2) - 1, -(PLANE // 2), -(tiles // 2)), axis=(0, 1, 2)).reshape(planes, members)
    got = lax.all_to_all(send, BOTH, 0, 0, axis_index_groups=ids.tolist(), tiled=True)
    send = pl.pallas_call(
        functools.partial(middle, tiles),
        out_shape=jax.ShapeDtypeStruct((planes, 8, 128), BF16),
        in_specs=[vmem()],
        out_specs=vmem(),
        compiler_params=params,
    )(got)
    relay = lax.all_to_all(send, BOTH, 0, 0, axis_index_groups=ids.T.tolist(), tiled=True)
    result = pl.pallas_call(
        assemble,
        out_shape=volume,
        in_specs=[vmem(), vmem()],
        out_specs=hbm(),
        scratch_shapes=[pltpu.SemaphoreType.DMA((9,))],
        compiler_params=params,
        cost_estimate=pl.CostEstimate(flops=0, bytes_accessed=600_000, transcendentals=0),
    )(inner, edges)
    mask = near_mask.reshape(1, 9)
    blocks = near_blocks.reshape(-1, 256)
    part = pl.pallas_call(
        functools.partial(near_inside, tiles),
        out_shape=jax.ShapeDtypeStruct((1, 256), F32),
        in_specs=[vmem()] * 3,
        out_specs=vmem(),
        compiler_params=params,
        cost_estimate=pl.CostEstimate(flops=2 * 16 * 2304 * 256, bytes_accessed=2304 * 512, transcendentals=0),
    )(mask, got, blocks)
    boundary = pl.pallas_call(
        functools.partial(finish, planes),
        out_shape=jax.ShapeDtypeStruct((1, 256), F32),
        in_specs=[vmem()] * 6,
        out_specs=vmem(),
        compiler_params=params,
    )(mask, block_ranks.reshape(1, 1), part, relay, blocks, far_left.reshape(16, 256))
    return result.reshape(initial_field.shape), boundary.reshape(1, 1, 256)


def solution(mesh):
    placed = (
        P(None, "slab", "tile", None),
        P(None, "slab", "tile", None),
        P("slab", "tile", None),
        P(),
        P(),
        P("slab", "tile", None),
        P("slab", "tile", None, None, None),
        P("slab", "tile", None),
        P(None, "slab", "tile", None),
        P(None, None, "slab", "tile", None),
        P("slab"),
    )
    return jax.shard_map(
        local,
        mesh=mesh,
        in_specs=placed,
        out_specs=(P(None, "slab", "tile", None), P("slab", "tile", None)),
        check_vma=False,
    )
```

```python
import functools

import jax
import jax.numpy as jnp
import numpy as np
from jax import lax
from jax.experimental import pallas as pl
from jax.experimental.pallas import tpu as pltpu
from jax.sharding import PartitionSpec as P

RELAX = 0.8
KEEP = 1.0 - RELAX
PLANE = 8
F32 = jnp.float32
BF16 = jnp.bfloat16
BOTH = ("slab", "tile")


def seat(member, count):
    return (member + count - count // 2) % count


def seated(member, count):
    return lax.rem(jnp.clip(member, 0, count - 1) + count - count // 2, count)


def table_rows(stiff_ref, mass_ref, width):
    stiffness = stiff_ref[...]
    weight = RELAX / (6.0 * stiffness + mass_ref[...])
    rows = []
    for table in (weight, stiffness * weight):
        rows += [jnp.broadcast_to(table[:, entry:entry + 1], (1, width)) for entry in range(8)]
    return rows


def lookup(material, rows):
    weight = jnp.broadcast_to(rows[0], material.shape)
    coupling = jnp.broadcast_to(rows[8], material.shape)
    for entry in range(1, 8):
        here = material == entry
        weight = jnp.where(here, rows[entry], weight)
        coupling = jnp.where(here, rows[8 + entry], coupling)
    return weight, coupling


def x_sum(value):
    width = value.shape[-1]
    lane = lax.broadcasted_iota(jnp.int32, value.shape, value.ndim - 1)
    before = jnp.where(lane == 0, 0.0, pltpu.roll(value, 1, value.ndim - 1))
    after = jnp.where(lane == width - 1, 0.0, pltpu.roll(value, width - 1, value.ndim - 1))
    return before + after


def row_sum(value, first, last):
    length = value.shape[0]
    row = lax.broadcasted_iota(jnp.int32, value.shape, 0)
    before = jnp.where(row == 0, first, pltpu.roll(value, 1, 0))
    after = jnp.where(row == length - 1, last, pltpu.roll(value, length - 1, 0))
    return before + after


def line_rows(ref, y, *lead):
    lines = [ref[(*lead, slice(16 * z + y, 16 * z + y + 1), slice(None))] for z in range(8)]
    row = lax.broadcasted_iota(jnp.int32, (8, lines[0].shape[1]), 0)
    value = jnp.broadcast_to(lines[0], row.shape)
    for z in range(1, 8):
        value = jnp.where(row == z, lines[z], value)
    return value


def y_faces(field_hbm, source_hbm, material_hbm, first_ref, last_ref, field_ref, source_ref, material_ref, sems):
    pairs = [(field_hbm.at[:, :, y, :], field_ref.at[k]) for k, y in enumerate((0, 15, 1, 14))]
    pairs += [(source_hbm.at[:, :, y, :], source_ref.at[k]) for k, y in enumerate((0, 15))]
    pairs += [(material_hbm.at[:, y, :], material_ref.at[k]) for k, y in enumerate((0, 15))]
    copies = [pltpu.make_async_copy(src, dst, sems.at[k]) for k, (src, dst) in enumerate(pairs)]
    for copy in copies:
        copy.start()
    for copy in copies:
        copy.wait()
    for k, out_ref in enumerate((first_ref, last_ref)):
        values = [field_ref[k, c] for c in range(3)]
        totals = [field_ref[2 + k, c] + row_sum(values[c], 0.0, 0.0) + x_sum(values[c]) for c in range(3)]
        planes = values + [source_ref[k, c] for c in range(3)] + totals + [1.0 + material_ref[k].astype(F32)]
        for pair in range(5):
            both = jnp.concatenate(planes[2 * pair:2 * pair + 2], axis=0)
            out_ref[16 * pair:16 * pair + 16, :] = both.astype(BF16)


def rim_rows(first, last):
    row = lax.broadcasted_iota(jnp.int32, (16, first.shape[1]), 0)
    return jnp.where(row == 0, first, jnp.where(row == 15, last, 0.0))


def z_faces(field_ref, base_ref, coupling_ref, before_ref, after_ref, far_ref, pair_ref):
    even = lax.rem(lax.axis_index("slab"), 2) == 0
    before = bands(before_ref, 2)
    after = bands(after_ref, 2)
    faces = []
    for z in (0, 7):
        here = slice(16 * z, 16 * z + 16)
        coupling = coupling_ref[here, :]
        lines, values, partials = [], [], []
        for c in range(3):
            at = 8 * (c % 2) + z
            lines += [before[c // 2][at:at + 1, :], after[c // 2][at:at + 1, :]]
            values.append(field_ref[c, here, :])
            partials.append(base_ref[c, here, :] + coupling * rim_rows(lines[2 * c], lines[2 * c + 1]))
        faces.append(values + partials + [coupling, stacked(lines, 16)])
    for k, (first, last) in enumerate(zip(*faces)):
        here = slice(16 * k, 16 * k + 16)
        far_ref[here, :] = jnp.where(even, first, last).astype(BF16)
        pair_ref[here, :] = jnp.where(even, last, first).astype(BF16)


def stacked(lines, height):
    row = lax.broadcasted_iota(jnp.int32, (height, lines[0].shape[1]), 0)
    value = jnp.zeros(row.shape, F32)
    for k in range(len(lines)):
        value = jnp.where(row == k, lines[k], value)
    return value


def column_of(row):
    length = row.shape[1]
    down = lax.broadcasted_iota(jnp.int32, (length, length), 0)
    along = lax.broadcasted_iota(jnp.int32, (length, length), 1)
    return jnp.sum(jnp.where(down == along, row, 0.0), axis=1, keepdims=True)


def bands(ref, count):
    return [ref[16 * k:16 * k + 16, :].astype(F32) for k in range(count)]


EDGES = (0, 1, 6, 7)


def no_halo(stiff_ref, mass_ref, field_ref, source_ref, material_ref, cells_ref,
            base_ref, scaled_ref, coupling_ref, edge_ref, chosen_ref, place_ref):
    rows = table_rows(stiff_ref, mass_ref, field_ref.shape[-1])
    for z in range(8):
        here = slice(16 * z, 16 * z + 16)
        weight, coupling = lookup(material_ref[here, :], rows)
        coupling_ref[here, :] = coupling
        for c in range(3):
            value = field_ref[c, here, :]
            total = row_sum(value, 0.0, 0.0) + x_sum(value)
            if z > 0:
                total = total + field_ref[c, 16 * z - 16:16 * z, :]
            if z < 7:
                total = total + field_ref[c, 16 * z + 16:16 * z + 32, :]
            scaled = weight * source_ref[c, here, :]
            scaled_ref[c, here, :] = scaled
            base_ref[c, here, :] = KEEP * value + scaled + coupling * total

    width = field_ref.shape[-1]
    count = cells_ref.shape[1]
    cells = cells_ref[...].astype(F32)
    line = jnp.floor((cells + 0.5) * (1.0 / width))
    place_ref[...] = jnp.broadcast_to(column_of(cells - width * line), (count, 128))
    line_column = column_of(line)
    along = lax.broadcasted_iota(jnp.int32, (count, 192), 1).astype(F32)
    part = jnp.floor(along * (1.0 / 64) + 0.001)
    shift = along - 64.0 * part
    inner = 128.0 * part + shift + 32.0
    outer = 128.0 * part + jnp.where(shift < 32.0, shift, shift + 64.0)
    edge_ref[...] = jnp.where(outer == line_column, 1.0, 0.0).astype(BF16)
    chosen_ref[...] = jnp.where(inner == line_column, 1.0, 0.0).astype(BF16)


def relax_inner(stiff_ref, mass_ref, field_ref, base_ref, scaled_ref, coupling_ref, before_ref, after_ref, chosen_ref, place_ref,
                once_ref, rim_ref, out_ref, spread_ref, plain_ref):
    rows = table_rows(stiff_ref, mass_ref, field_ref.shape[-1])
    lines = []
    for side, (ref, y) in enumerate(((before_ref, 0), (after_ref, 15))):
        halo = bands(ref, 5)
        planes = [halo[k // 2][8 * (k % 2):8 * (k % 2) + 8] for k in range(10)]
        weight, coupling = lookup(planes[9] - 1.0, rows)
        coupling = jnp.where(planes[9] > 0.0, coupling, 0.0)
        rim_ref[6 * side + 3] = coupling
        for c in range(3):
            total = planes[6 + c] + line_rows(field_ref, y, c)
            rim_ref[6 * side + c] = KEEP * planes[c] + weight * planes[3 + c] + coupling * total
        lines.append(planes[:3])
    for z in range(8):
        here = slice(16 * z, 16 * z + 16)
        for c in range(3):
            halo = rim_rows(lines[0][c][z:z + 1], lines[1][c][z:z + 1])
            once_ref[c, here, :] = base_ref[c, here, :] + coupling_ref[here, :] * halo
    for z in range(2, 6):
        here = slice(16 * z, 16 * z + 16)
        for c in range(3):
            value = once_ref[c, here, :]
            total = once_ref[c, 16 * z - 16:16 * z, :] + once_ref[c, 16 * z + 16:16 * z + 32, :] + x_sum(value)
            total = total + row_sum(value, rim_ref[c, z:z + 1, :], rim_ref[6 + c, z:z + 1, :])
            result = KEEP * value + scaled_ref[c, here, :] + coupling_ref[here, :] * total
            out_ref[c, 16 * z - 32:16 * z - 16, :] = result
            at = 64 * c + 16 * z - 32
            plain_ref[at:at + 16, :] = result.astype(BF16)
    picked = jnp.dot(chosen_ref[...], plain_ref[...], preferred_element_type=F32)
    spread_ref[...] = spread_of(picked, place_ref[:, 0:1])


def spread_of(picked, place_column):
    along = lax.broadcasted_iota(jnp.int32, picked.shape, 1).astype(F32)
    single = jnp.where(along == place_column, picked, 0.0).astype(BF16)
    return jnp.dot(single, jnp.ones((picked.shape[1], 128), BF16), preferred_element_type=F32)


def relax_edges(planes, field_ref, once_ref, scaled_ref, coupling_ref, rim_ref, edge_ref, place_ref, spread_ref,
                far_ref, pair_ref, right_ref, out_ref, send_ref, plain_ref):
    even = lax.rem(lax.axis_index("slab"), 2) == 0
    both = list(zip(bands(far_ref, 8), bands(pair_ref, 8)))
    halo = [[jnp.where(even, far, pair) for far, pair in both], [jnp.where(even, pair, far) for far, pair in both]]
    row8 = lax.broadcasted_iota(jnp.int32, (8, field_ref.shape[-1]), 0)
    for c in range(3):
        once = {z: once_ref[c, 16 * z:16 * z + 16, :] for z in (1, 2, 5, 6)}
        once[0] = once_ref[c, 0:16, :] + coupling_ref[0:16, :] * halo[0][c]
        once[7] = once_ref[c, 112:128, :] + coupling_ref[112:128, :] * halo[1][c]
        once[-1] = halo[0][3 + c] + halo[0][6] * field_ref[c, 0:16, :]
        once[8] = halo[1][3 + c] + halo[1][6] * field_ref[c, 112:128, :]
        rims = []
        for side in range(2):
            at = 2 * c + side
            corner = jnp.where(row8 == 0, halo[0][7][at:at + 1], 0.0) + jnp.where(row8 == 7, halo[1][7][at:at + 1], 0.0)
            rims.append(rim_ref[6 * side + c] + rim_ref[6 * side + 3] * corner)
        for order, z in enumerate(EDGES):
            here = slice(16 * z, 16 * z + 16)
            total = once[z - 1] + once[z + 1] + x_sum(once[z])
            total = total + row_sum(once[z], rims[0][z:z + 1], rims[1][z:z + 1])
            result = KEEP * once[z] + scaled_ref[c, here, :] + coupling_ref[here, :] * total
            out_ref[c, 16 * order:16 * order + 16, :] = result
            at = 64 * c + 16 * order
            plain_ref[at:at + 16, :] = result.astype(BF16)

    picked = jnp.dot(edge_ref[...], plain_ref[...], preferred_element_type=F32)
    spread = spread_ref[...] + spread_of(picked, place_ref[:, 0:1])
    far = jnp.dot(right_ref[...], spread.astype(BF16), preferred_element_type=F32)
    ranks = 16
    lane = lax.broadcasted_iota(jnp.int32, (PLANE, 128), 1)
    parts = [jnp.zeros((PLANE, 128), F32) for _ in range(2)]
    for k in range(ranks):
        for z in range(planes):
            group = far[PLANE * (k * planes + z):PLANE * (k * planes + z + 1), :]
            at = z * ranks + k
            parts[at // 128] = jnp.where(lane == at % 128, group, parts[at // 128])
    down = lax.broadcasted_iota(jnp.int32, (128, 128), 0)
    across = lax.broadcasted_iota(jnp.int32, (128, 128), 1)
    traces = []
    for half in range(2):
        piece = jnp.where(down == across, spread[128 * half:128 * half + 128, :], 0.0)
        traces.append(jnp.sum(piece, axis=0, keepdims=True))
    tiles = send_ref.shape[0] // PLANE
    for to in range(PLANE):
        packet = stacked([parts[0][to:to + 1, :], parts[1][to:to + 1, :]] + traces, 4).astype(BF16)
        for tile in range(tiles):
            send_ref[seat(to, PLANE) * tiles + seat(tile, tiles)] = packet


def assemble(inner_ref, edges_ref, out_hbm, sems):
    copies = []
    for c in range(3):
        for source, target in ((edges_ref.at[c, 0:32], (0, 32)), (inner_ref.at[c], (32, 64)), (edges_ref.at[c, 32:64], (96, 32))):
            copies.append(pltpu.make_async_copy(source, out_hbm.at[c, pl.ds(*target), :], sems.at[len(copies)]))
    for copy in copies:
        copy.start()
    for copy in copies:
        copy.wait()


def middle(tiles, got_ref, send_ref):
    across = lax.rem(lax.axis_index("slab"), PLANE)
    tile = lax.axis_index("tile")
    total = jnp.sum(got_ref[...].astype(F32), axis=0)
    other = jnp.where(across == 0, PLANE - 1, 0)
    relay = []
    for b in range(3):
        wanted = tile + b - 1
        inside = (wanted >= 0) & (wanted < tiles)
        packet = got_ref[seated(other, PLANE) * tiles + seated(wanted, tiles)].astype(F32)
        packet = jnp.where(inside, packet, 0.0)
        relay += [packet[2:3, :], packet[3:4, :]]
    high = total.astype(BF16).astype(F32)
    low = total - high
    for half in range(2):
        packet = stacked([high[half:half + 1, :], low[half:half + 1, :]] + relay, 8).astype(BF16)
        for z in range(8 * half, min(8 * half + 8, send_ref.shape[0])):
            send_ref[seat(z - 2, send_ref.shape[0])] = packet


def masked_rows(rows, factors):
    lines = [jnp.concatenate(row, axis=1) * factor.astype(F32) for row, factor in zip(rows, factors)]
    return stacked(lines, 16).astype(BF16)


def products(rows, blocks, count):
    every = lax.dot_general(rows, blocks, (((1,), (1,)), ((), ())), preferred_element_type=F32)
    result = every[0:1, 0:256]
    for k in range(1, count):
        result = result + every[k:k + 1, 256 * k:256 * k + 256]
    return result


def near_inside(tiles, mask_ref, got_ref, near_ref, out_ref):
    across = lax.rem(lax.axis_index("slab"), PLANE)
    tile = lax.axis_index("tile")
    rows = []
    for a in range(-1, 2):
        for b in range(-1, 2):
            up, beside = across + a, tile + b
            inside = (up >= 0) & (up < PLANE) & (beside >= 0) & (beside < tiles)
            packet = got_ref[seated(up, PLANE) * tiles + seated(beside, tiles)].astype(F32)
            packet = jnp.where(inside, packet, 0.0)
            rows.append((packet[2:3, :], packet[3:4, :]))
    out_ref[...] = products(masked_rows(rows, [mask_ref[0:1, q:q + 1] for q in range(9)]), near_ref[...], 9)


def finish(planes, mask_ref, rank_ref, part_ref, relay_ref, near_ref, left_ref, out_ref):
    slab = lax.axis_index("slab")
    across = lax.rem(slab, PLANE)
    plane = lax.div(slab, PLANE)
    upward = across == PLANE - 1
    start = jnp.where(upward, plane + 1, plane - 1)
    edge = ((across == 0) | upward) & (start >= 0) & (start < planes)
    packet = jnp.where(edge, relay_ref[lax.rem(seated(start, planes) + planes - 2, planes)].astype(F32), 0.0)
    rows = [(packet[2 + 2 * b:3 + 2 * b, :], packet[3 + 2 * b:4 + 2 * b, :]) for b in range(3)]
    first = jnp.where(upward, 6, 0)
    blocks = near_ref[pl.ds(pl.multiple_of(256 * first, 256), 768), :]
    factors = [jnp.where(upward, mask_ref[0:1, 6 + b:7 + b], mask_ref[0:1, b:b + 1]) for b in range(3)]
    near = products(masked_rows(rows, factors), blocks, 3)
    total = jnp.sum(relay_ref[...].astype(F32), axis=0)
    total = jnp.broadcast_to(total[0:1, :] + total[1:2, :], (8, 128))
    lane = lax.broadcasted_iota(jnp.int32, total.shape, 1)
    at = 16 * lax.rem(plane, 8)
    total = jnp.where((lane >= at) & (lane < at + rank_ref[...]), total, 0.0)
    high = total.astype(BF16).astype(F32)
    halves = jnp.concatenate([high, total - high], axis=0).astype(BF16)
    left = jnp.concatenate([left_ref[...]] * 8, axis=0)
    far = jnp.dot(halves, left, preferred_element_type=F32)
    out_ref[...] = part_ref[...] + near + far[0:1, :] + far[8:9, :]


def vmem():
    return pl.BlockSpec(memory_space=pltpu.VMEM)


def hbm():
    return pl.BlockSpec(memory_space=pltpu.HBM)


def exchange(first, last, axis):
    devices = lax.axis_size(axis)
    up = [(i, i + 1) for i in range(devices - 1)]
    down = [(j, i) for i, j in up]
    return lax.ppermute(last, axis, up), lax.ppermute(first, axis, down)


def swap(far, pair, axis):
    devices = lax.axis_size(axis)
    far = lax.ppermute(far, axis, [(i, i + 1 if i % 2 else i - 1) for i in range(1, devices - 1)])
    return far, lax.ppermute(pair, axis, [(i, i ^ 1) for i in range(devices)])


def local(initial_field, source, material, stiffness_table, mass_table, trace_cells, near_blocks, near_mask, far_left, far_right,
          block_ranks):
    slabs, tiles = lax.axis_size("slab"), lax.axis_size("tile")
    planes = slabs // PLANE
    volume = jax.ShapeDtypeStruct((3, 128, 384), F32)
    face = jax.ShapeDtypeStruct((80, 384), BF16)
    params = pltpu.CompilerParams(vmem_limit_bytes=24 * 1024 * 1024)
    first, last = pl.pallas_call(
        y_faces,
        out_shape=(face, face),
        in_specs=[hbm()] * 3,
        out_specs=(vmem(), vmem()),
        scratch_shapes=[
            pltpu.VMEM((4, 3, 8, 384), F32), pltpu.VMEM((2, 3, 8, 384), F32), pltpu.VMEM((2, 8, 384), jnp.int32),
            pltpu.SemaphoreType.DMA((8,)),
        ],
        compiler_params=pltpu.CompilerParams(vmem_limit_bytes=55050 * 1024),
    )(initial_field, source, material)
    tables = (stiffness_table.reshape(1, 8), mass_table.reshape(1, 8))
    field = initial_field.reshape(3, 128, 384)
    sources = source.reshape(3, 128, 384)
    cells = material.reshape(128, 384)
    before, after = exchange(first, last, "tile")
    index = jax.ShapeDtypeStruct((256, 192), BF16)
    column = jax.ShapeDtypeStruct((256, 128), F32)
    base, scaled, coupling, edge, chosen, place = pl.pallas_call(
        no_halo,
        out_shape=(volume, volume, jax.ShapeDtypeStruct((128, 384), F32), index, index, column),
        in_specs=[vmem()] * 6,
        out_specs=(vmem(),) * 6,
        compiler_params=params,
        cost_estimate=pl.CostEstimate(flops=6_000_000, bytes_accessed=3_000_000, transcendentals=0),
    )(*tables, field, sources, cells, trace_cells.reshape(1, 256))
    face = jax.ShapeDtypeStruct((128, 384), BF16)
    far, pair = pl.pallas_call(
        z_faces,
        out_shape=(face, face),
        in_specs=[vmem()] * 5,
        out_specs=(vmem(), vmem()),
        compiler_params=params,
    )(field, base, coupling, before, after)
    far, pair = swap(far, pair, "slab")
    members = PLANE * tiles
    once, rim, inner, spread = pl.pallas_call(
        relax_inner,
        out_shape=(volume, jax.ShapeDtypeStruct((12, 8, 384), F32), jax.ShapeDtypeStruct((3, 64, 384), F32), column),
        in_specs=[vmem()] * 10,
        out_specs=(vmem(),) * 4,
        scratch_shapes=[pltpu.VMEM((192, 384), BF16)],
        compiler_params=params,
        cost_estimate=pl.CostEstimate(flops=4_000_000, bytes_accessed=3_000_000, transcendentals=0),
    )(*tables, field, base, scaled, coupling, before, after, chosen, place)
    edges, send = pl.pallas_call(
        functools.partial(relax_edges, planes),
        out_shape=(jax.ShapeDtypeStruct((3, 64, 384), F32), jax.ShapeDtypeStruct((members, 4, 128), BF16)),
        in_specs=[vmem()] * 11,
        out_specs=(vmem(), vmem()),
        scratch_shapes=[pltpu.VMEM((192, 384), BF16)],
        compiler_params=params,
    )(field, once, scaled, coupling, rim, edge, place, spread, far, pair, far_right.reshape(-1, 256))
    ids = np.arange(slabs * tiles).reshape(planes, PLANE, tiles)
    ids = np.roll(ids, (-(planes // 2) - 2, -(PLANE // 2), -(tiles // 2)), axis=(0, 1, 2)).reshape(planes, members)
    got = lax.all_to_all(send, BOTH, 0, 0, axis_index_groups=ids.tolist(), tiled=True)
    send = pl.pallas_call(
        functools.partial(middle, tiles),
        out_shape=jax.ShapeDtypeStruct((planes, 8, 128), BF16),
        in_specs=[vmem()],
        out_specs=vmem(),
        compiler_params=params,
    )(got)
    relay = lax.all_to_all(send, BOTH, 0, 0, axis_index_groups=ids.T.tolist(), tiled=True)
    result = pl.pallas_call(
        assemble,
        out_shape=volume,
        in_specs=[vmem(), vmem()],
        out_specs=hbm(),
        scratch_shapes=[pltpu.SemaphoreType.DMA((9,))],
        compiler_params=params,
        cost_estimate=pl.CostEstimate(flops=0, bytes_accessed=600_000, transcendentals=0),
    )(inner, edges)
    mask = near_mask.reshape(1, 9)
    blocks = near_blocks.reshape(-1, 256)
    part = pl.pallas_call(
        functools.partial(near_inside, tiles),
        out_shape=jax.ShapeDtypeStruct((1, 256), F32),
        in_specs=[vmem()] * 3,
        out_specs=vmem(),
        compiler_params=params,
        cost_estimate=pl.CostEstimate(flops=2 * 16 * 2304 * 256, bytes_accessed=2304 * 512, transcendentals=0),
    )(mask, got, blocks)
    boundary = pl.pallas_call(
        functools.partial(finish, planes),
        out_shape=jax.ShapeDtypeStruct((1, 256), F32),
        in_specs=[vmem()] * 6,
        out_specs=vmem(),
        compiler_params=params,
    )(mask, block_ranks.reshape(1, 1), part, relay, blocks, far_left.reshape(16, 256))
    return result.reshape(initial_field.shape), boundary.reshape(1, 1, 256)


def solution(mesh):
    placed = (
        P(None, "slab", "tile", None),
        P(None, "slab", "tile", None),
        P("slab", "tile", None),
        P(),
        P(),
        P("slab", "tile", None),
        P("slab", "tile", None, None, None),
        P("slab", "tile", None),
        P(None, "slab", "tile", None),
        P(None, None, "slab", "tile", None),
        P("slab"),
    )
    return jax.shard_map(
        local,
        mesh=mesh,
        in_specs=placed,
        out_specs=(P(None, "slab", "tile", None), P("slab", "tile", None)),
        check_vma=False,
    )
```
